32 devices in a mesh: batch: 8 (over z, x), height: 4 (over y, core).
Axes of the slice: x: 2, y: 2, z: 4, core: 2. Of those that a mesh axis runs over, the one named last changes fastest.
Arguments:
- images: bfloat16 [64, 16, 14, 1024], P('batch', 'height'), may hold values from -11 to 11
- counts: int32 [8], P('batch'), may hold values from 4 to 8, as said below
- row_valid: int32 [16], P('height'), may hold values from 0 to 1, as said below
- w_reduce: bfloat16 [1024, 256], replicated, may hold values from -0.1875 to 0.1875
- gain_one: float32 [256], replicated, may hold values from 0.5 to 1.5
- bias_one: float32 [256], replicated, may hold values from -0.5 to 0.5
- w_split: bfloat16 [3, 3, 128, 512], replicated, may hold values from -0.1875 to 0.1875
- gain_two: float32 [512], replicated, may hold values from 0.5 to 1.5
- bias_two: float32 [512], replicated, may hold values from -0.5 to 0.5
- w_squeeze: float32 [256, 128], replicated, may hold values from -0.375 to 0.375
- gain_mid: float32 [128], replicated, may hold values from 0.5 to 1.5
- bias_mid: float32 [128], replicated, may hold values from -0.5 to 0.5
- w_excite: float32 [128, 512], replicated, may hold values from -0.5 to 0.5
- bias_excite: float32 [512], replicated, may hold values from -3 to 3
- w_expand: bfloat16 [256, 1024], replicated, may hold values from -0.375 to 0.375
- gain_three: float32 [1024], replicated, may hold values from 0.5 to 1.5
- bias_three: float32 [1024], replicated, may hold values from -0.5 to 0.5
- cotangent: bfloat16 [64, 16, 14, 1024], P('batch', 'height'), may hold values from -6 to 6
Outputs:
- output: bfloat16 [64, 16, 14, 1024], P('batch', 'height')
- grad_images: bfloat16 [64, 16, 14, 1024], P('batch', 'height')
- grad_reduce: float32 [1024, 256], replicated
- grad_gain_one: float32 [256], replicated
- grad_bias_one: float32 [256], replicated
- grad_split: float32 [3, 3, 128, 512], replicated
- grad_gain_two: float32 [512], replicated
- grad_bias_two: float32 [512], replicated
- grad_squeeze: float32 [256, 128], replicated
- grad_gain_mid: float32 [128], replicated
- grad_bias_mid: float32 [128], replicated
- grad_excite: float32 [128, 512], replicated
- grad_bias_excite: float32 [512], replicated
- grad_expand: float32 [256, 1024], replicated
- grad_gain_three: float32 [1024], replicated
- grad_bias_three: float32 [1024], replicated
The draws below stay inside these ranges and needn't reach their ends.
Inputs may be any that keep to these rules, and one draw needn't show every extreme that they name: `counts`: between 4 and 8; some device holds 8 images and some 8 // 2. `row_valid`: in each block of 4 slots the ones come first; each block holds 14 // 4 or that plus 1 row, 14 in all, blocks in image order.
All inputs are finite; a program needn't handle non-finite values.
Results may differ from the reference program's by a relative error of at most 0.0081.
Values may be sent and summed in bfloat16 or wider, within the bound.
A program may use at most 64 MiB of HBM per device.

```python
import jax
import jax.numpy as jnp
from jax import lax

C_IN = 1024
MID = 256
ATT = 128
SPLIT = 512
GROUP_IN = 128
IMG_H = 14
IMG_W = 14
ROWS_DEV = 4
IMG_DEV = 8
IMAGES = 64
ROWS = 16


def draw_images(key, part):
    key = jax.random.fold_in(key, 3)
    slot = jnp.arange(IMAGES, dtype=jnp.float32)
    rising = jnp.exp(jnp.log(0.6) + jnp.log(3.0) * slot / max(IMAGES - 1, 1))
    values = jnp.clip(jax.random.normal(key, (IMAGES, ROWS, IMG_W, C_IN), jnp.float32), -6.0, 6.0)
    return (values * rising[:, None, None, None]).astype(jnp.bfloat16)


def draw_counts(key, part):
    key = jax.random.fold_in(key, 1)
    key_values, key_order = jax.random.split(key)
    devices = IMAGES // IMG_DEV
    values = jax.random.randint(key_values, (devices,), IMG_DEV // 2, IMG_DEV + 1, dtype=jnp.int32)
    order = jax.random.permutation(key_order, devices)
    values = values.at[order[0]].set(IMG_DEV)
    return values.at[order[1]].set(IMG_DEV // 2)


def draw_row_valid(key, part):
    key = jax.random.fold_in(key, 2)
    blocks = ROWS // ROWS_DEV
    extra = (jax.random.permutation(key, blocks) < IMG_H % blocks).astype(jnp.int32)
    filled = IMG_H // blocks + extra
    marks = jnp.arange(ROWS_DEV, dtype=jnp.int32)[None, :] < filled[:, None]
    return marks.astype(jnp.int32).reshape(ROWS)


def shard_levels(stream_key, dims, cuts, least, largest):
    factor_of, own = 1.0, jax.random.fold_in(stream_key, 6)
    for axis_at, parts in cuts:
        draws = jnp.exp(jax.random.uniform(jax.random.fold_in(own, axis_at), (parts,), jnp.float32, least / len(cuts), largest / len(cuts)))
        factor_of = factor_of * jnp.repeat(draws, dims[axis_at] // parts).reshape([-1 if axis == axis_at else 1 for axis in range(len(dims))])
    return factor_of


def gaussian(stream_key, shape, scale, reach, cuts=(), kind=jnp.bfloat16):
    factor_of = shard_levels(stream_key, shape, cuts, -0.22, 0.18) if cuts else 1.0
    array = jax.random.normal(stream_key, shape, jnp.float32) * scale * factor_of
    return jnp.minimum(jnp.maximum(array, -reach), reach).astype(kind)


def setup_inputs(seed: int = 0) -> dict:
    key_list = jax.random.split(jax.random.key(seed), 19)
    images = draw_images(jax.random.fold_in(key_list[18], 71), 0)
    counts = draw_counts(jax.random.fold_in(key_list[18], 71), 0)
    row_valid = draw_row_valid(jax.random.fold_in(key_list[18], 71), 0)
    w_reduce = gaussian(key_list[3], (C_IN, MID), C_IN ** -0.5, 0.1875)
    gain_one = jnp.clip(jax.random.uniform(key_list[4], (MID,), jnp.float32, 0.5, 1.5), 0.5, 1.5)
    bias_one = jnp.clip(jax.random.uniform(key_list[5], (MID,), jnp.float32, -0.5, 0.5), -0.5, 0.5)
    w_split = gaussian(key_list[6], (3, 3, GROUP_IN, SPLIT), (9 * GROUP_IN) ** -0.5, 0.1875)
    gain_two = jnp.clip(jax.random.uniform(key_list[7], (SPLIT,), jnp.float32, 0.5, 1.5), 0.5, 1.5)
    bias_two = jnp.clip(jax.random.uniform(key_list[8], (SPLIT,), jnp.float32, -0.5, 0.5), -0.5, 0.5)
    w_squeeze = gaussian(key_list[9], (MID, ATT), MID ** -0.5, 0.375, (), jnp.float32)
    gain_mid = jnp.clip(jax.random.uniform(key_list[10], (ATT,), jnp.float32, 0.5, 1.5), 0.5, 1.5)
    bias_mid = jnp.clip(jax.random.uniform(key_list[11], (ATT,), jnp.float32, -0.5, 0.5), -0.5, 0.5)
    w_excite = gaussian(key_list[12], (ATT, SPLIT), ATT ** -0.5, 0.5, (), jnp.float32)
    bias_excite = gaussian(key_list[13], (SPLIT,), 0.5, 3.0, (), jnp.float32)
    w_expand = gaussian(key_list[14], (MID, C_IN), MID ** -0.5, 0.375)
    gain_three = jnp.clip(jax.random.uniform(key_list[15], (C_IN,), jnp.float32, 0.5, 1.5), 0.5, 1.5)
    bias_three = jnp.clip(jax.random.uniform(key_list[16], (C_IN,), jnp.float32, -0.5, 0.5), -0.5, 0.5)
    cotangent = gaussian(key_list[17], (IMAGES, ROWS, IMG_W, C_IN), 1.0, 6.0, ((0, 8), (1, 4)))
    return {"images": images, "counts": counts, "row_valid": row_valid, "w_reduce": w_reduce, "gain_one": gain_one, "bias_one": bias_one, "w_split": w_split, "gain_two": gain_two, "bias_two": bias_two, "w_squeeze": w_squeeze, "gain_mid": gain_mid, "bias_mid": bias_mid, "w_excite": w_excite, "bias_excite": bias_excite, "w_expand": w_expand, "gain_three": gain_three, "bias_three": bias_three, "cotangent": cotangent}


epsilon = 1e-05

@jax.custom_vjp
def low(v):
    return lax.optimization_barrier(v.astype(jnp.bfloat16)).astype(jnp.float32)

@jax.custom_vjp
def low_back(v):
    return v

def low_keep(v):
    return (low(v), None)

def low_pass(kept, grad):
    return (grad,)

def back_keep(v):
    return (v, None)

def back_low(kept, grad):
    return (low(grad),)
low.defvjp(low_keep, low_pass)
low_back.defvjp(back_keep, back_low)

def swish_act(values):
    return values * jax.nn.sigmoid(values)

def normalize(values, weights, count, gain, shift, axes):
    mean = lax.optimization_barrier(jnp.sum(values * weights, axis=axes)) / count
    spread = lax.optimization_barrier(jnp.sum(values * values * weights, axis=axes)) / count - mean * mean
    return (values - mean) * lax.rsqrt(spread + epsilon) * gain + shift

def forward(images, w_reduce, gain_one, bias_one, w_split, gain_two, bias_two, w_squeeze, gain_mid, bias_mid, w_excite, bias_excite, w_expand, gain_three, bias_three, pixel_weights, slot_live, pix_total, slot_total):
    highest = lax.Precision.HIGHEST
    axes = (0, 1, 2)
    conv_one = low_back(jnp.einsum('nhwc,cd->nhwd', images, w_reduce, precision=highest))
    hidden = low(swish_act(normalize(conv_one, pixel_weights, pix_total, gain_one, bias_one, axes)) * pixel_weights)
    conv_two = low_back(lax.conv_general_dilated(hidden, w_split, (1, 1), 'SAME', dimension_numbers=('NHWC', 'HWIO', 'NHWC'), feature_group_count=2, precision=highest))
    act_two = swish_act(normalize(conv_two, pixel_weights, pix_total, gain_two, bias_two, axes)) * pixel_weights
    half_width = act_two.shape[3] // 2
    split_one = act_two[..., :half_width]
    split_two = act_two[..., half_width:]
    pooled = lax.optimization_barrier(jnp.mean(split_one + split_two, axis=(1, 2)))
    squeeze = jnp.dot(pooled, w_squeeze, precision=highest)
    middle = swish_act(normalize(squeeze, slot_live[:, None], slot_total, gain_mid, bias_mid, (0,)))
    logits = jnp.dot(middle, w_excite, precision=highest) + bias_excite
    attention = jax.nn.softmax(logits.reshape(-1, 2, half_width), axis=1)
    mixed_sum = low(attention[:, 0, None, None, :] * split_one + attention[:, 1, None, None, :] * split_two)
    conv_three = low_back(jnp.einsum('nhwc,cd->nhwd', mixed_sum, w_expand, precision=highest))
    residual = normalize(conv_three, pixel_weights, pix_total, gain_three, bias_three, axes) + images
    return swish_act(residual) * pixel_weights

def reference(images, counts, row_valid, w_reduce, gain_one, bias_one, w_split, gain_two, bias_two, w_squeeze, gain_mid, bias_mid, w_excite, bias_excite, w_expand, gain_three, bias_three, cotangent):
    slots = images.shape[0]
    positions = jnp.argsort(1 - row_valid, stable=True)[:IMG_H].astype(jnp.int32)
    inputs = images[:, positions].astype(jnp.float32)
    tangent = cotangent[:, positions].astype(jnp.float32)
    slot_index = jnp.arange(slots, dtype=jnp.int32)
    slot_live = (slot_index % IMG_DEV < counts[slot_index // IMG_DEV]).astype(jnp.float32)
    pixel_weights = slot_live[:, None, None, None]
    slot_total = jnp.sum(slot_live)
    pix_total = slot_total * (IMG_H * IMG_W)
    params = (inputs, w_reduce.astype(jnp.float32), gain_one, bias_one, w_split.astype(jnp.float32), gain_two, bias_two, w_squeeze, gain_mid, bias_mid, w_excite, bias_excite, w_expand.astype(jnp.float32), gain_three, bias_three)

    def apply_block(*values):
        return forward(*values, pixel_weights, slot_live, pix_total, slot_total)
    result, pullback = jax.vjp(apply_block, *params)
    grads = pullback(tangent)
    blank = jnp.zeros((slots, ROWS, IMG_W, C_IN), jnp.float32)
    output = blank.at[:, positions].set(result).astype(jnp.bfloat16)
    grad_images = blank.at[:, positions].set(grads[0]).astype(jnp.bfloat16)
    return (output, grad_images, grads[1], grads[2], grads[3], grads[4], grads[5], grads[6], grads[7], grads[8], grads[9], grads[10], grads[11], grads[12], grads[13], grads[14])
```

```python
import functools

import jax
import jax.numpy as jnp
from jax import lax
from jax.experimental import pallas as pl
from jax.experimental.pallas import tpu as pltpu
from jax.sharding import PartitionSpec as P

IMG_H = 14
IMG_W = 14
EPSILON = 1e-05
MESH = pl.DeviceIdType.MESH
F32 = jnp.float32
BF16 = jnp.bfloat16
HIGHEST = lax.Precision.HIGHEST
COLS = 16
GROUP = 8
NN = (((1,), (0,)), ((), ()))
NT = (((1,), (1,)), ((), ()))
TN = (((0,), (0,)), ((), ()))


def dot(lhs, rhs, dims=NN, precision=None):
    return lax.dot_general(lhs, rhs, dims, precision=precision, preferred_element_type=F32)


def sigmoid(values):
    return 0.5 * jnp.tanh(0.5 * values) + 0.5


def swish(values):
    return values * sigmoid(values)


def swish_slope(values):
    sigma = sigmoid(values)
    return sigma + values * sigma * (1.0 - sigma)


def tiled(row, times):
    return jnp.concatenate([row] * times, axis=1) if times > 1 else row


def colsum(values):
    return jnp.sum(values, axis=0, keepdims=True)


def put_rows(ref, at, row):
    for k in range(row.shape[1] // 128):
        ref[at + k : at + k + 1, :] = row[:, k * 128 : (k + 1) * 128]


def get_rows(ref, at, count):
    return jnp.concatenate([ref[at + k : at + k + 1, :] for k in range(count)], axis=1)


def per_slot(values, slots):
    return jnp.sum(values.reshape(slots, COLS, values.shape[1]), axis=1)


def main_kernel(n_batch, n_height, sizes, *refs):
    (
        counts, row_valid, gain_one, bias_one, gain_two, bias_two, gain_mid, bias_mid,
        bias_excite, gain_three, bias_three,
        images, cotangent, w_reduce_in, w_split_in, w_squeeze_in, w_excite_in, w_expand_in,
        output, grad_images, big_e, big_s, big_r, big_q, vectors,
        img4, cot4, out4, w_reduce, w_split, w_squeeze, w_excite, w_expand,
        x, g, pix, c1, hs, c2, act, slope2, mixed, c3, d3, xo, gc3, gm, d2, gc2, gh, slope1, gc1,
        gc2_own, x_t, mixed_t, hs_t, att, attx, gpx, pooled, sq_all, tot,
        m1, m2, m34, m5, m6, m78, m9, m10, em_src,
        s1, s2, s34, s5, s6, s78, s9, s10, em_all,
        last1, up1, down1, last2, up2, down2, last3, up3, down3,
        full_e, half_e, quart_e, in1_e, in2_e, in3_e, in4_e, shard_e, done_e,
        full_s, half_s, quart_s, in1_s, in2_s, in3_s, in4_s, shard_s, done_s,
        full_r, half_r, quart_r, in1_r, in2_r, in3_r, in4_r, shard_r, done_r,
        full_q, half_q, quart_q, in1_q, in2_q, in3_q, in4_q, shard_q, done_q,
        local_sem, all_send, all_recv, halo_send, halo_recv, em_sems, red_send, red_recv,
    ) = refs
    slots, rows, cols, width = sizes
    narrow = w_reduce.shape[1]
    split = w_split.shape[1]
    half = split // 2
    cg = w_split.shape[0] // 9
    inner = w_squeeze.shape[1]
    block = slots * COLS
    pixels = rows * block
    total = n_batch * n_height
    area = float(IMG_H * IMG_W)
    b = lax.axis_index("batch")
    h = lax.axis_index("height")
    me = b * n_height + h

    loads = [
        pltpu.make_async_copy(src, dst, local_sem.at[k])
        for k, (src, dst) in enumerate(
            [
                (images, img4), (w_reduce_in, w_reduce), (w_split_in, w_split), (cotangent, cot4),
                (w_squeeze_in, w_squeeze), (w_excite_in, w_excite), (w_expand_in, w_expand),
            ]
        )
    ]
    for load in loads:
        load.start()

    barrier = pltpu.get_barrier_semaphore()

    def greet(j, carry):
        t = lax.rem(me + j, total)
        pl.semaphore_signal(
            barrier, inc=1, device_id=(t // n_height, lax.rem(t, n_height)), device_id_type=MESH
        )
        return carry

    lax.fori_loop(1, total, greet, 0)

    def send_all(src, dst, k):
        def one(j, carry):
            t = lax.rem(me + j, total)
            pltpu.make_async_remote_copy(
                src_ref=src, dst_ref=dst.at[me], send_sem=all_send.at[k], recv_sem=all_recv.at[k],
                device_id=(t // n_height, lax.rem(t, n_height)), device_id_type=MESH,
            ).start()
            return carry

        lax.fori_loop(1, total, one, 0)
        dst[me] = src[...]

    def all_copy(dst, k):
        return pltpu.make_async_remote_copy(
            src_ref=dst.at[pl.ds(0, total - 1)], dst_ref=dst.at[pl.ds(0, total - 1)],
            send_sem=all_send.at[k], recv_sem=all_recv.at[k], device_id=(b, h), device_id_type=MESH,
        )

    def sum_all(dst, k):
        all_copy(dst, k).wait_recv()

        def one(i, acc):
            return acc + jnp.sum(dst[pl.ds(i * 8, 8)], axis=0)

        acc = lax.fori_loop(0, total // 8, one, jnp.zeros(dst.shape[1:], F32))
        tot[0 : dst.shape[1], :] = acc

    def halo_copies(first, last, up, down, k):
        above = pltpu.make_async_remote_copy(
            src_ref=last, dst_ref=up, send_sem=halo_send.at[2 * k], recv_sem=halo_recv.at[2 * k],
            device_id=(b, lax.rem(h + 1, n_height)), device_id_type=MESH,
        )
        below = pltpu.make_async_remote_copy(
            src_ref=first, dst_ref=down, send_sem=halo_send.at[2 * k + 1],
            recv_sem=halo_recv.at[2 * k + 1],
            device_id=(b, lax.rem(h + n_height - 1, n_height)), device_id_type=MESH,
        )
        return above, below

    def halo_start(first, last, up, down, k):
        above, below = halo_copies(first, last, up, down, k)

        @pl.when(h < n_height - 1)
        def _():
            above.start()

        @pl.when(h > 0)
        def _():
            below.start()

        @pl.when(h == 0)
        def _():
            up[...] = jnp.zeros(up.shape, F32)

        @pl.when(h == n_height - 1)
        def _():
            down[...] = jnp.zeros(down.shape, F32)

    def halo_wait(first, last, up, down, k):
        above, below = halo_copies(first, last, up, down, k)

        @pl.when(h > 0)
        def _():
            above.wait_recv()

        @pl.when(h < n_height - 1)
        def _():
            below.wait_recv()

    def halo_sent(first, last, up, down, k):
        above, below = halo_copies(first, last, up, down, k)

        @pl.when(h < n_height - 1)
        def _():
            above.wait_send()

        @pl.when(h > 0)
        def _():
            below.wait_send()

    count = counts[0]
    filled = row_valid[0]
    for r in range(1, rows):
        filled = filled + row_valid[r]

    def flag(cond):
        return jnp.where(cond, 1.0, 0.0).astype(F32)

    def own(at):
        return flag((at >= 1) & (at <= filled))

    def ext(at):
        return flag(
            ((at >= 1) & (at <= filled))
            | ((at == 0) & (h > 0))
            | ((at == filled + 1) & (h < n_height - 1))
        )

    def mask(scale, lanes, start=0, size=block):
        return tiled(pix[start : start + size, :] * scale, lanes // 128)

    def block_at(at):
        return pl.ds(at * block if isinstance(at, int) else pl.multiple_of(at * block, block), block)

    def set_last(src, last):
        value = jnp.zeros(last.shape, F32)
        for r in range(rows):
            value = value + src[block_at(r + 1), :] * flag(filled == r + 1)
        last[...] = value

    def patch(ref, up, down):
        ref[block_at(0), :] = up[...]
        ref[block_at(rows + 1), :] = down[...]
        whole = flag(filled == rows)
        ref[block_at(rows), :] = ref[block_at(rows), :] * whole + down[...] * (1.0 - whole)

    iota = lax.broadcasted_iota(jnp.int32, (block, 128), 0)
    pix[...] = jnp.where(((iota >> 4) < count) & ((iota & 15) < cols), 1.0, 0.0)

    def pad_in(src, dst):
        def one(i, carry):
            r, s = i // slots, lax.rem(i, slots)
            live = flag((s < count) & (r < filled))
            dst[i, 0:cols, :] = (src[s, r].astype(F32) * live).astype(BF16)
            dst[i, cols:COLS, :] = jnp.zeros((COLS - cols, width), BF16)
            return carry

        lax.fori_loop(0, rows * slots, one, 0)

    def pad_out(src, dst):
        def one(i, carry):
            r, s = i // slots, lax.rem(i, slots)
            dst[s, r] = src[i, 0:cols, :]
            return carry

        lax.fori_loop(0, rows * slots, one, 0)

    kh, kq = lax.rem(h, 2), h // 2
    pair_one = (b, h + 1 - 2 * kh)
    pair_two = (b, h + 2 - 4 * kq)
    gi = lax.rem(b, GROUP)
    g0 = b - gi
    n_groups = n_batch // GROUP
    g_at = b // GROUP

    class Bucket:
        def __init__(self, at, full, half_, quart, in1, in2, in3, in4, shard, done):
            self.at, self.full, self.half, self.quart = at, full, half_, quart
            self.in1, self.in2, self.in3, self.in4 = in1, in2, in3, in4
            self.shard, self.done = shard, done
            self.size = full.shape[0]
            self.u2, self.u4, self.u32 = self.size // 2, self.size // 4, self.size // (4 * GROUP)
            self.kind = full.dtype
            self.tile = 8 if self.kind == F32 else 16
            self.quarter_at = pl.multiple_of(kh * self.u2 + kq * self.u4, self.tile)
            self.shard_at = pl.multiple_of(self.quarter_at + gi * self.u32, self.tile)

        def remote(self, stage, src, dst, device):
            k = self.at * 8 + stage
            return pltpu.make_async_remote_copy(
                src_ref=src, dst_ref=dst, send_sem=red_send.at[k], recv_sem=red_recv.at[k],
                device_id=device, device_id_type=MESH,
            )

        def halves(self):
            return self.remote(
                0, self.full.at[pl.ds(pl.multiple_of((1 - kh) * self.u2, self.tile), self.u2)], self.in1, pair_one
            )

        def quarters(self):
            return self.remote(
                1, self.half.at[pl.ds(pl.multiple_of((1 - kq) * self.u4, self.tile), self.u4)], self.in2, pair_two
            )

        def start_one(self):
            self.halves().start()

        def start_two(self):
            self.halves().wait_recv()
            step = self.u2 // 4

            def one(i, carry):
                at = pl.multiple_of(i * step, self.tile)
                mine = self.full[pl.ds(pl.multiple_of(kh * self.u2 + at, self.tile), step), :].astype(F32)
                self.half[pl.ds(at, step), :] = (mine + self.in1[pl.ds(at, step), :].astype(F32)).astype(self.kind)
                return carry

            lax.fori_loop(0, 4, one, 0)
            self.quarters().start()

        def pieces(self, t):
            return self.remote(
                2, self.quart.at[pl.ds(pl.multiple_of(t * self.u32, self.tile), self.u32)], self.in3.at[gi], (g0 + t, h)
            )

        def pieces_all(self):
            many = self.in3.at[pl.ds(0, GROUP - 1)]
            return self.remote(2, many, many, (b, h))

        def start_three(self):
            self.quarters().wait_recv()
            step = self.u4 // GROUP

            def one(i, carry):
                at = pl.multiple_of(i * step, self.tile)
                mine = self.half[pl.ds(pl.multiple_of(kq * self.u4 + at, self.tile), step), :].astype(F32)
                self.quart[pl.ds(at, step), :] = (mine + self.in2[pl.ds(at, step), :].astype(F32)).astype(self.kind)
                return carry

            lax.fori_loop(0, GROUP, one, 0)

            def send(j, carry):
                self.pieces(lax.rem(gi + j, GROUP)).start()
                return carry

            lax.fori_loop(1, GROUP, send, 0)
            self.in3[gi] = self.quart[pl.ds(pl.multiple_of(gi * self.u32, self.tile), self.u32), :]

        def others(self, t):
            return self.remote(3, self.shard, self.in4.at[g_at], (t * GROUP + gi, h))

        def others_all(self):
            many = self.in4.at[pl.ds(0, n_groups - 1)]
            return self.remote(3, many, many, (b, h))

        def shards(self, t):
            return self.remote(4, self.done.at[pl.ds(self.shard_at, self.u32)],
                               self.done.at[pl.ds(self.shard_at, self.u32)], (g0 + t, h))

        def shards_all(self):
            many = self.done.at[pl.ds(0, (GROUP - 1) * self.u32)]
            return self.remote(4, many, many, (b, h))

        def start_four(self):
            self.pieces_all().wait_recv()
            value = self.in3[0].astype(F32)
            for t in range(1, GROUP):
                value = value + self.in3[t].astype(F32)
            if n_groups > 1:
                self.shard[...] = value.astype(self.kind)

                def send_group(j, carry):
                    self.others(lax.rem(g_at + j, n_groups)).start()
                    return carry

                lax.fori_loop(1, n_groups, send_group, 0)
                self.in4[g_at] = self.shard[...]
                self.others_all().wait_recv()
                value = self.in4[0].astype(F32)
                for t in range(1, n_groups):
                    value = value + self.in4[t].astype(F32)
            self.done[pl.ds(self.shard_at, self.u32), :] = value.astype(self.kind)

            def send(j, carry):
                self.shards(lax.rem(gi + j, GROUP)).start()
                return carry

            lax.fori_loop(1, GROUP, send, 0)

        def quarter_back(self):
            part = self.done.at[pl.ds(self.quarter_at, self.u4)]
            return self.remote(5, part, part, pair_two)

        def half_back(self):
            part = self.done.at[pl.ds(pl.multiple_of(kh * self.u2, self.tile), self.u2)]
            return self.remote(6, part, part, pair_one)

        def start_five(self):
            self.shards_all().wait_recv()
            self.quarter_back().start()

        def start_six(self):
            self.quarter_back().wait_recv()
            self.half_back().start()

        def finish(self):
            self.half_back().wait_recv()

        def sent(self):
            self.halves().wait_send()
            self.quarters().wait_send()
            self.pieces_all().wait_send()
            if n_groups > 1:
                self.others_all().wait_send()
            self.shards_all().wait_send()
            self.quarter_back().wait_send()
            self.half_back().wait_send()

    bucket_e = Bucket(0, full_e, half_e, quart_e, in1_e, in2_e, in3_e, in4_e, shard_e, done_e)
    bucket_s = Bucket(1, full_s, half_s, quart_s, in1_s, in2_s, in3_s, in4_s, shard_s, done_s)
    bucket_r = Bucket(2, full_r, half_r, quart_r, in1_r, in2_r, in3_r, in4_r, shard_r, done_r)
    bucket_q = Bucket(3, full_q, half_q, quart_q, in1_q, in2_q, in3_q, in4_q, shard_q, done_q)

    loads[0].wait()
    pad_in(img4, x)
    loads[1].wait()
    sum_one = jnp.zeros((1, narrow), F32)
    square_one = jnp.zeros((1, narrow), F32)
    for q in range(rows // 2):
        value = dot(x[pl.ds(q * 2 * slots, 2 * slots)].reshape(2 * block, width), w_reduce[...])
        c1[pl.ds((1 + 2 * q) * block, 2 * block), :] = value
        sum_one = sum_one + colsum(value)
        square_one = square_one + colsum(value * value)
    m1[...] = jnp.zeros(m1.shape, F32)
    put_rows(m1, 0, sum_one)
    put_rows(m1, narrow // 128, square_one)
    m1[4:5, :] = jnp.zeros((1, 128), F32) + count.astype(F32)
    pl.semaphore_wait(barrier, total - 1)
    send_all(m1, s1, 0)
    set_last(c1, last1)
    first1 = c1.at[block_at(1)]
    halo_start(first1, last1, up1, down1, 0)
    loads[3].wait()
    pad_in(cot4, g)

    sum_all(s1, 0)
    slot_total = tot[4:5, :] / n_height
    pix_total = slot_total * area
    m_one = tiled(pix_total, narrow // 128)
    mean = get_rows(tot, 0, narrow // 128) / m_one
    inv_one = lax.rsqrt(get_rows(tot, 2, narrow // 128) / m_one - mean * mean + EPSILON)
    shift_one = mean * inv_one
    scale = inv_one * gain_one[...]
    offset = bias_one[...] - mean * scale
    scale_one, offset_one = scale, offset
    halo_wait(first1, last1, up1, down1, 0)
    patch(c1, up1, down1)

    def hide(at, carry):
        value = c1[block_at(at), :] * scale_one + offset_one
        value = swish(value) * mask(ext(at), narrow)
        hs[0, block_at(at), :] = pltpu.roll(value, 1, axis=0).astype(BF16)
        hs[1, block_at(at), :] = value.astype(BF16)
        hs[2, block_at(at), :] = pltpu.roll(value, block - 1, axis=0).astype(BF16)
        return carry

    lax.fori_loop(0, rows + 2, hide, 0)

    loads[2].wait()
    for q in range(rows // 2):
        for gr in range(2):
            lhs = jnp.concatenate(
                [
                    hs[bb, (a + 2 * q) * block : (a + 2 * q + 2) * block, gr * cg : (gr + 1) * cg]
                    for a in range(3)
                    for bb in range(3)
                ],
                axis=1,
            )
            c2[(1 + 2 * q) * block : (3 + 2 * q) * block, gr * half : (gr + 1) * half] = dot(
                lhs, w_split[:, gr * half : (gr + 1) * half]
            )
    m2[...] = jnp.zeros(m2.shape, F32)
    for j in range(2):
        lanes = pl.ds(j * half, half)

        def moments(r, carry):
            value = c2[block_at(r), lanes] * mask(own(r), half)
            return carry[0] + colsum(value), carry[1] + colsum(value * value)

        zero = jnp.zeros((1, half), F32)
        sums = lax.fori_loop(1, rows + 1, moments, (zero, zero))
        put_rows(m2, j * (half // 128), sums[0])
        put_rows(m2, split // 128 + j * (half // 128), sums[1])
    send_all(m2, s2, 1)
    set_last(c2, last2)
    first2 = c2.at[block_at(1)]
    halo_start(first2, last2, up2, down2, 1)
    x_t[...] = x[...].reshape(pixels, width).T

    sum_all(s2, 1)
    m_two = tiled(pix_total, split // 128)
    mean = get_rows(tot, 0, split // 128) / m_two
    inv_two = lax.rsqrt(get_rows(tot, split // 128, split // 128) / m_two - mean * mean + EPSILON)
    shift_two = mean * inv_two
    scale_two = inv_two * gain_two[...]
    offset_two = bias_two[...] - mean * scale_two
    pool = jnp.zeros((slots, half), F32)
    for j in range(2):
        lanes = pl.ds(j * half, half)
        sc, of = scale_two[:, j * half : (j + 1) * half], offset_two[:, j * half : (j + 1) * half]

        def activate(r, acc):
            value = swish(c2[block_at(r), lanes] * sc + of) * mask(own(r), half)
            act[block_at(r - 1), lanes] = value
            return acc + value

        acc = lax.fori_loop(1, rows + 1, activate, jnp.zeros((block, half), F32))
        pool = pool + per_slot(acc, slots)
    pool = pool / area
    pooled[...] = pool
    loads[4].wait()
    m34[...] = dot(pool, w_squeeze[...], precision=HIGHEST)
    send_all(m34, s34, 2)
    for bb in range(3):
        hs_t[bb] = hs[bb].T

    loads[5].wait()
    all_copy(s34, 2).wait_recv()

    def gather(i, carry):
        value = jnp.sum(s34[pl.ds(i * n_height, n_height)], axis=0)
        sq_all[i] = value
        return carry[0] + colsum(value), carry[1] + colsum(value * value)

    zero = jnp.zeros((1, inner), F32)
    sum_mid, square_mid = lax.fori_loop(0, n_batch, gather, (zero, zero))
    mean = sum_mid / slot_total
    inv_mid = lax.rsqrt(square_mid / slot_total - mean * mean + EPSILON)
    norm_mid = (sq_all[b] - mean) * inv_mid
    pre_mid = norm_mid * gain_mid[...] + bias_mid[...]
    middle = swish(pre_mid)
    logits = dot(middle, w_excite[...], precision=HIGHEST) + bias_excite[...]
    top = jnp.maximum(logits[:, :half], logits[:, half:])
    expo_one = jnp.exp(logits[:, :half] - top)
    expo_two = jnp.exp(logits[:, half:] - top)
    att_one = expo_one / (expo_one + expo_two)
    att_two = expo_two / (expo_one + expo_two)
    att[:, 0:half] = att_one
    att[:, half:split] = att_two
    for s in range(slots):
        attx[s * COLS : (s + 1) * COLS, :] = jnp.broadcast_to(att[s : s + 1, :], (COLS, split))

    def mix(r, carry):
        at = block_at(r)
        mixed[at, :] = (
            attx[:, 0:half] * act[at, 0:half] + attx[:, half:split] * act[at, half:split]
        ).astype(BF16)
        return carry

    lax.fori_loop(0, rows, mix, 0)
    loads[6].wait()
    for j in range(width // 256):
        lanes = pl.ds(j * 256, 256)
        sums = jnp.zeros((1, 256), F32)
        squares = jnp.zeros((1, 256), F32)
        for q in range(rows // 2):
            at = pl.ds(q * 2 * block, 2 * block)
            value = dot(mixed[at, :], w_expand[:, lanes])
            c3[at, lanes] = value
            sums = sums + colsum(value)
            squares = squares + colsum(value * value)
        put_rows(m5, j * 2, sums)
        put_rows(m5, width // 128 + j * 2, squares)
    send_all(m5, s5, 3)
    mixed_t[...] = mixed[...].T
    halo_wait(first2, last2, up2, down2, 1)
    halo_sent(first2, last2, up2, down2, 1)
    patch(c2, up2, down2)
    for j in range(2):
        lanes = pl.ds(j * half, half)
        sc, of = scale_two[:, j * half : (j + 1) * half], offset_two[:, j * half : (j + 1) * half]

        def slopes(at, carry):
            value = swish_slope(c2[block_at(at), lanes] * sc + of)
            slope2[block_at(at), lanes] = value * mask(ext(at), half)
            return carry

        lax.fori_loop(0, rows + 2, slopes, 0)

    def slopes_one(r, carry):
        value = swish_slope(c1[block_at(r + 1), :] * scale_one + offset_one)
        slope1[block_at(r), :] = value * mask(own(r + 1), narrow)
        return carry

    lax.fori_loop(0, rows, slopes_one, 0)

    sum_all(s5, 3)
    wide = width // 128
    m_three = tiled(pix_total, wide)
    mean = get_rows(tot, 0, wide) / m_three
    inv_three = lax.rsqrt(get_rows(tot, wide, wide) / m_three - mean * mean + EPSILON)
    shift_three = mean * inv_three
    scale_three = inv_three * gain_three[...]
    offset_three = bias_three[...] - mean * scale_three
    part = block // 2
    for j in range(width // 256):
        lanes = pl.ds(j * 256, 256)
        cut = slice(j * 256, (j + 1) * 256)
        sc, of = scale_three[:, cut], offset_three[:, cut]
        iv, sh = inv_three[:, cut], shift_three[:, cut]

        def finish_row(i, carry):
            r, k = i // 2, lax.rem(i, 2)
            at = pl.ds(pl.multiple_of(i * part, part), part)
            images_at = pl.ds(i * (slots // 2), slots // 2)
            conv = c3[at, lanes]
            pre = conv * sc + of + x[images_at, :, lanes].reshape(part, 256).astype(F32)
            sigma = sigmoid(pre)
            value = pre * sigma
            live = tiled(pix[pl.ds(pl.multiple_of(k * part, part), part), :] * own(r + 1), 2)
            xo[images_at, :, lanes] = (value * live).astype(BF16).reshape(slots // 2, COLS, 256)
            slope = sigma + value * (1.0 - sigma)
            grad = g[images_at, :, lanes].reshape(part, 256).astype(F32) * slope
            d3[at, lanes] = grad
            return carry[0] + colsum(grad), carry[1] + colsum(grad * (conv * iv - sh))

        zero = jnp.zeros((1, 256), F32)
        sums = lax.fori_loop(0, 2 * rows, finish_row, (zero, zero))
        put_rows(m6, j * 2, sums[0])
        put_rows(m6, wide + j * 2, sums[1])
    send_all(m6, s6, 4)
    pad_out(xo, out4)
    out_copy = pltpu.make_async_copy(out4, output, local_sem.at[7])
    out_copy.start()

    sum_all(s6, 4)
    gb_three = get_rows(tot, 0, wide)
    gg_three = get_rows(tot, wide, wide)
    vectors[0:1, :] = gb_three
    vectors[1:2, :] = gg_three
    gg = gg_three / m_three
    k_one = scale_three
    k_three = k_one * inv_three * gg
    k_two = k_one * (gb_three / m_three - shift_three * gg)
    for j in range(width // 256):
        lanes = pl.ds(j * 256, 256)
        cut = slice(j * 256, (j + 1) * 256)
        ka, kb, kc = k_one[:, cut], k_two[:, cut], k_three[:, cut]

        def back_three(i, carry):
            at = pl.ds(pl.multiple_of(i * part, part), part)
            gc3[at, lanes] = (d3[at, lanes] * ka - kb - c3[at, lanes] * kc).astype(BF16)
            return carry

        lax.fori_loop(0, 2 * rows, back_three, 0)
    for q in range(rows // 2):
        gm[pl.ds((1 + 2 * q) * block, 2 * block), :] = dot(
            gc3[pl.ds(2 * q * block, 2 * block), :], w_expand[...], NT
        )
    set_last(gm, last3)
    first3 = gm.at[block_at(1)]
    halo_start(first3, last3, up3, down3, 2)
    grad_att = []
    for j in range(2):
        lanes = pl.ds(j * half, half)

        def attend(r, acc):
            return acc + gm[block_at(r + 1), :] * act[block_at(r), lanes]

        acc = lax.fori_loop(0, rows, attend, jnp.zeros((block, half), F32))
        grad_att.append(per_slot(acc, slots))
    blend = att_one * grad_att[0] + att_two * grad_att[1]
    grad_logits = jnp.concatenate(
        [att_one * (grad_att[0] - blend), att_two * (grad_att[1] - blend)], axis=1
    )
    em_part = dot(grad_logits, w_excite[...], NT, HIGHEST) * swish_slope(pre_mid)
    em_src[...] = em_part
    m78[0:1, :] = colsum(em_part)
    m78[1:2, :] = colsum(em_part * norm_mid)

    def em_copy(j):
        return pltpu.make_async_remote_copy(
            src_ref=em_src, dst_ref=em_all.at[h], send_sem=em_sems.at[0], recv_sem=em_sems.at[1],
            device_id=(b, lax.rem(h + j, n_height)), device_id_type=MESH,
        )

    for j in range(1, n_height):
        em_copy(j).start()
    em_all[h] = em_src[...]
    send_all(m78, s78, 5)
    for j in range(width // 256):
        full_e[j * narrow : (j + 1) * narrow, :] = dot(
            mixed_t[...], gc3[:, j * 256 : (j + 1) * 256]
        ).astype(BF16)
    bucket_e.start_one()
    grad_excite = dot(middle, grad_logits, TN, HIGHEST)
    base = 9 * cg * 2
    full_s[base : base + inner, :] = grad_excite[:, :half].astype(BF16)
    full_s[base + inner : base + 2 * inner, :] = grad_excite[:, half:].astype(BF16)
    bias_part = colsum(grad_logits)
    put_rows(m10, 2 * (narrow // 128), bias_part)
    bucket_e.start_two()

    sum_all(s78, 5)
    gb_mid, gg_mid = tot[0:1, :], tot[1:2, :]
    vectors[4:5, 0:128] = gb_mid
    vectors[4:5, 128:256] = gg_mid
    many = em_all.at[pl.ds(0, n_height - 1)]
    em_wait = pltpu.make_async_remote_copy(
        src_ref=many, dst_ref=many, send_sem=em_sems.at[0], recv_sem=em_sems.at[1],
        device_id=(b, h), device_id_type=MESH,
    )
    em_wait.wait_recv()
    em = jnp.sum(em_all[...], axis=0)
    slot_live = jnp.where(lax.broadcasted_iota(jnp.int32, (slots, inner), 0) < count, 1.0, 0.0)
    grad_sq = (
        slot_live * inv_mid * gain_mid[...]
        * (em - gb_mid / slot_total - norm_mid * gg_mid / slot_total)
    )
    grad_pooled = dot(grad_sq, w_squeeze[...], NT, HIGHEST) / area
    pooled_grad = dot(pooled[...], grad_sq, TN, HIGHEST)
    att[:, 0:half] = grad_pooled
    for s in range(slots):
        gpx[s * COLS : (s + 1) * COLS, :] = jnp.broadcast_to(att[s : s + 1, 0:half], (COLS, half))
    halo_wait(first3, last3, up3, down3, 2)
    halo_sent(first3, last3, up3, down3, 2)
    patch(gm, up3, down3)
    for j in range(2):
        lanes = pl.ds(j * half, half)
        iv, sh = inv_two[:, j * half : (j + 1) * half], shift_two[:, j * half : (j + 1) * half]

        def back_act(at, carry):
            value = (attx[:, lanes] * gm[block_at(at), :] + gpx[...]) * slope2[block_at(at), lanes]
            d2[block_at(at), lanes] = value
            value = value * own(at)
            norm = c2[block_at(at), lanes] * iv - sh
            return carry[0] + colsum(value), carry[1] + colsum(value * norm)

        zero = jnp.zeros((1, half), F32)
        sums = lax.fori_loop(0, rows + 2, back_act, (zero, zero))
        put_rows(m9, j * (half // 128), sums[0])
        put_rows(m9, split // 128 + j * (half // 128), sums[1])
    send_all(m9, s9, 6)
    full_q[...] = pooled_grad
    bucket_q.start_one()
    bucket_e.start_three()

    sum_all(s9, 6)
    gb_two = get_rows(tot, 0, split // 128)
    gg_two = get_rows(tot, split // 128, split // 128)
    vectors[2:3, 0:split] = gb_two
    vectors[2:3, split : 2 * split] = gg_two
    gg = gg_two / m_two
    k_one = scale_two
    k_three = k_one * inv_two * gg
    k_two = k_one * (gb_two / m_two - shift_two * gg)
    for j in range(2):
        lanes = pl.ds(j * half, half)
        cut = slice(j * half, (j + 1) * half)
        ka, kb, kc = k_one[:, cut], k_two[:, cut], k_three[:, cut]

        def back_two(at, carry):
            value = d2[block_at(at), lanes] * ka - kb - c2[block_at(at), lanes] * kc
            gc2[block_at(at), lanes] = (value * mask(ext(at), half)).astype(BF16)
            return carry

        lax.fori_loop(0, rows + 2, back_two, 0)
    gc2_own[...] = (gc2[block_at(rows), :].astype(F32) * own(rows)).astype(BF16)
    for gr in range(2):
        outs = []
        for bb in range(3):
            lhs = jnp.concatenate(
                [gc2[(2 - a) * block : (2 - a) * block + pixels, gr * half : (gr + 1) * half] for a in range(3)],
                axis=1,
            )
            rhs = jnp.concatenate(
                [
                    w_split[(a * 3 + bb) * cg : (a * 3 + bb + 1) * cg, gr * half : (gr + 1) * half]
                    for a in range(3)
                ],
                axis=1,
            )
            outs.append(dot(lhs, rhs, NT))
        gh[:, gr * cg : (gr + 1) * cg] = (
            outs[1] + pltpu.roll(outs[2], 1, axis=0) + pltpu.roll(outs[0], pixels - 1, axis=0)
        )

    def back_hidden(r, carry):
        value = gh[block_at(r), :] * slope1[block_at(r), :]
        gh[block_at(r), :] = value
        norm = c1[block_at(r + 1), :] * inv_one - shift_one
        return carry[0] + colsum(value), carry[1] + colsum(value * norm)

    zero = jnp.zeros((1, narrow), F32)
    sums = lax.fori_loop(0, rows, back_hidden, (zero, zero))
    put_rows(m10, 0, sums[0])
    put_rows(m10, narrow // 128, sums[1])
    send_all(m10, s10, 7)
    for gr in range(2):
        for bb in range(3):
            lhs = jnp.concatenate(
                [hs_t[bb, gr * cg : (gr + 1) * cg, a * block : a * block + pixels] for a in range(3)], axis=0
            )
            lanes = slice(gr * half, (gr + 1) * half)
            rhs = jnp.concatenate([gc2[block:pixels, lanes], gc2_own[:, lanes]], axis=0)
            value = dot(lhs, rhs)
            for a in range(3):
                at = gr * 9 * cg + (a * 3 + bb) * cg
                full_s[at : at + cg, :] = value[a * cg : (a + 1) * cg].astype(BF16)
    base = base + 2 * inner
    if base < full_s.shape[0]:
        full_s[base:, :] = jnp.zeros((full_s.shape[0] - base, 256), BF16)
    bucket_s.start_one()
    bucket_q.start_two()
    bucket_e.start_four()

    sum_all(s10, 7)
    gb_one = get_rows(tot, 0, narrow // 128)
    gg_one = get_rows(tot, narrow // 128, narrow // 128)
    vectors[3:4, 0:narrow] = gb_one
    vectors[3:4, narrow : 2 * narrow] = gg_one
    vectors[3:4, 2 * narrow : 2 * narrow + split] = get_rows(tot, 2 * (narrow // 128), split // 128)
    gg = gg_one / m_one
    k_one = scale_one
    k_three = k_one * inv_one * gg
    k_two = k_one * (gb_one / m_one - shift_one * gg)

    def back_one(r, carry):
        value = gh[block_at(r), :] * k_one - k_two - c1[block_at(r + 1), :] * k_three
        gc1[block_at(r), :] = (value * mask(own(r + 1), narrow)).astype(BF16)
        return carry

    lax.fori_loop(0, rows, back_one, 0)
    for q in range(2):
        at = q * (width // 2)
        full_r[at : at + width // 2, :] = dot(x_t[at : at + width // 2, :], gc1[...]).astype(BF16)
    bucket_r.start_one()
    bucket_s.start_two()
    bucket_q.start_three()
    bucket_r.start_two()
    bucket_e.start_five()
    out_copy.wait()

    def back_image(r, carry):
        value = d3[block_at(r), :] + dot(gc1[block_at(r), :], w_reduce[...], NT)
        xo[pl.ds(r * slots, slots)] = value.astype(BF16).reshape(slots, COLS, width)
        return carry

    lax.fori_loop(0, rows, back_image, 0)
    bucket_q.start_four()
    bucket_s.start_three()
    bucket_r.start_three()
    bucket_e.start_six()
    pad_out(xo, out4)
    image_copy = pltpu.make_async_copy(out4, grad_images, local_sem.at[7])
    image_copy.start()
    bucket_q.start_five()
    bucket_s.start_four()
    bucket_r.start_four()
    bucket_e.finish()
    copy_e = pltpu.make_async_copy(done_e, big_e, local_sem.at[0])
    copy_e.start()
    bucket_q.start_six()
    bucket_s.start_five()
    bucket_r.start_five()
    bucket_s.start_six()
    bucket_r.start_six()
    bucket_s.finish()
    copy_s = pltpu.make_async_copy(done_s, big_s, local_sem.at[1])
    copy_s.start()
    bucket_q.finish()
    copy_q = pltpu.make_async_copy(done_q, big_q, local_sem.at[3])
    copy_q.start()
    bucket_r.finish()
    copy_r = pltpu.make_async_copy(done_r, big_r, local_sem.at[2])
    copy_r.start()

    for k, dst in enumerate((s1, s2, s34, s5, s6, s78, s9, s10)):
        all_copy(dst, k).wait_send()
    halo_sent(first1, last1, up1, down1, 0)
    em_wait.wait_send()
    bucket_e.sent()
    bucket_s.sent()
    bucket_r.sent()
    bucket_q.sent()
    image_copy.wait()
    copy_e.wait()
    copy_s.wait()
    copy_r.wait()
    copy_q.wait()


def unpack_kernel(
    out_a, gimg_a, big_e, big_s, big_r, big_q, vectors,
    output, grad_images, grad_reduce, grad_gain_one, grad_bias_one, grad_split, grad_gain_two, grad_bias_two,
    grad_squeeze, grad_gain_mid, grad_bias_mid, grad_excite, grad_bias_excite, grad_expand, grad_gain_three,
    grad_bias_three, sems,
):
    one = pltpu.make_async_copy(out_a, output, sems.at[0])
    two = pltpu.make_async_copy(gimg_a, grad_images, sems.at[1])
    one.start()
    two.start()
    narrow = grad_expand.shape[0]
    taps, split = grad_split.shape
    half = split // 2
    inner = grad_excite.shape[0]
    for j in range(grad_expand.shape[1] // 256):
        grad_expand[:, j * 256 : (j + 1) * 256] = big_e[j * narrow : (j + 1) * narrow, :].astype(F32)
    for gr in range(2):
        grad_split[:, gr * half : (gr + 1) * half] = big_s[gr * taps : (gr + 1) * taps, :].astype(F32)
    base = 2 * taps
    for gr in range(2):
        grad_excite[:, gr * half : (gr + 1) * half] = big_s[
            base + gr * inner : base + (gr + 1) * inner, :
        ].astype(F32)
    grad_squeeze[...] = big_q[...]
    grad_reduce[...] = big_r[...].astype(F32)
    grad_bias_three[...] = vectors[0:1, :]
    grad_gain_three[...] = vectors[1:2, :]
    grad_bias_two[...] = vectors[2:3, 0:split]
    grad_gain_two[...] = vectors[2:3, split : 2 * split]
    grad_bias_one[...] = vectors[3:4, 0:narrow]
    grad_gain_one[...] = vectors[3:4, narrow : 2 * narrow]
    grad_bias_excite[...] = vectors[3:4, 2 * narrow : 2 * narrow + split]
    grad_bias_mid[...] = vectors[4:5, 0:inner]
    grad_gain_mid[...] = vectors[4:5, inner : 2 * inner]
    one.wait()
    two.wait()


def shards(
    n_batch, n_height,
    images, counts, row_valid, w_reduce, gain_one, bias_one, w_split, gain_two, bias_two, w_squeeze,
    gain_mid, bias_mid, w_excite, bias_excite, w_expand, gain_three, bias_three, cotangent,
):
    slots, rows, cols, width = images.shape
    narrow = w_reduce.shape[1]
    split = w_split.shape[3]
    taps = 9 * w_split.shape[2]
    inner = w_squeeze.shape[1]
    half = split // 2
    total = n_batch * n_height
    block = slots * COLS
    pixels = rows * block
    padded = pixels + 2 * block
    n_groups = n_batch // GROUP

    def row(v):
        return v.reshape(1, -1)

    unit = 4 * GROUP * 16
    size_e = width // 256 * narrow
    size_s = -(-(2 * taps + 2 * inner) // unit) * unit
    size_r = width

    def bucket(size, lanes=256, kind=BF16):
        cut = size // (4 * GROUP)
        shapes = [
            (size, lanes), (size // 2, lanes), (size // 4, lanes), (size // 2, lanes), (size // 4, lanes),
            (GROUP, cut, lanes), (n_groups, cut, lanes), (cut, lanes), (size, lanes),
        ]
        return [pltpu.VMEM(dims, kind) for dims in shapes]

    heights = [8, 8, 8, 16, 16, 2, 8, 8]
    vm = pltpu.VMEM
    scratch = (
        [vm(images.shape, BF16), vm(images.shape, BF16), vm(images.shape, BF16)]
        + [vm((width, narrow), BF16), vm((taps, split), BF16), vm((narrow, inner), F32), vm((inner, split), F32),
           vm((narrow, width), BF16)]
        + [vm((rows * slots, COLS, width), BF16), vm((rows * slots, COLS, width), BF16), vm((block, 128), F32)]
        + [vm((padded, narrow), F32), vm((3, padded, narrow), BF16), vm((padded, split), F32), vm((pixels, split), F32),
           vm((padded, split), F32), vm((pixels, half), BF16), vm((pixels, width), F32), vm((pixels, width), F32),
           vm((rows * slots, COLS, width), BF16), vm((pixels, width), BF16), vm((padded, half), F32),
           vm((padded, split), F32), vm((padded, split), BF16), vm((pixels, narrow), F32), vm((pixels, narrow), F32),
           vm((pixels, narrow), BF16), vm((block, split), BF16)]
        + [vm((width, pixels), BF16), vm((half, pixels), BF16), vm((3, narrow, padded), BF16), vm((slots, split), F32),
           vm((block, split), F32), vm((block, half), F32), vm((slots, half), F32), vm((n_batch, slots, inner), F32),
           vm((16, 128), F32)]
        + [vm((k, 128), F32) for k in heights] + [vm((slots, inner), F32)]
        + [vm((total, k, 128), F32) for k in heights] + [vm((n_height, slots, inner), F32)]
        + [vm((block, narrow), F32)] * 3 + [vm((block, split), F32)] * 3 + [vm((block, half), F32)] * 3
        + bucket(size_e) + bucket(size_s) + bucket(size_r) + bucket(narrow, inner, F32)
        + [pltpu.SemaphoreType.DMA((8,)), pltpu.SemaphoreType.DMA((8,)), pltpu.SemaphoreType.DMA((8,)),
           pltpu.SemaphoreType.DMA((6,)), pltpu.SemaphoreType.DMA((6,)), pltpu.SemaphoreType.DMA((2,)),
           pltpu.SemaphoreType.DMA((32,)), pltpu.SemaphoreType.DMA((32,))]
    )
    smem = pl.BlockSpec(memory_space=pltpu.SMEM)
    vmem = pl.BlockSpec(memory_space=pltpu.VMEM)
    hbm = pl.BlockSpec(memory_space=pl.ANY)
    shape = jax.ShapeDtypeStruct
    out_a, gimg_a, big_e, big_s, big_r, big_q, vectors = pl.pallas_call(
        functools.partial(main_kernel, n_batch, n_height, images.shape),
        out_shape=(
            shape(images.shape, BF16), shape(images.shape, BF16), shape((size_e, 256), BF16),
            shape((size_s, 256), BF16), shape((size_r, 256), BF16), shape((narrow, inner), F32),
            shape((8, width), F32),
        ),
        in_specs=[smem, smem] + [vmem] * 9 + [hbm] * 7,
        out_specs=[hbm] * 6 + [vmem],
        scratch_shapes=scratch,
        compiler_params=pltpu.CompilerParams(
            collective_id=0, has_side_effects=True, vmem_limit_bytes=58 * 1024 * 1024
        ),
    )(
        counts, row_valid, row(gain_one), row(bias_one), row(gain_two), row(bias_two), row(gain_mid), row(bias_mid),
        row(bias_excite), row(gain_three), row(bias_three),
        images, cotangent, w_reduce, w_split.reshape(taps, split), w_squeeze, w_excite, w_expand,
    )
    outs = pl.pallas_call(
        unpack_kernel,
        out_shape=(
            shape(images.shape, BF16), shape(images.shape, BF16), shape((width, narrow), F32),
            shape((1, narrow), F32), shape((1, narrow), F32), shape((taps, split), F32),
            shape((1, split), F32), shape((1, split), F32), shape((narrow, inner), F32),
            shape((1, inner), F32), shape((1, inner), F32), shape((inner, split), F32),
            shape((1, split), F32), shape((narrow, width), F32), shape((1, width), F32), shape((1, width), F32),
        ),
        in_specs=[hbm, hbm] + [vmem] * 5,
        out_specs=[hbm, hbm] + [vmem] * 14,
        scratch_shapes=[pltpu.SemaphoreType.DMA((2,))],
        compiler_params=pltpu.CompilerParams(vmem_limit_bytes=40 * 1024 * 1024),
    )(out_a, gimg_a, big_e, big_s, big_r, big_q, vectors)
    result = []
    for value, like in zip(outs, (
        None, None, None, gain_one, bias_one, w_split, gain_two, bias_two, None, gain_mid, bias_mid, None, bias_excite,
        None, gain_three, bias_three,
    )):
        result.append(value if like is None else value.reshape(like.shape))
    return tuple(result)


def solution(mesh):
    axes = mesh.shape
    split_in = P("batch", "height", None, None)
    return jax.shard_map(
        functools.partial(shards, axes["batch"], axes["height"]),
        mesh=mesh,
        in_specs=(split_in, P("batch"), P("height")) + (P(),) * 14 + (split_in,),
        out_specs=(split_in, split_in) + (P(),) * 14,
        check_vma=False,
    )
```

```python
import functools

import jax
import jax.numpy as jnp
from jax import lax
from jax.experimental import pallas as pl
from jax.experimental.pallas import tpu as pltpu
from jax.sharding import PartitionSpec as P

IMG_H = 14
IMG_W = 14
EPSILON = 1e-05
MESH = pl.DeviceIdType.MESH
F32 = jnp.float32
BF16 = jnp.bfloat16
HIGHEST = lax.Precision.HIGHEST
COLS = 16
GROUP = 8
NN = (((1,), (0,)), ((), ()))
NT = (((1,), (1,)), ((), ()))
TN = (((0,), (0,)), ((), ()))


def dot(lhs, rhs, dims=NN, precision=None):
    return lax.dot_general(lhs, rhs, dims, precision=precision, preferred_element_type=F32)


def sigmoid(values):
    return 0.5 * jnp.tanh(0.5 * values) + 0.5


def swish(values):
    return values * sigmoid(values)


def swish_slope(values):
    sigma = sigmoid(values)
    return sigma + values * sigma * (1.0 - sigma)


def tiled(row, times):
    return jnp.concatenate([row] * times, axis=1) if times > 1 else row


def colsum(values):
    return jnp.sum(values, axis=0, keepdims=True)


def put_rows(ref, at, row):
    for k in range(row.shape[1] // 128):
        ref[at + k : at + k + 1, :] = row[:, k * 128 : (k + 1) * 128]


def get_rows(ref, at, count):
    return jnp.concatenate([ref[at + k : at + k + 1, :] for k in range(count)], axis=1)


def per_slot(values, slots):
    return jnp.sum(values.reshape(slots, COLS, values.shape[1]), axis=1)


def bucket_parts(size, tile):
    unit = 16 * tile
    first = -(-(size // unit) // 2) * unit
    return [(0, first, "yx"), (first, size - first, "xy")][: 2 if size > first else 1]


def main_kernel(n_batch, n_height, sizes, *refs):
    (
        counts, row_valid, gain_one, bias_one, gain_two, bias_two, gain_mid, bias_mid,
        bias_excite, gain_three, bias_three,
        images, cotangent, w_reduce_in, w_split_in, w_squeeze_in, w_excite_in, w_expand_in,
        output, grad_images, big_e, big_a, big_b, big_r, big_q, vectors,
        img4, cot4, out4, w_reduce, w_split, w_squeeze, w_excite, w_expand,
        x, g, pix, to_pad, from_pad, c1, hs, c2, act, slope2, mixed, c3, d3, xo, gc3, gm, d2, gc2, gh, slope1, gc1,
        gc2_own, x_t, mixed_t, hs_t, att, attx, gpx, pooled, sq_all, tot,
        m1, m2, m34, m5, m6, m78, m9, m10, p5, p6, em_src,
        s1, s2, s34, s5, s6, s78, s9, s10, em_all,
        last1, up1, down1, last2, up2, down2, last3, up3, down3,
        local_sem, all_send, all_recv, pair_send, pair_recv, halo_send, halo_recv, em_sems, red_send, red_recv,
        *bucket_refs,
    ) = refs
    slots, cols, rows, width = sizes
    narrow = w_reduce.shape[1]
    split = w_split.shape[1]
    half = split // 2
    cg = w_split.shape[0] // 9
    inner = w_squeeze.shape[1]
    block = slots * COLS
    pixels = rows * block
    total = n_batch * n_height
    area = float(IMG_H * IMG_W)
    b = lax.axis_index("batch")
    h = lax.axis_index("height")
    me = b * n_height + h

    sends = []
    due = {}

    def arrive(key):
        due.pop(key)()

    def move(key, src, dst):
        copy = pltpu.make_async_copy(src, dst, local_sem.at[key])
        copy.start()
        due["move", key] = copy.wait

    for k, (src, dst) in enumerate(
        [
            (images, img4), (w_reduce_in, w_reduce), (w_split_in, w_split), (cotangent, cot4),
            (w_squeeze_in, w_squeeze), (w_excite_in, w_excite), (w_expand_in, w_expand),
        ]
    ):
        move(k, src, dst)

    barrier = pltpu.get_barrier_semaphore()

    def greet(j, carry):
        t = lax.rem(me + j, total)
        pl.semaphore_signal(
            barrier, inc=1, device_id=(t // n_height, lax.rem(t, n_height)), device_id_type=MESH
        )
        return carry

    lax.fori_loop(1, total, greet, 0)


    kh, kq = lax.rem(h, 2), h // 2
    pair_one = (b, h + 1 - 2 * kh)
    pair_two = (b, h + 2 - 4 * kq)

    def circle(dst):
        if dst.shape[0] == total:
            return me, lambda t: (t // n_height, lax.rem(t, n_height))
        pairs = n_height // 2
        return b * pairs + kq, lambda t: (t // pairs, 2 * lax.rem(t, pairs) + kh)

    def send_all(src, dst, k):
        here, device = circle(dst)
        others = dst.shape[0]

        def one(j, carry):
            pltpu.make_async_remote_copy(
                src_ref=src, dst_ref=dst.at[here], send_sem=all_send.at[k], recv_sem=all_recv.at[k],
                device_id=device(lax.rem(here + j, others)), device_id_type=MESH,
            ).start()
            return carry

        lax.fori_loop(1, others, one, 0)
        dst[here] = src[...]
        sends.append(lambda: all_copy(dst, k).wait_send())
        due["all", k] = lambda: all_copy(dst, k).wait_recv()

    def all_copy(dst, k):
        many = dst.at[pl.ds(0, dst.shape[0] - 1)]
        return pltpu.make_async_remote_copy(
            src_ref=many, dst_ref=many,
            send_sem=all_send.at[k], recv_sem=all_recv.at[k], device_id=(b, h), device_id_type=MESH,
        )

    def send_pairs(src, arrived, dst, k):
        copy = pltpu.make_async_remote_copy(
            src_ref=src, dst_ref=arrived, send_sem=pair_send.at[k], recv_sem=pair_recv.at[k],
            device_id=pair_one, device_id_type=MESH,
        )
        copy.start()
        copy.wait()
        src[...] = src[...] + arrived[...]
        send_all(src, dst, k)

    def sum_all(dst, k):
        arrive(("all", k))

        def one(i, acc):
            return acc + jnp.sum(dst[pl.ds(i * 8, 8)], axis=0)

        acc = lax.fori_loop(0, dst.shape[0] // 8, one, jnp.zeros(dst.shape[1:], F32))
        tot[0 : dst.shape[1], :] = acc

    def halo_copies(first, last, up, down, k):
        above = pltpu.make_async_remote_copy(
            src_ref=last, dst_ref=up, send_sem=halo_send.at[2 * k], recv_sem=halo_recv.at[2 * k],
            device_id=(b, lax.rem(h + 1, n_height)), device_id_type=MESH,
        )
        below = pltpu.make_async_remote_copy(
            src_ref=first, dst_ref=down, send_sem=halo_send.at[2 * k + 1],
            recv_sem=halo_recv.at[2 * k + 1],
            device_id=(b, lax.rem(h + n_height - 1, n_height)), device_id_type=MESH,
        )
        return above, below

    def halo_start(first, last, up, down, k):
        above, below = halo_copies(first, last, up, down, k)

        @pl.when(h < n_height - 1)
        def _():
            above.start()

        @pl.when(h > 0)
        def _():
            below.start()

        sends.append(lambda: halo_sent(first, last, up, down, k))
        due["halo", k] = lambda: halo_here(first, last, up, down, k)

        @pl.when(h == 0)
        def _():
            up[...] = jnp.zeros(up.shape, F32)

        @pl.when(h == n_height - 1)
        def _():
            down[...] = jnp.zeros(down.shape, F32)

    def halo_here(first, last, up, down, k):
        above, below = halo_copies(first, last, up, down, k)

        @pl.when(h > 0)
        def _():
            above.wait_recv()

        @pl.when(h < n_height - 1)
        def _():
            below.wait_recv()

    def halo_sent(first, last, up, down, k):
        above, below = halo_copies(first, last, up, down, k)

        @pl.when(h < n_height - 1)
        def _():
            above.wait_send()

        @pl.when(h > 0)
        def _():
            below.wait_send()

    count = counts[0]
    filled = row_valid[0]
    for r in range(1, rows):
        filled = filled + row_valid[r]

    def flag(cond):
        return jnp.where(cond, 1.0, 0.0).astype(F32)

    def own(at):
        return flag((at >= 1) & (at <= filled))

    def ext(at):
        return flag(
            ((at >= 1) & (at <= filled))
            | ((at == 0) & (h > 0))
            | ((at == filled + 1) & (h < n_height - 1))
        )

    def mask(scale, lanes, start=0, size=block):
        return tiled(pix[start : start + size, :] * scale, lanes // 128)

    def block_at(at):
        return pl.ds(at * block if isinstance(at, int) else pl.multiple_of(at * block, block), block)

    def set_last(src, last):
        value = jnp.zeros(last.shape, F32)
        for r in range(rows):
            value = value + src[block_at(r + 1), :] * flag(filled == r + 1)
        last[...] = value

    def patch(ref, up, down):
        ref[block_at(0), :] = up[...]
        ref[block_at(rows + 1), :] = down[...]
        whole = flag(filled == rows)
        ref[block_at(rows), :] = ref[block_at(rows), :] * whole + down[...] * (1.0 - whole)

    iota = lax.broadcasted_iota(jnp.int32, (block, 128), 0)
    pix[...] = jnp.where(((iota >> 4) < count) & ((iota & 15) < cols), 1.0, 0.0)

    def places(shape, dim):
        at = lax.broadcasted_iota(jnp.int32, shape, dim)
        r, s, c = at // block, (at >> 4) & (slots - 1), at & 15
        return r, s, c, (s * cols + c) * rows + r

    def place_in():
        shape = (pixels, slots * cols * rows)
        r, s, c, at = places(shape, 0)
        live = (c < cols) & (s < count) & (r < filled)
        other = lax.broadcasted_iota(jnp.int32, shape, 1)
        to_pad[...] = jnp.where((other == at) & live, 1.0, 0.0).astype(BF16)

    def place_out():
        shape = (slots * cols * rows, pixels)
        r, s, c, at = places(shape, 1)
        other = lax.broadcasted_iota(jnp.int32, shape, 0)
        from_pad[...] = jnp.where((other == at) & (c < cols), 1.0, 0.0).astype(BF16)

    def pad_in(src, dst):
        value = src[...].reshape(slots * cols * rows, width)
        for q in range(rows):
            at = slice(q * block, (q + 1) * block)
            dst[at, :] = dot(to_pad[at, :], value).astype(BF16)

    def pad_out(src, dst):
        for j in range(width // 256):
            lanes = slice(j * 256, (j + 1) * 256)
            value = dot(from_pad[...], src[:, lanes]).astype(BF16)
            dst[:, :, lanes] = value.reshape(slots * cols, rows, 256)

    bx, bz = lax.rem(b, 2), lax.rem(b // 2, 4)
    group, n_groups = b // GROUP, n_batch // GROUP
    peers = {"y": (kq, pair_two), "x": (bx, (b + 1 - 2 * bx, h))}
    bucket_refs = iter(bucket_refs)

    def add(dst, src, src_at, other, count):
        step = 64 if count % 64 == 0 else count

        def one(i, carry):
            at = pl.multiple_of(i * step, step)
            mine = src[pl.ds(pl.multiple_of(src_at + at, 8), step), :].astype(F32)
            dst[pl.ds(at, step), :] = (mine + other[pl.ds(at, step), :].astype(F32)).astype(dst.dtype)
            return carry

        lax.fori_loop(0, count // step, one, 0)

    class Part:
        def __init__(self, bucket, k, at, size, order):
            self.bucket, self.at, self.size = bucket, at, size
            self.sems = bucket.sems + 8 * (k + 1)
            self.in1, self.sum1, self.in2, self.sum2, self.in3, self.in4, self.shard = (
                next(bucket_refs) for _ in range(7)
            )
            (self.i1, self.peer1), (self.i2, self.peer2) = peers[order[0]], peers[order[1]]
            tile = bucket.tile
            self.u1, self.u2, self.u3 = size // 2, size // 4, size // 16
            self.at1 = pl.multiple_of(bucket.base + at + self.i1 * self.u1, tile)
            self.at2 = pl.multiple_of(self.at1 + self.i2 * self.u2, tile)
            self.at3 = pl.multiple_of(self.at2 + bz * self.u3, tile)

        def copy(self, stage, src, dst, device):
            return self.bucket.remote(self.sems + stage, src, dst, device)

        def launch(self, stage, src, dst, device):
            self.copy(stage, src, dst, device).start()
            self.expect(stage, dst)

        def expect(self, stage, many):
            sends.append(lambda: self.copy(stage, many, many, (b, h)).wait_send())
            due[self.sems, stage] = lambda: self.copy(stage, many, many, (b, h)).wait_recv()

        def cut(self, ref, at, size):
            return ref.at[pl.ds(pl.multiple_of(at, self.bucket.tile), size)]

        def s1(self):
            self.launch(0, self.cut(self.bucket.half, self.at + (1 - self.i1) * self.u1, self.u1), self.in1, self.peer1)

        def s2(self):
            arrive((self.sems, 0))
            add(self.sum1, self.bucket.half, self.at + self.i1 * self.u1, self.in1, self.u1)
            self.launch(1, self.cut(self.sum1, (1 - self.i2) * self.u2, self.u2), self.in2, self.peer2)

        def s3(self):
            arrive((self.sems, 1))
            add(self.sum2, self.sum1, self.i2 * self.u2, self.in2, self.u2)
            for j in range(1, 4):
                t = lax.rem(bz + j, 4)
                device = (b + 2 * (t - bz), h)
                self.copy(2, self.cut(self.sum2, t * self.u3, self.u3), self.in3.at[bz], device).start()
            self.expect(2, self.in3.at[pl.ds(0, 3)])
            self.in3[bz] = self.sum2[pl.ds(pl.multiple_of(bz * self.u3, self.bucket.tile), self.u3), :]

        def s4(self):
            arrive((self.sems, 2))
            value = self.in3[0].astype(F32)
            for t in range(1, 4):
                value = value + self.in3[t].astype(F32)
            kind = self.shard.dtype
            if n_groups > 1:
                self.shard[...] = value.astype(kind)

                def send_group(j, carry):
                    t = lax.rem(group + j, n_groups)
                    device = (b + GROUP * (t - group), h)
                    self.copy(3, self.shard, self.in4.at[group], device).start()
                    return carry

                lax.fori_loop(1, n_groups, send_group, 0)
                self.expect(3, self.in4.at[pl.ds(0, n_groups - 1)])
                self.in4[group] = self.shard[...]
                arrive((self.sems, 3))
                value = self.in4[0].astype(F32)
                for t in range(1, n_groups):
                    value = value + self.in4[t].astype(F32)
            done = self.bucket.done
            done[pl.ds(self.at3, self.u3), :] = self.bucket.final(value, self).astype(kind)
            mine = done.at[pl.ds(self.at3, self.u3)]
            for j in range(1, 4):
                t = lax.rem(bz + j, 4)
                self.copy(4, mine, mine, (b + 2 * (t - bz), h)).start()
            self.expect(4, done.at[pl.ds(0, 3 * self.u3)])

        def s5(self):
            arrive((self.sems, 4))
            mine = self.bucket.done.at[pl.ds(self.at2, self.u2)]
            self.launch(5, mine, mine, self.peer2)

        def s6(self):
            arrive((self.sems, 5))
            mine = self.bucket.done.at[pl.ds(self.at1, self.u1)]
            self.launch(6, mine, mine, self.peer1)

        def s7(self):
            arrive((self.sems, 6))

    class Bucket:
        def __init__(self, at):
            self.full, self.in0, self.half, self.done = (next(bucket_refs) for _ in range(4))
            self.tile = 8 if self.full.dtype == F32 else 16
            self.sems = at * 24
            self.size = self.full.shape[0] // 2
            self.base = pl.multiple_of(kh * self.size, self.tile)
            self.final = lambda value, part: value
            self.parts = [Part(self, k, *spec) for k, spec in enumerate(bucket_parts(self.size, self.tile))]

        def remote(self, k, src, dst, device):
            return pltpu.make_async_remote_copy(
                src_ref=src, dst_ref=dst, send_sem=red_send.at[k], recv_sem=red_recv.at[k],
                device_id=device, device_id_type=MESH,
            )

        def launch(self, stage, src, dst):
            copy = self.remote(self.sems + stage, src, dst, pair_one)
            copy.start()
            sends.append(copy.wait_send)
            due[self.sems, stage] = copy.wait_recv

        def s0(self):
            self.launch(0, self.full.at[pl.ds(pl.multiple_of((1 - kh) * self.size, self.tile), self.size)], self.in0)

        def s1(self):
            arrive((self.sems, 0))
            add(self.half, self.full, self.base, self.in0, self.size)
            for part in self.parts:
                part.s1()

        def s2(self):
            for part in self.parts:
                part.s2()

        def s3(self):
            for part in self.parts:
                part.s3()

        def s4(self):
            for part in self.parts:
                part.s4()

        def s5(self):
            for part in self.parts:
                part.s5()

        def s6(self):
            for part in self.parts:
                part.s6()

        def s7(self):
            for part in self.parts:
                part.s7()
            mine = self.done.at[pl.ds(self.base, self.size)]
            self.launch(1, mine, mine)

        def s8(self):
            arrive((self.sems, 1))

    bucket_e, bucket_a, bucket_b, bucket_r, bucket_q = (Bucket(k) for k in range(5))

    place_in()
    arrive(("move", 0))
    pad_in(img4, x)
    arrive(("move", 1))
    sum_one = jnp.zeros((1, narrow), F32)
    square_one = jnp.zeros((1, narrow), F32)
    for q in range(rows // 2):
        value = dot(x[pl.ds(q * 2 * block, 2 * block), :], w_reduce[...])
        c1[pl.ds((1 + 2 * q) * block, 2 * block), :] = value
        sum_one = sum_one + colsum(value)
        square_one = square_one + colsum(value * value)
    m1[...] = jnp.zeros(m1.shape, F32)
    put_rows(m1, 0, sum_one)
    put_rows(m1, narrow // 128, square_one)
    m1[4:5, :] = jnp.zeros((1, 128), F32) + count.astype(F32)
    pl.semaphore_wait(barrier, total - 1)
    send_all(m1, s1, 0)
    set_last(c1, last1)
    first1 = c1.at[block_at(1)]
    halo_start(first1, last1, up1, down1, 0)
    arrive(("move", 3))
    pad_in(cot4, g)

    sum_all(s1, 0)
    slot_total = tot[4:5, :] / n_height
    pix_total = slot_total * area
    m_one = tiled(pix_total, narrow // 128)
    mean = get_rows(tot, 0, narrow // 128) / m_one
    inv_one = lax.rsqrt(get_rows(tot, 2, narrow // 128) / m_one - mean * mean + EPSILON)
    shift_one = mean * inv_one
    scale = inv_one * gain_one[...]
    offset = bias_one[...] - mean * scale
    scale_one, offset_one = scale, offset
    arrive(("halo", 0))
    patch(c1, up1, down1)

    def hide(at, carry):
        value = c1[block_at(at), :] * scale_one + offset_one
        value = swish(value) * mask(ext(at), narrow)
        hs[0, block_at(at), :] = pltpu.roll(value, 1, axis=0).astype(BF16)
        hs[1, block_at(at), :] = value.astype(BF16)
        hs[2, block_at(at), :] = pltpu.roll(value, block - 1, axis=0).astype(BF16)
        return carry

    lax.fori_loop(0, rows + 2, hide, 0)

    arrive(("move", 2))
    for q in range(rows // 2):
        for gr in range(2):
            lhs = jnp.concatenate(
                [
                    hs[bb, (a + 2 * q) * block : (a + 2 * q + 2) * block, gr * cg : (gr + 1) * cg]
                    for a in range(3)
                    for bb in range(3)
                ],
                axis=1,
            )
            c2[(1 + 2 * q) * block : (3 + 2 * q) * block, gr * half : (gr + 1) * half] = dot(
                lhs, w_split[:, gr * half : (gr + 1) * half]
            )
    m2[...] = jnp.zeros(m2.shape, F32)
    for j in range(2):
        lanes = pl.ds(j * half, half)

        def moments(r, carry):
            value = c2[block_at(r), lanes] * mask(own(r), half)
            return carry[0] + colsum(value), carry[1] + colsum(value * value)

        zero = jnp.zeros((1, half), F32)
        sums = lax.fori_loop(1, rows + 1, moments, (zero, zero))
        put_rows(m2, j * (half // 128), sums[0])
        put_rows(m2, split // 128 + j * (half // 128), sums[1])
    send_all(m2, s2, 1)
    set_last(c2, last2)
    first2 = c2.at[block_at(1)]
    halo_start(first2, last2, up2, down2, 1)
    x_t[...] = x[...].T
    place_out()

    sum_all(s2, 1)
    m_two = tiled(pix_total, split // 128)
    mean = get_rows(tot, 0, split // 128) / m_two
    inv_two = lax.rsqrt(get_rows(tot, split // 128, split // 128) / m_two - mean * mean + EPSILON)
    shift_two = mean * inv_two
    scale_two = inv_two * gain_two[...]
    offset_two = bias_two[...] - mean * scale_two
    pool = jnp.zeros((slots, half), F32)
    for j in range(2):
        lanes = pl.ds(j * half, half)
        sc, of = scale_two[:, j * half : (j + 1) * half], offset_two[:, j * half : (j + 1) * half]

        def activate(r, acc):
            value = swish(c2[block_at(r), lanes] * sc + of) * mask(own(r), half)
            act[block_at(r - 1), lanes] = value
            return acc + value

        acc = lax.fori_loop(1, rows + 1, activate, jnp.zeros((block, half), F32))
        pool = pool + per_slot(acc, slots)
    pool = pool / area
    pooled[...] = pool
    arrive(("move", 4))
    m34[...] = dot(pool, w_squeeze[...], precision=HIGHEST)
    send_all(m34, s34, 2)
    for bb in range(3):
        hs_t[bb] = hs[bb].T

    arrive(("move", 5))
    arrive(("all", 2))

    def gather(i, carry):
        value = jnp.sum(s34[pl.ds(i * n_height, n_height)], axis=0)
        sq_all[i] = value
        return carry[0] + colsum(value), carry[1] + colsum(value * value)

    zero = jnp.zeros((1, inner), F32)
    sum_mid, square_mid = lax.fori_loop(0, n_batch, gather, (zero, zero))
    mean = sum_mid / slot_total
    inv_mid = lax.rsqrt(square_mid / slot_total - mean * mean + EPSILON)
    norm_mid = (sq_all[b] - mean) * inv_mid
    pre_mid = norm_mid * gain_mid[...] + bias_mid[...]
    middle = swish(pre_mid)
    logits = dot(middle, w_excite[...], precision=HIGHEST) + bias_excite[...]
    top = jnp.maximum(logits[:, :half], logits[:, half:])
    expo_one = jnp.exp(logits[:, :half] - top)
    expo_two = jnp.exp(logits[:, half:] - top)
    att_one = expo_one / (expo_one + expo_two)
    att_two = expo_two / (expo_one + expo_two)
    att[:, 0:half] = att_one
    att[:, half:split] = att_two
    for s in range(slots):
        attx[s * COLS : (s + 1) * COLS, :] = jnp.broadcast_to(att[s : s + 1, :], (COLS, split))

    def mix(r, carry):
        at = block_at(r)
        mixed[at, :] = (
            attx[:, 0:half] * act[at, 0:half] + attx[:, half:split] * act[at, half:split]
        ).astype(BF16)
        return carry

    lax.fori_loop(0, rows, mix, 0)
    arrive(("move", 6))
    for j in range(width // 256):
        lanes = pl.ds(j * 256, 256)
        sums = jnp.zeros((1, 256), F32)
        squares = jnp.zeros((1, 256), F32)
        for q in range(rows // 2):
            at = pl.ds(q * 2 * block, 2 * block)
            value = dot(mixed[at, :], w_expand[:, lanes])
            c3[at, lanes] = value
            sums = sums + colsum(value)
            squares = squares + colsum(value * value)
        put_rows(m5, j * 2, sums)
        put_rows(m5, width // 128 + j * 2, squares)
    send_pairs(m5, p5, s5, 3)
    mixed_t[...] = mixed[...].T
    arrive(("halo", 1))
    patch(c2, up2, down2)
    for j in range(2):
        lanes = pl.ds(j * half, half)
        sc, of = scale_two[:, j * half : (j + 1) * half], offset_two[:, j * half : (j + 1) * half]

        def slopes(at, carry):
            value = swish_slope(c2[block_at(at), lanes] * sc + of)
            slope2[block_at(at), lanes] = value * mask(ext(at), half)
            return carry

        lax.fori_loop(0, rows + 2, slopes, 0)

    def slopes_one(r, carry):
        value = swish_slope(c1[block_at(r + 1), :] * scale_one + offset_one)
        slope1[block_at(r), :] = value * mask(own(r + 1), narrow)
        return carry

    lax.fori_loop(0, rows, slopes_one, 0)

    sum_all(s5, 3)
    wide = width // 128
    m_three = tiled(pix_total, wide)
    mean = get_rows(tot, 0, wide) / m_three
    inv_three = lax.rsqrt(get_rows(tot, wide, wide) / m_three - mean * mean + EPSILON)
    shift_three = mean * inv_three
    scale_three = inv_three * gain_three[...]
    offset_three = bias_three[...] - mean * scale_three
    part = block // 2
    for j in range(width // 256):
        lanes = pl.ds(j * 256, 256)
        cut = slice(j * 256, (j + 1) * 256)
        sc, of = scale_three[:, cut], offset_three[:, cut]
        iv, sh = inv_three[:, cut], shift_three[:, cut]

        def finish_row(i, carry):
            r, k = i // 2, lax.rem(i, 2)
            at = pl.ds(pl.multiple_of(i * part, part), part)
            conv = c3[at, lanes]
            pre = conv * sc + of + x[at, lanes].astype(F32)
            sigma = sigmoid(pre)
            value = pre * sigma
            live = tiled(pix[pl.ds(pl.multiple_of(k * part, part), part), :] * own(r + 1), 2)
            xo[at, lanes] = (value * live).astype(BF16)
            slope = sigma + value * (1.0 - sigma)
            grad = g[at, lanes].astype(F32) * slope
            d3[at, lanes] = grad
            return carry[0] + colsum(grad), carry[1] + colsum(grad * (conv * iv - sh))

        zero = jnp.zeros((1, 256), F32)
        sums = lax.fori_loop(0, 2 * rows, finish_row, (zero, zero))
        put_rows(m6, j * 2, sums[0])
        put_rows(m6, wide + j * 2, sums[1])
    send_pairs(m6, p6, s6, 4)
    pad_out(xo, out4)
    move(7, out4, output)

    sum_all(s6, 4)
    gb_three = get_rows(tot, 0, wide)
    gg_three = get_rows(tot, wide, wide)
    vectors[0:1, :] = gb_three
    vectors[1:2, :] = gg_three
    gg = gg_three / m_three
    k_one = scale_three
    k_three = k_one * inv_three * gg
    k_two = k_one * (gb_three / m_three - shift_three * gg)
    for j in range(width // 256):
        lanes = pl.ds(j * 256, 256)
        cut = slice(j * 256, (j + 1) * 256)
        ka, kb, kc = k_one[:, cut], k_two[:, cut], k_three[:, cut]

        def back_three(i, carry):
            at = pl.ds(pl.multiple_of(i * part, part), part)
            gc3[at, lanes] = (d3[at, lanes] * ka - kb - c3[at, lanes] * kc).astype(BF16)
            return carry

        lax.fori_loop(0, 2 * rows, back_three, 0)
    for q in range(rows // 2):
        gm[pl.ds((1 + 2 * q) * block, 2 * block), :] = dot(
            gc3[pl.ds(2 * q * block, 2 * block), :], w_expand[...], NT
        )
    set_last(gm, last3)
    first3 = gm.at[block_at(1)]
    halo_start(first3, last3, up3, down3, 2)
    grad_att = []
    for j in range(2):
        lanes = pl.ds(j * half, half)

        def attend(r, acc):
            return acc + gm[block_at(r + 1), :] * act[block_at(r), lanes]

        acc = lax.fori_loop(0, rows, attend, jnp.zeros((block, half), F32))
        grad_att.append(per_slot(acc, slots))
    blend = att_one * grad_att[0] + att_two * grad_att[1]
    grad_logits = jnp.concatenate(
        [att_one * (grad_att[0] - blend), att_two * (grad_att[1] - blend)], axis=1
    )
    em_part = dot(grad_logits, w_excite[...], NT, HIGHEST) * swish_slope(pre_mid)
    em_src[...] = em_part
    m78[0:1, :] = colsum(em_part)
    m78[1:2, :] = colsum(em_part * norm_mid)

    many = em_all.at[pl.ds(0, n_height - 1)]
    em_wait = pltpu.make_async_remote_copy(
        src_ref=many, dst_ref=many, send_sem=em_sems.at[0], recv_sem=em_sems.at[1],
        device_id=(b, h), device_id_type=MESH,
    )

    def em_copy(j):
        return pltpu.make_async_remote_copy(
            src_ref=em_src, dst_ref=em_all.at[h], send_sem=em_sems.at[0], recv_sem=em_sems.at[1],
            device_id=(b, lax.rem(h + j, n_height)), device_id_type=MESH,
        )

    for j in range(1, n_height):
        em_copy(j).start()
    sends.append(lambda: em_wait.wait_send())
    due["em"] = lambda: em_wait.wait_recv()
    em_all[h] = em_src[...]
    send_all(m78, s78, 5)
    for j in range(width // 256):
        bucket_e.full[j * narrow : (j + 1) * narrow, :] = dot(
            mixed_t[...], gc3[:, j * 256 : (j + 1) * 256]
        ).astype(BF16)
    bucket_e.s0()
    grad_excite = dot(middle, grad_logits, TN, HIGHEST)
    last = bucket_b.full.shape[0] - 2 * inner
    bucket_b.full[last : last + inner, :] = grad_excite[:, :half].astype(BF16)
    bucket_b.full[last + inner :, :] = grad_excite[:, half:].astype(BF16)
    bias_part = colsum(grad_logits)
    put_rows(m10, 2 * (narrow // 128), bias_part)
    bucket_e.s1()

    sum_all(s78, 5)
    gb_mid, gg_mid = tot[0:1, :], tot[1:2, :]
    vectors[4:5, 0:128] = gb_mid
    vectors[4:5, 128:256] = gg_mid
    arrive("em")
    em = jnp.sum(em_all[...], axis=0)
    slot_live = jnp.where(lax.broadcasted_iota(jnp.int32, (slots, inner), 0) < count, 1.0, 0.0)
    grad_sq = (
        slot_live * inv_mid * gain_mid[...]
        * (em - gb_mid / slot_total - norm_mid * gg_mid / slot_total)
    )
    grad_pooled = dot(grad_sq, w_squeeze[...], NT, HIGHEST) / area
    pooled_grad = dot(pooled[...], grad_sq, TN, HIGHEST)
    att[:, 0:half] = grad_pooled
    for s in range(slots):
        gpx[s * COLS : (s + 1) * COLS, :] = jnp.broadcast_to(att[s : s + 1, 0:half], (COLS, half))
    arrive(("halo", 2))
    patch(gm, up3, down3)
    for j in range(2):
        lanes = pl.ds(j * half, half)
        iv, sh = inv_two[:, j * half : (j + 1) * half], shift_two[:, j * half : (j + 1) * half]

        def back_act(at, carry):
            value = (attx[:, lanes] * gm[block_at(at), :] + gpx[...]) * slope2[block_at(at), lanes]
            d2[block_at(at), lanes] = value
            value = value * own(at)
            norm = c2[block_at(at), lanes] * iv - sh
            return carry[0] + colsum(value), carry[1] + colsum(value * norm)

        zero = jnp.zeros((1, half), F32)
        sums = lax.fori_loop(0, rows + 2, back_act, (zero, zero))
        put_rows(m9, j * (half // 128), sums[0])
        put_rows(m9, split // 128 + j * (half // 128), sums[1])
    send_all(m9, s9, 6)
    bucket_q.full[...] = pooled_grad
    bucket_q.s0()
    bucket_e.s2()
    bucket_q.s1()

    sum_all(s9, 6)
    gb_two = get_rows(tot, 0, split // 128)
    gg_two = get_rows(tot, split // 128, split // 128)
    vectors[2:3, 0:split] = gb_two
    vectors[2:3, split : 2 * split] = gg_two
    gg = gg_two / m_two
    k_one = scale_two
    k_three = k_one * inv_two * gg
    k_two = k_one * (gb_two / m_two - shift_two * gg)
    for j in range(2):
        lanes = pl.ds(j * half, half)
        cut = slice(j * half, (j + 1) * half)
        ka, kb, kc = k_one[:, cut], k_two[:, cut], k_three[:, cut]

        def back_two(at, carry):
            value = d2[block_at(at), lanes] * ka - kb - c2[block_at(at), lanes] * kc
            gc2[block_at(at), lanes] = (value * mask(ext(at), half)).astype(BF16)
            return carry

        lax.fori_loop(0, rows + 2, back_two, 0)
    gc2_own[...] = (gc2[block_at(rows), :].astype(F32) * own(rows)).astype(BF16)
    bucket_e.s3()
    bucket_q.s2()

    def taps_grad(gr, bb, dst, at):
        lhs = jnp.concatenate(
            [hs_t[bb, gr * cg : (gr + 1) * cg, a * block : a * block + pixels] for a in range(3)], axis=0
        )
        lanes = slice(gr * half, (gr + 1) * half)
        rhs = jnp.concatenate([gc2[block:pixels, lanes], gc2_own[:, lanes]], axis=0)
        dst[at : at + 3 * cg, :] = dot(lhs, rhs).astype(BF16)

    for k in range(6):
        near = k * 3 * cg < bucket_a.full.shape[0]
        bucket = bucket_a if near else bucket_b
        taps_grad(k // 3, k % 3, bucket.full, k * 3 * cg - (0 if near else bucket_a.full.shape[0]))
        if (k + 1) * 3 * cg == bucket_a.full.shape[0]:
            bucket_a.s0()
    bucket_b.s0()
    bucket_a.s1()
    for gr in range(2):
        outs = []
        for bb in range(3):
            lhs = jnp.concatenate(
                [gc2[(2 - a) * block : (2 - a) * block + pixels, gr * half : (gr + 1) * half] for a in range(3)],
                axis=1,
            )
            rhs = jnp.concatenate(
                [
                    w_split[(a * 3 + bb) * cg : (a * 3 + bb + 1) * cg, gr * half : (gr + 1) * half]
                    for a in range(3)
                ],
                axis=1,
            )
            outs.append(dot(lhs, rhs, NT))
        gh[:, gr * cg : (gr + 1) * cg] = (
            outs[1] + pltpu.roll(outs[2], 1, axis=0) + pltpu.roll(outs[0], pixels - 1, axis=0)
        )

    bucket_b.s1()

    def back_hidden(r, carry):
        value = gh[block_at(r), :] * slope1[block_at(r), :]
        gh[block_at(r), :] = value
        norm = c1[block_at(r + 1), :] * inv_one - shift_one
        return carry[0] + colsum(value), carry[1] + colsum(value * norm)

    zero = jnp.zeros((1, narrow), F32)
    sums = lax.fori_loop(0, rows, back_hidden, (zero, zero))
    put_rows(m10, 0, sums[0])
    put_rows(m10, narrow // 128, sums[1])
    send_all(m10, s10, 7)
    bucket_a.s2()
    bucket_e.s4()
    bucket_q.s3()
    bucket_b.s2()
    sum_all(s10, 7)
    gb_one = get_rows(tot, 0, narrow // 128)
    gg_one = get_rows(tot, narrow // 128, narrow // 128)
    vectors[3:4, 0:narrow] = gb_one
    vectors[3:4, narrow : 2 * narrow] = gg_one
    vectors[3:4, 2 * narrow : 2 * narrow + split] = get_rows(tot, 2 * (narrow // 128), split // 128)
    gg = gg_one / m_one
    k_one = scale_one
    k_three = k_one * inv_one * gg
    k_two = k_one * (gb_one / m_one - shift_one * gg)

    def back_one(r, carry):
        value = gh[block_at(r), :] * k_one - k_two - c1[block_at(r + 1), :] * k_three
        gc1[block_at(r), :] = (value * mask(own(r + 1), narrow)).astype(BF16)
        return carry

    lax.fori_loop(0, rows, back_one, 0)
    for q in range(2):
        at = q * (width // 2)
        bucket_r.full[at : at + width // 2, :] = dot(x_t[at : at + width // 2, :], gc1[...]).astype(BF16)
    bucket_r.s0()
    bucket_a.s3()
    bucket_r.s1()
    bucket_b.s3()
    bucket_e.s5()
    bucket_q.s4()
    arrive(("move", 7))

    def back_image(r, carry):
        value = d3[block_at(r), :] + dot(gc1[block_at(r), :], w_reduce[...], NT)
        xo[block_at(r), :] = value.astype(BF16)
        return carry

    lax.fori_loop(0, rows, back_image, 0)
    bucket_r.s2()
    bucket_a.s4()
    bucket_e.s6()
    bucket_b.s4()
    bucket_r.s3()
    pad_out(xo, out4)
    move(7, out4, grad_images)
    bucket_q.s5()
    bucket_a.s5()
    bucket_e.s7()
    bucket_b.s5()
    bucket_r.s4()
    bucket_q.s6()
    bucket_a.s6()
    bucket_e.s8()
    move(0, bucket_e.done, big_e)
    bucket_b.s6()
    bucket_r.s5()
    bucket_q.s7()
    bucket_a.s7()
    bucket_b.s7()
    bucket_r.s6()
    bucket_q.s8()
    move(3, bucket_q.done, big_q)
    bucket_a.s8()
    move(1, bucket_a.done, big_a)
    bucket_b.s8()
    move(4, bucket_b.done, big_b)
    bucket_r.s7()
    bucket_r.s8()
    move(2, bucket_r.done, big_r)

    for wait in sends:
        wait()
    for key in list(due):
        arrive(key)


def unpack_kernel(
    out_a, gimg_a, big_e, big_a, big_b, big_r, big_q, vectors,
    output, grad_images, grad_reduce, grad_split, grad_squeeze, grad_excite, grad_expand,
    grad_gain_one, grad_bias_one, grad_gain_two, grad_bias_two,
    grad_gain_mid, grad_bias_mid, grad_bias_excite, grad_gain_three, grad_bias_three,
    in_e, in_a, in_b, in_r, in_v, in_o, in_g, in_q, out_e, out_s, out_x, out_r, sems,
):
    def move(k, src, dst):
        copy = pltpu.make_async_copy(src, dst, sems.at[k])
        copy.start()
        return copy

    ins = [move(k, src, dst) for k, (src, dst) in enumerate(
        [(big_e, in_e), (big_a, in_a), (big_b, in_b), (big_r, in_r), (vectors, in_v), (out_a, in_o), (gimg_a, in_g),
         (big_q, in_q)]
    )]
    outs = []
    narrow = grad_expand.shape[0]
    taps, split = grad_split.shape
    half = split // 2
    inner = grad_excite.shape[0]
    ins[0].wait()
    for j in range(grad_expand.shape[1] // 256):
        out_e[:, j * 256 : (j + 1) * 256] = in_e[j * narrow : (j + 1) * narrow, :].astype(F32)
    outs.append(move(8, out_e, grad_expand))
    ins[1].wait()
    ins[2].wait()
    cg = taps // 9
    near = in_a.shape[0]
    for k in range(18):
        gr, bb, a = k // 9, k // 3 % 3, k % 3
        ref, at = (in_a, k * cg) if k * cg < near else (in_b, k * cg - near)
        out_s[(a * 3 + bb) * cg : (a * 3 + bb + 1) * cg, gr * half : (gr + 1) * half] = ref[at : at + cg, :].astype(F32)
    last = in_b.shape[0] - 2 * inner
    for gr in range(2):
        out_x[:, gr * half : (gr + 1) * half] = in_b[last + gr * inner : last + (gr + 1) * inner, :].astype(F32)
    outs.append(move(9, out_s, grad_split))
    outs.append(move(10, out_x, grad_excite))
    ins[3].wait()
    out_r[...] = in_r[...].astype(F32)
    outs.append(move(11, out_r, grad_reduce))
    ins[4].wait()
    grad_bias_three[...] = in_v[0:1, :]
    grad_gain_three[...] = in_v[1:2, :]
    grad_bias_two[...] = in_v[2:3, 0:split]
    grad_gain_two[...] = in_v[2:3, split : 2 * split]
    grad_bias_one[...] = in_v[3:4, 0:narrow]
    grad_gain_one[...] = in_v[3:4, narrow : 2 * narrow]
    grad_bias_excite[...] = in_v[3:4, 2 * narrow : 2 * narrow + split]
    grad_bias_mid[...] = in_v[4:5, 0:inner]
    grad_gain_mid[...] = in_v[4:5, inner : 2 * inner]
    for k, (src, dst) in enumerate([(in_o, output), (in_g, grad_images), (in_q, grad_squeeze)]):
        ins[5 + k].wait()
        outs.append(move(12 + k, src, dst))
    for copy in outs:
        copy.wait()


def shards(
    n_batch, n_height,
    images, counts, row_valid, w_reduce, gain_one, bias_one, w_split, gain_two, bias_two, w_squeeze,
    gain_mid, bias_mid, w_excite, bias_excite, w_expand, gain_three, bias_three, cotangent,
):
    slots, rows, cols, width = images.shape
    count = slots * rows * cols
    narrow = w_reduce.shape[1]
    split = w_split.shape[3]
    taps = 9 * w_split.shape[2]
    inner = w_squeeze.shape[1]
    half = split // 2
    total = n_batch * n_height
    block = slots * COLS
    pixels = rows * block
    padded = pixels + 2 * block
    n_groups = n_batch // GROUP

    def row(v):
        return v.reshape(1, -1)

    unit = 4 * GROUP * 16
    size_e = width // 256 * narrow
    size_a = -(-taps // unit) * unit
    size_b = 2 * taps + 2 * inner - size_a
    size_r = width

    def bucket(size, lanes=256, kind=BF16):
        kept = size // 2
        shapes = [(size, lanes), (kept, lanes), (kept, lanes), (size, lanes)]
        for _, rows_, _ in bucket_parts(kept, 8 if kind == F32 else 16):
            cut = rows_ // 16
            shapes += [(rows_ // 2, lanes)] * 2 + [(rows_ // 4, lanes)] * 2
            shapes += [(4, cut, lanes), (n_groups, cut, lanes), (cut, lanes)]
        return [pltpu.VMEM(dims, kind) for dims in shapes]

    heights = [8, 8, 8, 16, 16, 2, 8, 8]
    vm = pltpu.VMEM
    scratch = (
        [vm((slots * cols, rows, width), BF16)] * 3
        + [vm((width, narrow), BF16), vm((taps, split), BF16), vm((narrow, inner), F32), vm((inner, split), F32),
           vm((narrow, width), BF16)]
        + [vm((pixels, width), BF16), vm((pixels, width), BF16), vm((block, 128), F32), vm((pixels, count), BF16),
           vm((count, pixels), BF16)]
        + [vm((padded, narrow), F32), vm((3, padded, narrow), BF16), vm((padded, split), F32), vm((pixels, split), F32),
           vm((padded, split), F32), vm((pixels, half), BF16), vm((pixels, width), F32), vm((pixels, width), F32),
           vm((pixels, width), BF16), vm((pixels, width), BF16), vm((padded, half), F32),
           vm((padded, split), F32), vm((padded, split), BF16), vm((pixels, narrow), F32), vm((pixels, narrow), F32),
           vm((pixels, narrow), BF16), vm((block, split), BF16)]
        + [vm((width, pixels), BF16), vm((half, pixels), BF16), vm((3, narrow, padded), BF16), vm((slots, split), F32),
           vm((block, split), F32), vm((block, half), F32), vm((slots, half), F32), vm((n_batch, slots, inner), F32),
           vm((16, 128), F32)]
        + [vm((k, 128), F32) for k in heights] + [vm((16, 128), F32)] * 2 + [vm((slots, inner), F32)]
        + [vm((total // 2 if k == 16 else total, k, 128), F32) for k in heights] + [vm((n_height, slots, inner), F32)]
        + [vm((block, narrow), F32)] * 3 + [vm((block, split), F32)] * 3 + [vm((block, half), F32)] * 3
        + [pltpu.SemaphoreType.DMA((8,))] * 5
        + [pltpu.SemaphoreType.DMA((6,)), pltpu.SemaphoreType.DMA((6,)), pltpu.SemaphoreType.DMA((2,)),
           pltpu.SemaphoreType.DMA((120,)), pltpu.SemaphoreType.DMA((120,))]
        + bucket(size_e) + bucket(size_a) + bucket(size_b) + bucket(size_r) + bucket(narrow, inner, F32)
    )
    smem = pl.BlockSpec(memory_space=pltpu.SMEM)
    vmem = pl.BlockSpec(memory_space=pltpu.VMEM)
    hbm = pl.BlockSpec(memory_space=pltpu.HBM)
    shape = jax.ShapeDtypeStruct
    flat = (slots * cols, rows, width)

    def by_column(value):
        return value.transpose(0, 2, 1, 3).reshape(flat)

    def by_row(value):
        return value.reshape(slots, cols, rows, width).transpose(0, 2, 1, 3)

    out_a, gimg_a, big_e, big_a, big_b, big_r, big_q, vectors = pl.pallas_call(
        functools.partial(main_kernel, n_batch, n_height, (slots, cols, rows, width)),
        out_shape=(
            shape(flat, BF16), shape(flat, BF16), shape((size_e, 256), BF16),
            shape((size_a, 256), BF16), shape((size_b, 256), BF16), shape((size_r, 256), BF16), shape((narrow, inner), F32),
            shape((8, width), F32),
        ),
        in_specs=[smem, smem] + [vmem] * 9 + [hbm] * 7,
        out_specs=[hbm] * 7 + [vmem],
        scratch_shapes=scratch,
        compiler_params=pltpu.CompilerParams(
            collective_id=0, has_side_effects=True, vmem_limit_bytes=58 * 1024 * 1024
        ),
    )(
        counts, row_valid, row(gain_one), row(bias_one), row(gain_two), row(bias_two), row(gain_mid), row(bias_mid),
        row(bias_excite), row(gain_three), row(bias_three),
        by_column(images), by_column(cotangent), w_reduce, w_split.reshape(taps, split), w_squeeze, w_excite, w_expand,
    )
    (
        output, grad_images, grad_reduce, grad_split, grad_squeeze, grad_excite, grad_expand,
        grad_gain_one, grad_bias_one, grad_gain_two, grad_bias_two,
        grad_gain_mid, grad_bias_mid, grad_bias_excite, grad_gain_three, grad_bias_three,
    ) = pl.pallas_call(
        unpack_kernel,
        out_shape=(
            shape(flat, BF16), shape(flat, BF16), shape((width, narrow), F32), shape((taps, split), F32),
            shape((narrow, inner), F32), shape((inner, split), F32), shape((narrow, width), F32),
            shape((1, narrow), F32), shape((1, narrow), F32), shape((1, split), F32), shape((1, split), F32),
            shape((1, inner), F32), shape((1, inner), F32), shape((1, split), F32), shape((1, width), F32),
            shape((1, width), F32),
        ),
        in_specs=[hbm] * 8,
        out_specs=[hbm] * 7 + [vmem] * 9,
        scratch_shapes=[
            vm((size_e, 256), BF16), vm((size_a, 256), BF16), vm((size_b, 256), BF16), vm((size_r, 256), BF16), vm((8, width), F32),
            vm(flat, BF16), vm(flat, BF16), vm((narrow, inner), F32),
            vm((narrow, width), F32), vm((taps, split), F32), vm((inner, split), F32), vm((width, narrow), F32),
            pltpu.SemaphoreType.DMA((15,)),
        ],
        compiler_params=pltpu.CompilerParams(vmem_limit_bytes=60 * 1024 * 1024),
    )(out_a, gimg_a, big_e, big_a, big_b, big_r, big_q, vectors)

    def like(value, other):
        return value.reshape(other.shape)

    return (
        by_row(output), by_row(grad_images), grad_reduce, like(grad_gain_one, gain_one), like(grad_bias_one, bias_one),
        like(grad_split, w_split), like(grad_gain_two, gain_two), like(grad_bias_two, bias_two), grad_squeeze,
        like(grad_gain_mid, gain_mid), like(grad_bias_mid, bias_mid), grad_excite, like(grad_bias_excite, bias_excite),
        grad_expand, like(grad_gain_three, gain_three), like(grad_bias_three, bias_three),
    )


def solution(mesh):
    axes = mesh.shape
    split_in = P("batch", "height", None, None)
    return jax.shard_map(
        functools.partial(shards, axes["batch"], axes["height"]),
        mesh=mesh,
        in_specs=(split_in, P("batch"), P("height")) + (P(),) * 14 + (split_in,),
        out_specs=(split_in, split_in) + (P(),) * 14,
        check_vma=False,
    )
```

```python
import functools

import jax
import jax.numpy as jnp
from jax import lax
from jax.experimental import pallas as pl
from jax.experimental.pallas import tpu as pltpu
from jax.sharding import PartitionSpec as P

IMG_H = 14
IMG_W = 14
EPSILON = 1e-05
MESH = pl.DeviceIdType.MESH
F32 = jnp.float32
BF16 = jnp.bfloat16
HIGHEST = lax.Precision.HIGHEST
COLS = 16
GROUP = 8
NN = (((1,), (0,)), ((), ()))
NT = (((1,), (1,)), ((), ()))
TN = (((0,), (0,)), ((), ()))


def dot(lhs, rhs, dims=NN, precision=None):
    return lax.dot_general(lhs, rhs, dims, precision=precision, preferred_element_type=F32)


def sigmoid(values):
    return 0.5 * jnp.tanh(0.5 * values) + 0.5


def swish(values):
    return values * sigmoid(values)


def swish_slope(values):
    sigma = sigmoid(values)
    return sigma + values * sigma * (1.0 - sigma)


def tiled(row, times):
    return jnp.concatenate([row] * times, axis=1) if times > 1 else row


def colsum(values):
    return jnp.sum(values, axis=0, keepdims=True)


def put_rows(ref, at, row):
    for k in range(row.shape[1] // 128):
        piece = row[:, k * 128 : (k + 1) * 128]
        if len(ref.shape) == 3:
            ref[(at + k) // 2, (at + k) % 2 : (at + k) % 2 + 1, :] = piece
        else:
            ref[at + k : at + k + 1, :] = piece


def get_rows(ref, at, count):
    return jnp.concatenate([ref[at + k : at + k + 1, :] for k in range(count)], axis=1)


def per_slot(values, slots):
    return jnp.sum(values.reshape(slots, COLS, values.shape[1]), axis=1)


def main_kernel(n_batch, n_height, sizes, *refs):
    (
        counts, row_valid, *refs,
    ) = refs
    small_in, refs = refs[:9], refs[9:]
    (
        images, cotangent, w_reduce_in, w_split_in, w_squeeze_in, w_excite_in, w_expand_in,
        output, grad_images, big_e, big_a, big_b, big_c, big_r, big_q, vectors,
        gain_one, bias_one, gain_two, bias_two, gain_mid, bias_mid, bias_excite, gain_three, bias_three,
        img4, cot4, out4, w_reduce, w_split, w_squeeze, w_excite, w_expand,
        x, g, pix, to_pad, from_pad, c1, hs, c2, act, slope2, mixed, c3, d3, xo, gc3, gm, slope2n, gc2, gh, slope1, gc1,
        gc2_own, n1, d1, st_src, st_h, st_sum, st_low, st_b, wns, st_tot, x_t, mixed_t, hs_t, att, attx, gpx, pooled, sq_all, tot,
        m1, m2, m34, m5, m6, m78, m10, mx, mxb, p5, p6, em_src,
        s1, s2, s34, s5, s6, s78, s10, sx, sxb, em_all,
        first1, last1, up1, down1, first2, last2, up2, down2, first3, last3, up3, down3,
        local_sem, all_send, all_recv, pair_send, pair_recv, halo_send, halo_recv, red_send, red_recv,
        *bucket_refs,
    ) = refs
    slots, cols, rows, width = sizes
    narrow = w_reduce.shape[1]
    split = w_split.shape[1]
    half = split // 2
    cg = w_split.shape[0] // 9
    inner = w_squeeze.shape[1]
    block = slots * COLS
    pixels = rows * block
    total = n_batch * n_height
    area = float(IMG_H * IMG_W)
    b = lax.axis_index("batch")
    h = lax.axis_index("height")
    me = b * n_height + h

    sends = []
    due = {}

    def arrive(key):
        due.pop(key)()

    def move(key, src, dst):
        copy = pltpu.make_async_copy(src, dst, local_sem.at[key])
        copy.start()
        due["move", key] = copy.wait

    move(0, images, img4)
    move(1, w_reduce_in, w_reduce)
    barrier = pltpu.get_barrier_semaphore()

    def greet(j, carry):
        t = lax.rem(me + j, total)
        pl.semaphore_signal(
            barrier, inc=1, device_id=(t // n_height, lax.rem(t, n_height)), device_id_type=MESH
        )
        return carry

    lax.fori_loop(1, total, greet, 0)
    small = (gain_one, bias_one, gain_two, bias_two, gain_mid, bias_mid, bias_excite, gain_three, bias_three)
    for k, (src, dst) in enumerate(zip(small_in, small)):
        move(8 + k, src, dst)
    move(2, w_split_in, w_split)
    move(3, cotangent, cot4)
    move(4, w_squeeze_in, w_squeeze)
    move(5, w_excite_in, w_excite)
    move(6, w_expand_in, w_expand)


    kh, kq = lax.rem(h, 2), h // 2
    pair_one = (b, h + 1 - 2 * kh)
    pair_two = (b, h + 2 - 4 * kq)

    def circle(dst):
        if dst.shape[0] == total:
            return me, lambda t: (t // n_height, lax.rem(t, n_height))
        pairs = n_height // 2
        return b * pairs + kq, lambda t: (t // pairs, 2 * lax.rem(t, pairs) + kh)

    def send_all(src, dst, k):
        exchange(src, dst, k, *circle(dst))

    def exchange(src, dst, k, here, device):
        others = dst.shape[0]

        def one(j, carry):
            pltpu.make_async_remote_copy(
                src_ref=src, dst_ref=dst.at[here], send_sem=all_send.at[k], recv_sem=all_recv.at[k],
                device_id=device(lax.rem(here + j, others)), device_id_type=MESH,
            ).start()
            return carry

        lax.fori_loop(1, others, one, 0)
        dst[here] = src[...]
        sends.append(lambda: all_copy(dst, k).wait_send())
        due["all", k] = lambda: all_copy(dst, k).wait_recv()

    def all_copy(dst, k):
        many = dst.at[pl.ds(0, dst.shape[0] - 1)]
        return pltpu.make_async_remote_copy(
            src_ref=many, dst_ref=many,
            send_sem=all_send.at[k], recv_sem=all_recv.at[k], device_id=(b, h), device_id_type=MESH,
        )

    def send_pairs(src, arrived, dst, k):
        copy = pltpu.make_async_remote_copy(
            src_ref=src, dst_ref=arrived, send_sem=pair_send.at[k], recv_sem=pair_recv.at[k],
            device_id=pair_one, device_id_type=MESH,
        )
        copy.start()
        copy.wait()
        src[...] = src[...] + arrived[...]
        send_all(src, dst, k)

    def sum_all(dst, k):
        arrive(("all", k))

        def one(i, acc):
            return acc + jnp.sum(dst[pl.ds(i * 8, 8)], axis=0)

        acc = lax.fori_loop(0, dst.shape[0] // 8, one, jnp.zeros(dst.shape[1:], F32))
        if len(dst.shape) == 4:
            for i in range(dst.shape[1]):
                tot[2 * i : 2 * i + 2, :] = acc[i]
        else:
            tot[0 : dst.shape[1], :] = acc

    def halo_copies(first, last, up, down, k):
        above = pltpu.make_async_remote_copy(
            src_ref=last, dst_ref=up, send_sem=halo_send.at[2 * k], recv_sem=halo_recv.at[2 * k],
            device_id=(b, lax.rem(h + 1, n_height)), device_id_type=MESH,
        )
        below = pltpu.make_async_remote_copy(
            src_ref=first, dst_ref=down, send_sem=halo_send.at[2 * k + 1],
            recv_sem=halo_recv.at[2 * k + 1],
            device_id=(b, lax.rem(h + n_height - 1, n_height)), device_id_type=MESH,
        )
        return above, below

    def halo_start(first, last, up, down, k):
        above, below = halo_copies(first, last, up, down, k)

        @pl.when(h < n_height - 1)
        def _():
            above.start()

        @pl.when(h > 0)
        def _():
            below.start()

        sends.append(lambda: halo_sent(first, last, up, down, k))
        due["halo", k] = lambda: halo_here(first, last, up, down, k)

        @pl.when(h == 0)
        def _():
            up[...] = jnp.zeros(up.shape, up.dtype)

        @pl.when(h == n_height - 1)
        def _():
            down[...] = jnp.zeros(down.shape, down.dtype)

    def halo_here(first, last, up, down, k):
        above, below = halo_copies(first, last, up, down, k)

        @pl.when(h > 0)
        def _():
            above.wait_recv()

        @pl.when(h < n_height - 1)
        def _():
            below.wait_recv()

    def halo_sent(first, last, up, down, k):
        above, below = halo_copies(first, last, up, down, k)

        @pl.when(h < n_height - 1)
        def _():
            above.wait_send()

        @pl.when(h > 0)
        def _():
            below.wait_send()

    count = counts[0]
    filled = row_valid[0]
    for r in range(1, rows):
        filled = filled + row_valid[r]

    def flag(cond):
        return jnp.where(cond, 1.0, 0.0).astype(F32)

    def own(at):
        return flag((at >= 1) & (at <= filled))

    def ext(at):
        return flag(
            ((at >= 1) & (at <= filled))
            | ((at == 0) & (h > 0))
            | ((at == filled + 1) & (h < n_height - 1))
        )

    def mask(scale, lanes, start=0, size=block):
        return tiled(pix[start : start + size, :] * scale, lanes // 128)

    def block_at(at):
        return pl.ds(at * block if isinstance(at, int) else pl.multiple_of(at * block, block), block)

    def set_edges(src, first, last):
        first[...] = src[block_at(1), :].astype(first.dtype)
        value = jnp.zeros(last.shape, F32)
        for r in range(IMG_H // n_height - 1, rows):
            value = value + src[block_at(r + 1), :] * flag(filled == r + 1)
        last[...] = value.astype(last.dtype)

    def patch(ref, up, down):
        below = down[...].astype(F32)
        ref[block_at(0), :] = up[...].astype(F32)
        ref[block_at(rows + 1), :] = below
        whole = flag(filled == rows)
        ref[block_at(rows), :] = ref[block_at(rows), :] * whole + below * (1.0 - whole)

    iota = lax.broadcasted_iota(jnp.int32, (block, 128), 0)
    pix[...] = jnp.where(((iota >> 4) < count) & ((iota & 15) < cols), 1.0, 0.0)

    def places(shape, dim):
        at = lax.broadcasted_iota(jnp.int32, shape, dim)
        r, s, c = at // block, (at >> 4) & (slots - 1), at & 15
        return r, s, c, (s * cols + c) * rows + r

    def place_in():
        shape = (pixels, slots * cols * rows)
        r, s, c, at = places(shape, 0)
        live = (c < cols) & (s < count) & (r < filled)
        other = lax.broadcasted_iota(jnp.int32, shape, 1)
        to_pad[...] = jnp.where((other == at) & live, 1.0, 0.0).astype(BF16)

    def place_out():
        shape = (slots * cols * rows, pixels)
        r, s, c, at = places(shape, 1)
        other = lax.broadcasted_iota(jnp.int32, shape, 0)
        from_pad[...] = jnp.where((other == at) & (c < cols), 1.0, 0.0).astype(BF16)

    def pad_in(src, dst):
        value = src[...].reshape(slots * cols * rows, width)
        for q in range(rows):
            at = slice(q * block, (q + 1) * block)
            dst[at, :] = dot(to_pad[at, :], value).astype(BF16)

    def pad_out(src, dst):
        for j in range(width // 256):
            lanes = slice(j * 256, (j + 1) * 256)
            value = dot(from_pad[...], src[:, lanes]).astype(BF16)
            dst[:, :, lanes] = value.reshape(slots * cols, rows, 256)

    bx, bz = lax.rem(b, 2), lax.rem(b // 2, 4)
    group, n_groups = b // GROUP, n_batch // GROUP
    plane = 2 * kq + bx
    bucket_refs = iter(bucket_refs)

    def in_plane(t):
        return (b - bx + lax.rem(t, 2), 2 * (t // 2) + kh)

    def in_line(t):
        return (b + 2 * (t - bz), h)

    class Bucket:
        def __init__(self, at):
            self.full, self.in0, self.half, self.in1, self.sum1, self.in2, self.in3, self.shard, self.done = (
                next(bucket_refs) for _ in range(9)
            )
            self.kind = self.full.dtype
            self.tile = 8 if self.kind == F32 else 16
            self.sems = at * 8
            self.u0 = self.full.shape[0] // 2
            self.u1, self.u2 = self.u0 // 4, self.u0 // 16
            self.at0 = self.whole(kh * self.u0)
            self.at1 = self.whole(self.at0 + plane * self.u1)
            self.at2 = self.whole(self.at1 + bz * self.u2)
            self.final = lambda value: value

        def whole(self, at):
            return pl.multiple_of(at, self.tile)

        def cut(self, ref, at, size):
            return ref.at[pl.ds(self.whole(at), size)]

        def copy(self, stage, src, dst, device):
            k = self.sems + stage
            return pltpu.make_async_remote_copy(
                src_ref=src, dst_ref=dst, send_sem=red_send.at[k], recv_sem=red_recv.at[k],
                device_id=device, device_id_type=MESH,
            )

        def expect(self, stage, many):
            sends.append(lambda: self.copy(stage, many, many, (b, h)).wait_send())
            due["bucket", self.sems + stage] = lambda: self.copy(stage, many, many, (b, h)).wait_recv()

        def arrived(self, stage):
            arrive(("bucket", self.sems + stage))

        def s0(self):
            self.copy(0, self.cut(self.full, (1 - kh) * self.u0, self.u0), self.in0, pair_one).start()
            self.expect(0, self.in0)

        def s1(self):
            self.arrived(0)
            step = self.u1

            def one(i, carry):
                at = self.whole(i * step)
                mine = self.full[pl.ds(self.whole(self.at0 + at), step), :].astype(F32)
                self.half[pl.ds(at, step), :] = (mine + self.in0[pl.ds(at, step), :].astype(F32)).astype(self.kind)
                return carry

            lax.fori_loop(0, 4, one, 0)
            for j in range(1, 4):
                t = lax.rem(plane + j, 4)
                self.copy(1, self.cut(self.half, t * self.u1, self.u1), self.in1.at[j - 1], in_plane(t)).start()
            self.expect(1, self.in1)

        def s2(self):
            self.arrived(1)
            step = self.u2

            def one(i, carry):
                at = self.whole(i * step)
                value = self.half[pl.ds(self.whole(plane * self.u1 + at), step), :].astype(F32)
                for j in range(3):
                    value = value + self.in1[j, pl.ds(at, step), :].astype(F32)
                self.sum1[pl.ds(at, step), :] = value.astype(self.kind)
                return carry

            lax.fori_loop(0, 4, one, 0)
            for j in range(1, 4):
                t = lax.rem(bz + j, 4)
                self.copy(2, self.cut(self.sum1, t * self.u2, self.u2), self.in2.at[j - 1], in_line(t)).start()
            self.expect(2, self.in2)

        def collect(self):
            self.arrived(2)
            value = self.sum1[pl.ds(self.whole(bz * self.u2), self.u2), :].astype(F32)
            for j in range(3):
                value = value + self.in2[j].astype(F32)
            if n_groups > 1:
                self.shard[...] = value.astype(self.kind)

                def send_group(j, carry):
                    t = lax.rem(group + j, n_groups)
                    self.copy(3, self.shard, self.in3.at[group], (b + GROUP * (t - group), h)).start()
                    return carry

                lax.fori_loop(1, n_groups, send_group, 0)
                self.expect(3, self.in3.at[pl.ds(0, n_groups - 1)])
                self.in3[group] = self.shard[...]
                self.arrived(3)
                value = self.in3[0].astype(F32)
                for t in range(1, n_groups):
                    value = value + self.in3[t].astype(F32)
            return value

        def s3(self):
            self.done[pl.ds(self.at2, self.u2), :] = self.final(self.collect()).astype(self.kind)
            mine = self.done.at[pl.ds(self.at2, self.u2)]
            for j in range(1, 4):
                self.copy(4, mine, mine, in_line(lax.rem(bz + j, 4))).start()
            self.expect(4, self.done.at[pl.ds(0, 3 * self.u2)])

        def s4(self):
            self.arrived(4)
            mine = self.done.at[pl.ds(self.at1, self.u1)]
            for j in range(1, 4):
                self.copy(5, mine, mine, in_plane(lax.rem(plane + j, 4))).start()
            self.expect(5, self.done.at[pl.ds(0, 3 * self.u1)])

        def s5(self):
            self.arrived(5)
            mine = self.done.at[pl.ds(self.at0, self.u0)]
            self.copy(6, mine, mine, pair_one).start()
            self.expect(6, mine)

        def s6(self):
            self.arrived(6)

    buckets = [Bucket(k) for k in range(7)]
    bucket_e, bucket_r, bucket_n, bucket_q = buckets[:4]
    taps_buckets = buckets[4:]
    bucket_a, bucket_b, bucket_c = taps_buckets

    def put_taps(at, value):
        start = 0
        for bucket in taps_buckets:
            size = bucket.full.shape[0]
            low, high = max(at, start), min(at + value.shape[0], start + size)
            if low < high:
                bucket.full[low - start : high - start, :] = value[low - at : high - at].astype(BF16)
            start += size

    place_in()
    arrive(("move", 0))
    pad_in(img4, x)
    arrive(("move", 1))
    sum_one = jnp.zeros((1, narrow), F32)
    square_one = jnp.zeros((1, narrow), F32)
    for q in range(rows // 2):
        value = dot(x[pl.ds(q * 2 * block, 2 * block), :], w_reduce[...])
        c1[pl.ds((1 + 2 * q) * block, 2 * block), :] = value
        sum_one = sum_one + colsum(value)
        square_one = square_one + colsum(value * value)
    put_rows(m1, 0, sum_one)
    put_rows(m1, narrow // 128, square_one)
    put_rows(m1, 4, jnp.zeros((1, 256), F32) + count.astype(F32))
    pl.semaphore_wait(barrier, total - 1)
    send_all(m1, s1, 0)
    set_edges(c1, first1, last1)
    halo_start(first1, last1, up1, down1, 0)
    arrive(("move", 3))
    pad_in(cot4, g)
    for j in range(width // 256):
        put_rows(mx, 2 * j, colsum(x[:, j * 256 : (j + 1) * 256].astype(F32)))
    for k in range(9):
        arrive(("move", 8 + k))

    sum_all(s1, 0)
    slot_total = tot[4:5, :] / n_height
    pix_total = slot_total * area
    m_one = tiled(pix_total, narrow // 128)
    mean = get_rows(tot, 0, narrow // 128) / m_one
    inv_one = lax.rsqrt(get_rows(tot, 2, narrow // 128) / m_one - mean * mean + EPSILON)
    shift_one = mean * inv_one
    scale = inv_one * gain_one[...]
    offset = bias_one[...] - mean * scale
    scale_one, offset_one = scale, offset
    arrive(("halo", 0))
    patch(c1, up1, down1)

    def hide(at, carry):
        value = c1[block_at(at), :] * scale_one + offset_one
        value = swish(value) * mask(ext(at), narrow)
        hs[0, block_at(at), :] = pltpu.roll(value, 1, axis=0).astype(BF16)
        hs[1, block_at(at), :] = value.astype(BF16)
        hs[2, block_at(at), :] = pltpu.roll(value, block - 1, axis=0).astype(BF16)
        return carry

    lax.fori_loop(0, rows + 2, hide, 0)

    arrive(("move", 2))
    for q in range(rows // 2):
        for gr in range(2):
            lhs = jnp.concatenate(
                [
                    hs[bb, (a + 2 * q) * block : (a + 2 * q + 2) * block, gr * cg : (gr + 1) * cg]
                    for a in range(3)
                    for bb in range(3)
                ],
                axis=1,
            )
            c2[(1 + 2 * q) * block : (3 + 2 * q) * block, gr * half : (gr + 1) * half] = dot(
                lhs, w_split[:, gr * half : (gr + 1) * half]
            )
    m2[...] = jnp.zeros(m2.shape, F32)
    for j in range(2):
        lanes = pl.ds(j * half, half)

        def moments(r, carry):
            value = c2[block_at(r), lanes] * mask(own(r), half)
            return carry[0] + colsum(value), carry[1] + colsum(value * value)

        zero = jnp.zeros((1, half), F32)
        sums = lax.fori_loop(1, rows + 1, moments, (zero, zero))
        put_rows(m2, j * (half // 128), sums[0])
        put_rows(m2, split // 128 + j * (half // 128), sums[1])
    send_all(m2, s2, 1)
    set_edges(c2, first2, last2)
    halo_start(first2, last2, up2, down2, 1)
    exchange(mx, sx, 8, h, lambda t: (b, t))
    place_out()
    for bb in range(3):
        hs_t[bb] = hs[bb].T

    def slopes_one(r, carry):
        conv = c1[block_at(r + 1), :]
        live = mask(own(r + 1), narrow)
        slope1[block_at(r), :] = swish_slope(conv * scale_one + offset_one) * live
        n1[block_at(r), :] = ((conv * inv_one - shift_one) * live).astype(BF16)
        return carry

    lax.fori_loop(0, rows, slopes_one, 0)

    sum_all(s2, 1)
    m_two = tiled(pix_total, split // 128)
    mean = get_rows(tot, 0, split // 128) / m_two
    inv_two = lax.rsqrt(get_rows(tot, split // 128, split // 128) / m_two - mean * mean + EPSILON)
    shift_two = mean * inv_two
    scale_two = inv_two * gain_two[...]
    offset_two = bias_two[...] - mean * scale_two
    pool = jnp.zeros((slots, half), F32)
    for j in range(2):
        lanes = pl.ds(j * half, half)
        sc, of = scale_two[:, j * half : (j + 1) * half], offset_two[:, j * half : (j + 1) * half]

        def activate(r, acc):
            value = swish(c2[block_at(r), lanes] * sc + of) * mask(own(r), half)
            act[block_at(r - 1), lanes] = value
            return acc + value

        acc = lax.fori_loop(1, rows + 1, activate, jnp.zeros((block, half), F32))
        pool = pool + per_slot(acc, slots)
    pool = pool / area
    pooled[...] = pool
    arrive(("move", 4))
    m34[...] = dot(pool, w_squeeze[...], precision=HIGHEST)
    send_all(m34, s34, 2)
    arrive(("all", 8))
    mxb[...] = jnp.sum(sx[...], axis=0)
    exchange(mxb, sxb, 12, b, lambda t: (t, h))
    arrive(("move", 5))
    arrive(("all", 2))

    def gather(i, carry):
        value = jnp.sum(s34[pl.ds(i * n_height, n_height)], axis=0)
        sq_all[i] = value
        return carry[0] + colsum(value), carry[1] + colsum(value * value)

    zero = jnp.zeros((1, inner), F32)
    sum_mid, square_mid = lax.fori_loop(0, n_batch, gather, (zero, zero))
    mean_mid = sum_mid / slot_total
    inv_mid = lax.rsqrt(square_mid / slot_total - mean_mid * mean_mid + EPSILON)
    norm_mid = (sq_all[b] - mean_mid) * inv_mid
    pre_mid = norm_mid * gain_mid[...] + bias_mid[...]
    middle = swish(pre_mid)
    logits = dot(middle, w_excite[...], precision=HIGHEST) + bias_excite[...]
    top = jnp.maximum(logits[:, :half], logits[:, half:])
    expo_one = jnp.exp(logits[:, :half] - top)
    expo_two = jnp.exp(logits[:, half:] - top)
    att_one = expo_one / (expo_one + expo_two)
    att_two = expo_two / (expo_one + expo_two)
    att[:, 0:half] = att_one
    att[:, half:split] = att_two
    for s in range(slots):
        attx[s * COLS : (s + 1) * COLS, :] = jnp.broadcast_to(att[s : s + 1, :], (COLS, split))

    def mix(r, carry):
        at = block_at(r)
        mixed[at, :] = (
            attx[:, 0:half] * act[at, 0:half] + attx[:, half:split] * act[at, half:split]
        ).astype(BF16)
        return carry

    lax.fori_loop(0, rows, mix, 0)
    arrive(("move", 6))
    for j in range(width // 256):
        lanes = pl.ds(j * 256, 256)
        sums = jnp.zeros((1, 256), F32)
        squares = jnp.zeros((1, 256), F32)
        for q in range(rows // 2):
            at = pl.ds(q * 2 * block, 2 * block)
            value = dot(mixed[at, :], w_expand[:, lanes])
            c3[at, lanes] = value
            sums = sums + colsum(value)
            squares = squares + colsum(value * value)
        put_rows(m5, j * 2, sums)
        put_rows(m5, width // 128 + j * 2, squares)
    send_pairs(m5, p5, s5, 3)
    mixed_t[...] = mixed[...].T
    arrive(("halo", 1))
    patch(c2, up2, down2)
    for j in range(2):
        lanes = pl.ds(j * half, half)
        cut = slice(j * half, (j + 1) * half)
        sc, of = scale_two[:, cut], offset_two[:, cut]
        iv, sh = inv_two[:, cut], shift_two[:, cut]

        def slopes(at, carry):
            conv = c2[block_at(at), lanes]
            value = swish_slope(conv * sc + of) * mask(ext(at), half)
            slope2[block_at(at), lanes] = value
            value = value * own(at)
            more = value * (conv * iv - sh)
            slope2n[block_at(at), lanes] = more
            return carry[0] + value, carry[1] + more

        zero = jnp.zeros((block, half), F32)
        sums = lax.fori_loop(0, rows + 2, slopes, (zero, zero))
        st_src[0:slots, lanes] = per_slot(sums[0], slots)
        st_src[slots : 2 * slots, lanes] = per_slot(sums[1], slots)
    exchange(st_src, st_h, 10, h, lambda t: (b, t))

    sum_all(s5, 3)
    wide = width // 128
    m_three = tiled(pix_total, wide)
    mean = get_rows(tot, 0, wide) / m_three
    inv_three = lax.rsqrt(get_rows(tot, wide, wide) / m_three - mean * mean + EPSILON)
    shift_three = mean * inv_three
    scale_three = inv_three * gain_three[...]
    offset_three = bias_three[...] - mean * scale_three
    part = block // 2
    for j in range(width // 256):
        lanes = pl.ds(j * 256, 256)
        cut = slice(j * 256, (j + 1) * 256)
        sc, of = scale_three[:, cut], offset_three[:, cut]
        iv, sh = inv_three[:, cut], shift_three[:, cut]

        def finish_row(i, carry):
            r, k = i // 2, lax.rem(i, 2)
            at = pl.ds(pl.multiple_of(i * part, part), part)
            conv = c3[at, lanes]
            pre = conv * sc + of + x[at, lanes].astype(F32)
            sigma = sigmoid(pre)
            value = pre * sigma
            live = tiled(pix[pl.ds(pl.multiple_of(k * part, part), part), :] * own(r + 1), 2)
            xo[at, lanes] = (value * live).astype(BF16)
            slope = sigma + value * (1.0 - sigma)
            grad = g[at, lanes].astype(F32) * slope
            d3[at, lanes] = grad
            return carry[0] + colsum(grad), carry[1] + colsum(grad * (conv * iv - sh))

        zero = jnp.zeros((1, 256), F32)
        sums = lax.fori_loop(0, 2 * rows, finish_row, (zero, zero))
        put_rows(m6, j * 2, sums[0])
        put_rows(m6, wide + j * 2, sums[1])
    send_pairs(m6, p6, s6, 4)
    pad_out(xo, out4)
    move(7, out4, output)
    arrive(("all", 12))
    tot[0:8, :] = jnp.sum(sxb[...], axis=0)
    x_mean = get_rows(tot, 0, width // 128) / tiled(pix_total, width // 128)

    def centre(r, carry):
        value = (x[block_at(r), :].astype(F32) - x_mean) * mask(own(r + 1), width)
        x_t[:, block_at(r)] = value.T.astype(BF16)
        return carry

    lax.fori_loop(0, rows, centre, 0)
    for q in range(2):
        at = slice(q * (width // 2), (q + 1) * (width // 2))
        bucket_n.full[at, :] = dot(x_t[at, :], n1[...]).astype(BF16)
    bucket_n.s0()
    arrive(("all", 10))
    st_sum[...] = jnp.sum(st_h[...], axis=0)
    st_low[...] = st_sum[...].astype(BF16)
    exchange(st_low, st_b, 11, b, lambda t: (t, h))

    sum_all(s6, 4)
    gb_three = get_rows(tot, 0, wide)
    gg_three = get_rows(tot, wide, wide)
    vectors[0:1, :] = gb_three
    vectors[1:2, :] = gg_three
    gg = gg_three / m_three
    k_one = scale_three
    k_three = k_one * inv_three * gg
    k_two = k_one * (gb_three / m_three - shift_three * gg)
    for j in range(width // 256):
        lanes = pl.ds(j * 256, 256)
        cut = slice(j * 256, (j + 1) * 256)
        ka, kb, kc = k_one[:, cut], k_two[:, cut], k_three[:, cut]

        def back_three(i, carry):
            at = pl.ds(pl.multiple_of(i * part, part), part)
            gc3[at, lanes] = (d3[at, lanes] * ka - kb - c3[at, lanes] * kc).astype(BF16)
            return carry

        lax.fori_loop(0, 2 * rows, back_three, 0)
    for q in range(rows // 2):
        gm[pl.ds((1 + 2 * q) * block, 2 * block), :] = dot(
            gc3[pl.ds(2 * q * block, 2 * block), :], w_expand[...], NT
        )
    att_sums = [[], [], []]
    for j in range(2):
        lanes = pl.ds(j * half, half)
        parts = [[], [], []]
        for k in range(2):
            zero = jnp.zeros((part, half), F32)

            def attend(r, acc):
                at = pl.ds(pl.multiple_of(r * block + k * part, part), part)
                up_at = pl.ds(pl.multiple_of((r + 1) * block + k * part, part), part)
                value = gm[up_at, :]
                return (
                    acc[0] + value * act[at, lanes],
                    acc[1] + value * own(r + 1) * slope2[up_at, lanes],
                    acc[2] + value * slope2n[up_at, lanes],
                )

            acc = lax.fori_loop(0, rows, attend, (zero, zero, zero))
            for i in range(3):
                parts[i].append(per_slot(acc[i], slots // 2))
        for i in range(3):
            att_sums[i].append(jnp.concatenate(parts[i], axis=0))
    grad_att = att_sums[0]
    blend = att_one * grad_att[0] + att_two * grad_att[1]
    grad_logits = jnp.concatenate(
        [att_one * (grad_att[0] - blend), att_two * (grad_att[1] - blend)], axis=1
    )
    em_part = dot(grad_logits, w_excite[...], NT, HIGHEST) * swish_slope(pre_mid)
    em_src[...] = em_part
    exchange(em_src, em_all, 9, h, lambda t: (b, t))
    mid_scale = inv_mid * gain_mid[...] / area
    pooled_part = dot(em_part * mid_scale, w_squeeze[...], NT, HIGHEST)
    for j in range(2):
        lanes = pl.ds(j * half, half)
        weight = att_one if j == 0 else att_two
        for i in range(2):
            sums = weight * att_sums[1 + i][j] + pooled_part * st_sum[i * slots : (i + 1) * slots, lanes]
            put_rows(m78, (i * 2 + j) * (half // 128), colsum(sums))
    put_rows(m78, 2 * split // 128, colsum(em_part))
    put_rows(m78, 2 * split // 128 + 1, colsum(em_part * norm_mid))
    send_all(m78, s78, 5)
    set_edges(gm, first3, last3)
    halo_start(first3, last3, up3, down3, 2)
    for j in range(width // 256):
        bucket_e.full[j * narrow : (j + 1) * narrow, :] = dot(
            mixed_t[...], gc3[:, j * 256 : (j + 1) * 256]
        ).astype(BF16)
    bucket_e.s0()
    grad_excite = dot(middle, grad_logits, TN, HIGHEST)
    for gr in range(2):
        put_taps(18 * cg + gr * inner, grad_excite[:, gr * half : (gr + 1) * half])
    bias_part = colsum(grad_logits)
    put_rows(m10, 2 * (narrow // 128), bias_part)
    bucket_n.s1()
    arrive(("all", 11))
    every = n_batch * slots
    mid_all = ((sq_all[...] - mean_mid) * inv_mid).reshape(every, inner)
    st_all = st_b[...].astype(F32)
    w_turned = tiled(w_squeeze[...].T, 2)
    for i in range(2):
        sums = st_all[:, i * slots : (i + 1) * slots, :].reshape(every, split)
        wns[:, i * split : (i + 1) * split] = w_turned * dot(mid_all, sums, TN, HIGHEST)
        st_tot[i : i + 1, :] = colsum(sums)
    bucket_e.s1()

    sum_all(s78, 5)
    rows_mid = 2 * split // 128
    gb_mid, gg_mid = tot[rows_mid : rows_mid + 1, :], tot[rows_mid + 1 : rows_mid + 2, :]
    vectors[4:5, 0:128] = gb_mid
    vectors[4:5, 128:256] = gg_mid
    mid_k = mid_scale / slot_total
    pooled_all = dot(jnp.broadcast_to(mid_k * gb_mid, (8, inner)), w_squeeze[...], NT, HIGHEST)[0:1]
    turned = dot(jnp.broadcast_to(mid_k * gg_mid, (8, inner)), wns[...], precision=HIGHEST)[0:1]
    pooled_all = tiled(pooled_all, 2)
    gb_two = get_rows(tot, 0, split // 128) - pooled_all * st_tot[0:1, :] - turned[:, :split]
    gg_two = get_rows(tot, split // 128, split // 128) - pooled_all * st_tot[1:2, :] - turned[:, split:]
    vectors[2:3, 0:split] = gb_two
    vectors[2:3, split : 2 * split] = gg_two
    arrive(("all", 9))
    em = jnp.sum(em_all[...], axis=0)
    slot_live = jnp.where(lax.broadcasted_iota(jnp.int32, (slots, inner), 0) < count, 1.0, 0.0)
    grad_sq = (
        slot_live * inv_mid * gain_mid[...]
        * (em - gb_mid / slot_total - norm_mid * gg_mid / slot_total)
    )
    grad_pooled = dot(grad_sq, w_squeeze[...], NT, HIGHEST) / area
    att[:, 0:half] = grad_pooled
    for s in range(slots):
        gpx[s * COLS : (s + 1) * COLS, :] = jnp.broadcast_to(att[s : s + 1, 0:half], (COLS, half))
    arrive(("halo", 2))
    patch(gm, up3, down3)
    gg = gg_two / m_two
    k_one = scale_two
    k_three = k_one * inv_two * gg
    k_two = k_one * (gb_two / m_two - shift_two * gg)
    for j in range(2):
        lanes = pl.ds(j * half, half)
        cut = slice(j * half, (j + 1) * half)
        ka, kb, kc = k_one[:, cut], k_two[:, cut], k_three[:, cut]

        def back_two(at, carry):
            value = (attx[:, lanes] * gm[block_at(at), :] + gpx[...]) * slope2[block_at(at), lanes]
            value = value * ka - kb - c2[block_at(at), lanes] * kc
            gc2[block_at(at), lanes] = (value * mask(ext(at), half)).astype(BF16)
            return carry

        lax.fori_loop(0, rows + 2, back_two, 0)
    gc2_own[...] = (gc2[block_at(rows), :].astype(F32) * own(rows)).astype(BF16)

    def taps_grad(k):
        gr, bb = k // 3, k % 3
        lhs = jnp.concatenate(
            [hs_t[bb, gr * cg : (gr + 1) * cg, a * block : a * block + pixels] for a in range(3)], axis=0
        )
        lanes = slice(gr * half, (gr + 1) * half)
        rhs = jnp.concatenate([gc2[block:pixels, lanes], gc2_own[:, lanes]], axis=0)
        put_taps(k * 3 * cg, dot(lhs, rhs))

    begun = []
    for k in range(6):
        taps_grad(k)
        ready = 0
        for bucket in taps_buckets[:2]:
            ready += bucket.full.shape[0]
            if ready <= (k + 1) * 3 * cg and bucket not in begun:
                begun.append(bucket)
                bucket.s0()
    bucket_n.s2()
    for gr in range(2):
        outs = []
        for bb in range(3):
            lhs = jnp.concatenate(
                [gc2[(2 - a) * block : (2 - a) * block + pixels, gr * half : (gr + 1) * half] for a in range(3)],
                axis=1,
            )
            rhs = jnp.concatenate(
                [
                    w_split[(a * 3 + bb) * cg : (a * 3 + bb + 1) * cg, gr * half : (gr + 1) * half]
                    for a in range(3)
                ],
                axis=1,
            )
            outs.append(dot(lhs, rhs, NT))
        gh[:, gr * cg : (gr + 1) * cg] = (
            outs[1] + pltpu.roll(outs[2], 1, axis=0) + pltpu.roll(outs[0], pixels - 1, axis=0)
        )

    bucket_a.s1()
    bucket_b.s1()
    bucket_e.s2()

    def back_hidden(r, carry):
        value = gh[block_at(r), :] * slope1[block_at(r), :]
        gh[block_at(r), :] = value
        d1[block_at(r), :] = value.astype(BF16)
        norm = c1[block_at(r + 1), :] * inv_one - shift_one
        return carry[0] + colsum(value), carry[1] + colsum(value * norm)

    zero = jnp.zeros((1, narrow), F32)
    sums = lax.fori_loop(0, rows, back_hidden, (zero, zero))
    put_rows(m10, 0, sums[0])
    put_rows(m10, narrow // 128, sums[1])
    send_all(m10, s10, 7)
    for q in range(2):
        at = slice(q * (width // 2), (q + 1) * (width // 2))
        bucket_r.full[at, :] = dot(x_t[at, :], d1[...]).astype(BF16)
    bucket_r.s0()
    bucket_c.s0()
    bucket_q.full[...] = dot(pooled[...], grad_sq, TN, HIGHEST)
    bucket_q.s0()
    bucket_r.s1()
    bucket_a.s2()
    bucket_e.s3()
    bucket_c.s1()
    bucket_q.s1()
    bucket_b.s2()
    kept_n = bucket_n.collect()
    sum_all(s10, 7)
    gb_one = get_rows(tot, 0, narrow // 128)
    gg_one = get_rows(tot, narrow // 128, narrow // 128)
    vectors[3:4, 0:narrow] = gb_one
    vectors[3:4, narrow : 2 * narrow] = gg_one
    vectors[3:4, 2 * narrow : 2 * narrow + split] = get_rows(tot, 2 * (narrow // 128), split // 128)
    gg = gg_one / m_one
    k_one = scale_one
    k_three = k_one * inv_one * gg
    k_two = k_one * (gb_one / m_one - shift_one * gg)

    def back_one(r, carry):
        value = gh[block_at(r), :] * k_one - k_two - c1[block_at(r + 1), :] * k_three
        gc1[block_at(r), :] = (value * mask(own(r + 1), narrow)).astype(BF16)
        return carry

    lax.fori_loop(0, rows, back_one, 0)
    bucket_r.final = lambda value: scale_one * (value - kept_n * gg)
    arrive(("move", 7))

    def back_image(r, carry):
        value = d3[block_at(r), :] + dot(gc1[block_at(r), :], w_reduce[...], NT)
        xo[block_at(r), :] = value.astype(BF16)
        return carry

    lax.fori_loop(0, rows, back_image, 0)
    bucket_a.s3()
    bucket_r.s2()
    bucket_e.s4()
    bucket_c.s2()
    bucket_q.s2()
    pad_out(xo, out4)
    move(7, out4, grad_images)
    bucket_b.s3()
    bucket_a.s4()
    bucket_r.s3()
    bucket_c.s3()
    bucket_q.s3()
    bucket_e.s5()
    bucket_b.s4()
    bucket_e.s6()
    move(0, bucket_e.done, big_e)
    bucket_a.s5()
    bucket_r.s4()
    bucket_c.s4()
    bucket_q.s4()
    bucket_a.s6()
    move(1, bucket_a.done, big_a)
    bucket_b.s5()
    bucket_q.s5()
    bucket_b.s6()
    move(4, bucket_b.done, big_b)
    bucket_r.s5()
    bucket_c.s5()
    bucket_q.s6()
    move(3, bucket_q.done, big_q)
    bucket_r.s6()
    move(2, bucket_r.done, big_r)
    bucket_c.s6()
    move(5, bucket_c.done, big_c)

    for wait in sends:
        wait()
    for key in list(due):
        arrive(key)


def unpack_kernel(
    out_a, gimg_a, big_e, big_a, big_b, big_c, big_r, big_q, vectors,
    output, grad_images, grad_reduce, grad_split, grad_squeeze, grad_excite, grad_expand,
    grad_gain_one, grad_bias_one, grad_gain_two, grad_bias_two,
    grad_gain_mid, grad_bias_mid, grad_bias_excite, grad_gain_three, grad_bias_three,
    in_e, in_a, in_b, in_c, in_r, in_v, in_o, in_g, in_q, out_e, out_s, out_x, out_r, sems,
):
    def move(k, src, dst):
        copy = pltpu.make_async_copy(src, dst, sems.at[k])
        copy.start()
        return copy

    ins = [move(k, src, dst) for k, (src, dst) in enumerate([
        (out_a, in_o), (big_e, in_e), (gimg_a, in_g), (big_r, in_r), (big_a, in_a), (big_b, in_b), (big_c, in_c),
        (big_q, in_q), (vectors, in_v),
    ])]
    outs = []
    narrow = grad_expand.shape[0]
    taps, split = grad_split.shape
    half = split // 2
    inner = grad_excite.shape[0]
    ins[0].wait()
    outs.append(move(9, in_o, output))
    ins[1].wait()
    for j in range(grad_expand.shape[1] // 256):
        out_e[:, j * 256 : (j + 1) * 256] = in_e[j * narrow : (j + 1) * narrow, :].astype(F32)
    outs.append(move(10, out_e, grad_expand))
    ins[2].wait()
    outs.append(move(11, in_g, grad_images))
    ins[3].wait()
    out_r[...] = in_r[...].astype(F32)
    outs.append(move(12, out_r, grad_reduce))
    for k in range(4, 7):
        ins[k].wait()

    def put(at, dst, to, lanes, size):
        start = 0
        for ref in (in_a, in_b, in_c):
            low, high = max(at, start), min(at + size, start + ref.shape[0])
            if low < high:
                dst[to + low - at : to + high - at, lanes] = ref[low - start : high - start, :].astype(F32)
            start += ref.shape[0]

    cg = taps // 9
    for k in range(18):
        gr, bb, a = k // 9, k // 3 % 3, k % 3
        put(k * cg, out_s, (a * 3 + bb) * cg, slice(gr * half, (gr + 1) * half), cg)
    outs.append(move(13, out_s, grad_split))
    for gr in range(2):
        put(18 * cg + gr * inner, out_x, 0, slice(gr * half, (gr + 1) * half), inner)
    outs.append(move(14, out_x, grad_excite))
    ins[7].wait()
    outs.append(move(15, in_q, grad_squeeze))
    ins[8].wait()
    grad_bias_three[...] = in_v[0:1, :]
    grad_gain_three[...] = in_v[1:2, :]
    grad_bias_two[...] = in_v[2:3, 0:split]
    grad_gain_two[...] = in_v[2:3, split : 2 * split]
    grad_bias_one[...] = in_v[3:4, 0:narrow]
    grad_gain_one[...] = in_v[3:4, narrow : 2 * narrow]
    grad_bias_excite[...] = in_v[3:4, 2 * narrow : 2 * narrow + split]
    grad_bias_mid[...] = in_v[4:5, 0:inner]
    grad_gain_mid[...] = in_v[4:5, inner : 2 * inner]
    for copy in outs:
        copy.wait()


def shards(
    n_batch, n_height,
    images, counts, row_valid, w_reduce, gain_one, bias_one, w_split, gain_two, bias_two, w_squeeze,
    gain_mid, bias_mid, w_excite, bias_excite, w_expand, gain_three, bias_three, cotangent,
):
    slots, rows, cols, width = images.shape
    count = slots * rows * cols
    narrow = w_reduce.shape[1]
    split = w_split.shape[3]
    taps = 9 * w_split.shape[2]
    inner = w_squeeze.shape[1]
    half = split // 2
    total = n_batch * n_height
    block = slots * COLS
    pixels = rows * block
    padded = pixels + 2 * block
    n_groups = n_batch // GROUP

    def row(v):
        return v.reshape(1, -1)

    unit = 4 * GROUP * 16
    size_e = width // 256 * narrow
    size_r = width
    taps_rows = 2 * taps + 2 * inner
    size_a = -(-taps_rows // (5 * unit)) * 2 * unit
    size_c = taps_rows - 2 * size_a

    def bucket(size, lanes=256, kind=BF16):
        kept = size // 2
        shapes = [
            (size, lanes), (kept, lanes), (kept, lanes), (3, kept // 4, lanes), (kept // 4, lanes),
            (3, kept // 16, lanes), (n_groups, kept // 16, lanes), (kept // 16, lanes), (size, lanes),
        ]
        return [pltpu.VMEM(dims, kind) for dims in shapes]

    messages = [(3, 2, 128), (8, 128), (8, 128), (16, 128), (16, 128), (5, 2, 128), (8, 128), (8, 128), (8, 128)]
    vm = pltpu.VMEM
    scratch = (
        [vm((1, k), F32) for k in (narrow, narrow, split, split, inner, inner, split, width, width)]
        + [vm((slots * cols, rows, width), BF16)] * 3
        + [vm((width, narrow), BF16), vm((taps, split), BF16), vm((narrow, inner), F32), vm((inner, split), F32),
           vm((narrow, width), BF16)]
        + [vm((pixels, width), BF16), vm((pixels, width), BF16), vm((block, 128), F32), vm((pixels, count), BF16),
           vm((count, pixels), BF16)]
        + [vm((padded, narrow), F32), vm((3, padded, narrow), BF16), vm((padded, split), F32), vm((pixels, split), F32),
           vm((padded, split), F32), vm((pixels, half), BF16), vm((pixels, width), F32), vm((pixels, width), F32),
           vm((pixels, width), BF16), vm((pixels, width), BF16), vm((padded, half), F32),
           vm((padded, split), F32), vm((padded, split), BF16), vm((pixels, narrow), F32), vm((pixels, narrow), F32),
           vm((pixels, narrow), BF16), vm((block, split), BF16), vm((pixels, narrow), BF16), vm((pixels, narrow), BF16)]
        + [vm((2 * slots, split), F32), vm((n_height, 2 * slots, split), F32), vm((2 * slots, split), F32),
           vm((2 * slots, split), BF16), vm((n_batch, 2 * slots, split), BF16), vm((inner, 2 * split), F32),
           vm((8, split), F32)]
        + [vm((width, pixels), BF16), vm((half, pixels), BF16), vm((3, narrow, padded), BF16), vm((slots, split), F32),
           vm((block, split), F32), vm((block, half), F32), vm((slots, half), F32), vm((n_batch, slots, inner), F32),
           vm((16, 128), F32)]
        + [vm(dims, F32) for dims in messages] + [vm((16, 128), F32)] * 2 + [vm((slots, inner), F32)]
        + [vm((total // 2 if dims[0] == 16 else total,) + dims, F32) for dims in messages[:-2]]
        + [vm((n_height,) + messages[-1], F32), vm((n_batch,) + messages[-1], F32)] + [vm((n_height, slots, inner), F32)]
        + [vm((block, narrow), F32)] * 4 + [vm((block, split), BF16)] * 4 + [vm((block, half), BF16)] * 4
        + [pltpu.SemaphoreType.DMA((k,)) for k in (17, 13, 13, 8, 8, 6, 6, 56, 56)]
        + bucket(size_e) + bucket(size_r) * 2 + bucket(narrow, inner, F32) + bucket(size_a) * 2 + bucket(size_c)
    )
    smem = pl.BlockSpec(memory_space=pltpu.SMEM)
    vmem = pl.BlockSpec(memory_space=pltpu.VMEM)
    hbm = pl.BlockSpec(memory_space=pltpu.HBM)
    shape = jax.ShapeDtypeStruct
    flat = (slots * cols, rows, width)

    def by_column(value):
        return value.transpose(0, 2, 1, 3).reshape(flat)

    def by_row(value):
        return value.reshape(slots, cols, rows, width).transpose(0, 2, 1, 3)

    out_a, gimg_a, big_e, big_a, big_b, big_c, big_r, big_q, vectors = pl.pallas_call(
        functools.partial(main_kernel, n_batch, n_height, (slots, cols, rows, width)),
        out_shape=(
            shape(flat, BF16), shape(flat, BF16), shape((size_e, 256), BF16),
            shape((size_a, 256), BF16), shape((size_a, 256), BF16), shape((size_c, 256), BF16), shape((size_r, 256), BF16),
            shape((narrow, inner), F32),
            shape((8, width), F32),
        ),
        in_specs=[smem, smem] + [hbm] * 16,
        out_specs=[hbm] * 8 + [vmem],
        scratch_shapes=scratch,
        compiler_params=pltpu.CompilerParams(
            collective_id=0, has_side_effects=True, vmem_limit_bytes=58 * 1024 * 1024
        ),
    )(
        counts, row_valid, row(gain_one), row(bias_one), row(gain_two), row(bias_two), row(gain_mid), row(bias_mid),
        row(bias_excite), row(gain_three), row(bias_three),
        by_column(images), by_column(cotangent), w_reduce, w_split.reshape(taps, split), w_squeeze, w_excite, w_expand,
    )
    (
        output, grad_images, grad_reduce, grad_split, grad_squeeze, grad_excite, grad_expand,
        grad_gain_one, grad_bias_one, grad_gain_two, grad_bias_two,
        grad_gain_mid, grad_bias_mid, grad_bias_excite, grad_gain_three, grad_bias_three,
    ) = pl.pallas_call(
        unpack_kernel,
        out_shape=(
            shape(flat, BF16), shape(flat, BF16), shape((width, narrow), F32), shape((taps, split), F32),
            shape((narrow, inner), F32), shape((inner, split), F32), shape((narrow, width), F32),
            shape((1, narrow), F32), shape((1, narrow), F32), shape((1, split), F32), shape((1, split), F32),
            shape((1, inner), F32), shape((1, inner), F32), shape((1, split), F32), shape((1, width), F32),
            shape((1, width), F32),
        ),
        in_specs=[hbm] * 9,
        out_specs=[hbm] * 7 + [vmem] * 9,
        scratch_shapes=[
            vm((size_e, 256), BF16), vm((size_a, 256), BF16), vm((size_a, 256), BF16), vm((size_c, 256), BF16), vm((size_r, 256), BF16),
            vm((8, width), F32),
            vm(flat, BF16), vm(flat, BF16), vm((narrow, inner), F32),
            vm((narrow, width), F32), vm((taps, split), F32), vm((inner, split), F32), vm((width, narrow), F32),
            pltpu.SemaphoreType.DMA((16,)),
        ],
        compiler_params=pltpu.CompilerParams(vmem_limit_bytes=60 * 1024 * 1024),
    )(out_a, gimg_a, big_e, big_a, big_b, big_c, big_r, big_q, vectors)

    def like(value, other):
        return value.reshape(other.shape)

    return (
        by_row(output), by_row(grad_images), grad_reduce, like(grad_gain_one, gain_one), like(grad_bias_one, bias_one),
        like(grad_split, w_split), like(grad_gain_two, gain_two), like(grad_bias_two, bias_two), grad_squeeze,
        like(grad_gain_mid, gain_mid), like(grad_bias_mid, bias_mid), grad_excite, like(grad_bias_excite, bias_excite),
        grad_expand, like(grad_gain_three, gain_three), like(grad_bias_three, bias_three),
    )


def solution(mesh):
    axes = mesh.shape
    split_in = P("batch", "height", None, None)
    return jax.shard_map(
        functools.partial(shards, axes["batch"], axes["height"]),
        mesh=mesh,
        in_specs=(split_in, P("batch"), P("height")) + (P(),) * 14 + (split_in,),
        out_specs=(split_in, split_in) + (P(),) * 14,
        check_vma=False,
    )
```

```python
import functools

import jax
import jax.numpy as jnp
from jax import lax
from jax.experimental import pallas as pl
from jax.experimental.pallas import tpu as pltpu
from jax.sharding import PartitionSpec as P

IMG_H = 14
IMG_W = 14
EPSILON = 1e-05
MESH = pl.DeviceIdType.MESH
F32 = jnp.float32
BF16 = jnp.bfloat16
HIGHEST = lax.Precision.HIGHEST
COLS = 16
GROUP = 8
NN = (((1,), (0,)), ((), ()))
NT = (((1,), (1,)), ((), ()))
TN = (((0,), (0,)), ((), ()))


def dot(lhs, rhs, dims=NN, precision=None):
    return lax.dot_general(lhs, rhs, dims, precision=precision, preferred_element_type=F32)


def sigmoid(values):
    return 0.5 * jnp.tanh(0.5 * values) + 0.5


def swish(values):
    return values * sigmoid(values)


def swish_slope(values):
    sigma = sigmoid(values)
    return sigma + values * sigma * (1.0 - sigma)


def tiled(row, times):
    return jnp.concatenate([row] * times, axis=1) if times > 1 else row


def colsum(values):
    return jnp.sum(values, axis=0, keepdims=True)


def put_rows(ref, at, row):
    for k in range(row.shape[1] // 128):
        piece = row[:, k * 128 : (k + 1) * 128]
        if len(ref.shape) == 3:
            ref[(at + k) // 2, (at + k) % 2 : (at + k) % 2 + 1, :] = piece
        else:
            ref[at + k : at + k + 1, :] = piece


def get_rows(ref, at, count):
    return jnp.concatenate([ref[at + k : at + k + 1, :] for k in range(count)], axis=1)


def per_slot(values, slots):
    return jnp.sum(values.reshape(slots, COLS, values.shape[1]), axis=1)


def main_kernel(n_batch, n_height, sizes, *refs):
    (
        counts_in, row_valid_in, *refs,
    ) = refs
    small_in, refs = refs[:9], refs[9:]
    (
        images, cotangent, w_reduce_in, w_split_in, w_squeeze_in, w_excite_in, w_expand_in,
        output, grad_images, big_e, big_a, big_b, big_c, big_r, big_q, vectors_out,
        gain_one, bias_one, gain_two, bias_two, gain_mid, bias_mid, bias_excite, gain_three, bias_three,
        img4, cot4, out4, w_reduce, w_split, w_squeeze, w_excite, w_expand,
        x, g, pix, to_pad, from_pad, c1, hs, c2, act, slope2, mixed, c3, d3, xo, gc3, gm, slope2n, gc2, gh, slope1, gc1,
        gc2_own, n1, d1, st_src, st_h, st_sum, st_low, st_b, wns, st_tot, x_t, mixed_t, hs_t, att, attx, gpx, pooled, sq_all, tot,
        m1, m2, m34, m5, m6, m78, m10, mx, mxb, p5, p6, vectors, pool_h, pool_sum, pool_b, em_sum, em_b, squeeze_grad, em_src,
        s1, s2, s34, s5, s6, s78, s10, sx, sxb, em_all,
        first1, last1, up1, down1, first2, last2, up2, down2, first3, last3, up3, down3,
        counts, row_valid, local_sem, all_send, all_recv, pair_send, pair_recv, halo_send, halo_recv, red_send, red_recv,
        *bucket_refs,
    ) = refs
    slots, cols, rows, width = sizes
    narrow = w_reduce.shape[1]
    split = w_split.shape[1]
    half = split // 2
    cg = w_split.shape[0] // 9
    inner = w_squeeze.shape[1]
    block = slots * COLS
    pixels = rows * block
    total = n_batch * n_height
    area = float(IMG_H * IMG_W)
    b = lax.axis_index("batch")
    h = lax.axis_index("height")
    me = b * n_height + h

    sends = []
    due = {}

    def arrive(key):
        due.pop(key)()

    def move(key, src, dst):
        copy = pltpu.make_async_copy(src, dst, local_sem.at[key])
        copy.start()
        due["move", key] = copy.wait

    move(17, counts_in, counts)
    move(18, row_valid_in, row_valid)
    move(0, images, img4)
    move(1, w_reduce_in, w_reduce)
    barrier = pltpu.get_barrier_semaphore()

    def greet(j, carry):
        t = lax.rem(me + j, total)
        pl.semaphore_signal(
            barrier, inc=1, device_id=(t // n_height, lax.rem(t, n_height)), device_id_type=MESH
        )
        return carry

    lax.fori_loop(1, total, greet, 0)
    small = (gain_one, bias_one, gain_two, bias_two, gain_mid, bias_mid, bias_excite, gain_three, bias_three)
    for k, (src, dst) in enumerate(zip(small_in, small)):
        move(8 + k, src, dst)
    move(2, w_split_in, w_split)
    move(3, cotangent, cot4)
    move(4, w_squeeze_in, w_squeeze)
    move(5, w_excite_in, w_excite)
    move(6, w_expand_in, w_expand)


    kh, kq = lax.rem(h, 2), h // 2
    pair_one = (b, h + 1 - 2 * kh)
    pair_two = (b, h + 2 - 4 * kq)

    def circle(dst):
        if dst.shape[0] == total:
            return me, lambda t: (t // n_height, lax.rem(t, n_height))
        pairs = n_height // 2
        return b * pairs + kq, lambda t: (t // pairs, 2 * lax.rem(t, pairs) + kh)

    def send_all(src, dst, k):
        exchange(src, dst, k, *circle(dst))

    def exchange(src, dst, k, here, device):
        others = dst.shape[0]

        def one(j, carry):
            t = jnp.where(2 * here < others, others - 1 - j, j)

            @pl.when(t != here)
            def _():
                pltpu.make_async_remote_copy(
                    src_ref=src, dst_ref=dst.at[here], send_sem=all_send.at[k], recv_sem=all_recv.at[k],
                    device_id=device(t), device_id_type=MESH,
                ).start()

            return carry

        lax.fori_loop(0, others, one, 0)
        dst[here] = src[...]
        sends.append(lambda: all_copy(dst, k).wait_send())
        due["all", k] = lambda: all_copy(dst, k).wait_recv()

    def all_copy(dst, k):
        many = dst.at[pl.ds(0, dst.shape[0] - 1)]
        return pltpu.make_async_remote_copy(
            src_ref=many, dst_ref=many,
            send_sem=all_send.at[k], recv_sem=all_recv.at[k], device_id=(b, h), device_id_type=MESH,
        )

    def send_pairs(src, arrived, dst, k):
        copy = pltpu.make_async_remote_copy(
            src_ref=src, dst_ref=arrived, send_sem=pair_send.at[k], recv_sem=pair_recv.at[k],
            device_id=pair_one, device_id_type=MESH,
        )
        copy.start()
        copy.wait()
        src[...] = src[...] + arrived[...]
        send_all(src, dst, k)

    def sum_all(dst, k):
        arrive(("all", k))

        def one(i, acc):
            return acc + jnp.sum(dst[pl.ds(i * 8, 8)].astype(F32), axis=0)

        acc = lax.fori_loop(0, dst.shape[0] // 8, one, jnp.zeros(dst.shape[1:], F32))
        if len(dst.shape) == 4:
            for i in range(dst.shape[1]):
                tot[2 * i : 2 * i + 2, :] = acc[i]
        else:
            tot[0 : dst.shape[1], :] = acc

    def halo_copies(first, last, up, down, k):
        above = pltpu.make_async_remote_copy(
            src_ref=last, dst_ref=up, send_sem=halo_send.at[2 * k], recv_sem=halo_recv.at[2 * k],
            device_id=(b, lax.rem(h + 1, n_height)), device_id_type=MESH,
        )
        below = pltpu.make_async_remote_copy(
            src_ref=first, dst_ref=down, send_sem=halo_send.at[2 * k + 1],
            recv_sem=halo_recv.at[2 * k + 1],
            device_id=(b, lax.rem(h + n_height - 1, n_height)), device_id_type=MESH,
        )
        return above, below

    def halo_start(first, last, up, down, k):
        above, below = halo_copies(first, last, up, down, k)

        @pl.when(h < n_height - 1)
        def _():
            above.start()

        @pl.when(h > 0)
        def _():
            below.start()

        sends.append(lambda: halo_sent(first, last, up, down, k))
        due["halo", k] = lambda: halo_here(first, last, up, down, k)

        @pl.when(h == 0)
        def _():
            up[...] = jnp.zeros(up.shape, up.dtype)

        @pl.when(h == n_height - 1)
        def _():
            down[...] = jnp.zeros(down.shape, down.dtype)

    def halo_here(first, last, up, down, k):
        above, below = halo_copies(first, last, up, down, k)

        @pl.when(h > 0)
        def _():
            above.wait_recv()

        @pl.when(h < n_height - 1)
        def _():
            below.wait_recv()

    def halo_sent(first, last, up, down, k):
        above, below = halo_copies(first, last, up, down, k)

        @pl.when(h < n_height - 1)
        def _():
            above.wait_send()

        @pl.when(h > 0)
        def _():
            below.wait_send()

    arrive(("move", 17))
    arrive(("move", 18))
    count = counts[0]
    filled = row_valid[0]
    for r in range(1, rows):
        filled = filled + row_valid[r]

    def flag(cond):
        return jnp.where(cond, 1.0, 0.0).astype(F32)

    def own(at):
        return flag((at >= 1) & (at <= filled))

    def ext(at):
        return flag(
            ((at >= 1) & (at <= filled))
            | ((at == 0) & (h > 0))
            | ((at == filled + 1) & (h < n_height - 1))
        )

    def mask(scale, lanes, start=0, size=block):
        return tiled(pix[start : start + size, :] * scale, lanes // 128)

    def block_at(at):
        return pl.ds(at * block if isinstance(at, int) else pl.multiple_of(at * block, block), block)

    def set_edges(src, first, last):
        first[...] = src[block_at(1), :].astype(first.dtype)
        value = jnp.zeros(last.shape, F32)
        for r in range(IMG_H // n_height - 1, rows):
            value = value + src[block_at(r + 1), :] * flag(filled == r + 1)
        last[...] = value.astype(last.dtype)

    def patch(ref, up, down):
        below = down[...].astype(F32)
        ref[block_at(0), :] = up[...].astype(F32)
        ref[block_at(rows + 1), :] = below
        whole = flag(filled == rows)
        ref[block_at(rows), :] = ref[block_at(rows), :] * whole + below * (1.0 - whole)

    iota = lax.broadcasted_iota(jnp.int32, (block, 128), 0)
    pix[...] = jnp.where(((iota >> 4) < count) & ((iota & 15) < cols), 1.0, 0.0)

    def places(shape, dim):
        at = lax.broadcasted_iota(jnp.int32, shape, dim)
        r, s, c = at // block, (at >> 4) & (slots - 1), at & 15
        return r, s, c, (s * cols + c) * rows + r

    def place_in():
        shape = (pixels, slots * cols * rows)
        r, s, c, at = places(shape, 0)
        live = (c < cols) & (s < count) & (r < filled)
        other = lax.broadcasted_iota(jnp.int32, shape, 1)
        to_pad[...] = jnp.where((other == at) & live, 1.0, 0.0).astype(BF16)

    def place_out():
        shape = (slots * cols * rows, pixels)
        r, s, c, at = places(shape, 1)
        other = lax.broadcasted_iota(jnp.int32, shape, 0)
        from_pad[...] = jnp.where((other == at) & (c < cols), 1.0, 0.0).astype(BF16)

    def pad_in(src, dst):
        value = src[...].reshape(slots * cols * rows, width)
        for q in range(rows):
            at = slice(q * block, (q + 1) * block)
            dst[at, :] = dot(to_pad[at, :], value).astype(BF16)

    def pad_out(src, dst):
        for j in range(width // 256):
            lanes = slice(j * 256, (j + 1) * 256)
            value = dot(from_pad[...], src[:, lanes]).astype(BF16)
            dst[:, :, lanes] = value.reshape(slots * cols, rows, 256)

    bx, bz = lax.rem(b, 2), lax.rem(b // 2, 4)
    group, n_groups = b // GROUP, n_batch // GROUP
    plane = 2 * kq + bx
    bucket_refs = iter(bucket_refs)

    def in_plane(t):
        return (b - bx + lax.rem(t, 2), 2 * (t // 2) + kh)

    def in_line(t):
        return (b + 2 * (t - bz), h)

    class Bucket:
        def __init__(self, at):
            self.full, self.in0, self.half, self.in1, self.sum1, self.in2, self.in3, self.shard, self.done = (
                next(bucket_refs) for _ in range(9)
            )
            self.kind = self.full.dtype
            self.tile = 8 if self.kind == F32 else 16
            self.sems = at * 8
            self.u0 = self.full.shape[0] // 2
            self.u1, self.u2 = self.u0 // 4, self.u0 // 16
            self.at0 = self.whole(kh * self.u0)
            self.at1 = self.whole(self.at0 + plane * self.u1)
            self.at2 = self.whole(self.at1 + bz * self.u2)
            self.final = lambda value: value

        def whole(self, at):
            return pl.multiple_of(at, self.tile)

        def cut(self, ref, at, size):
            return ref.at[pl.ds(self.whole(at), size)]

        def copy(self, stage, src, dst, device):
            k = self.sems + stage
            return pltpu.make_async_remote_copy(
                src_ref=src, dst_ref=dst, send_sem=red_send.at[k], recv_sem=red_recv.at[k],
                device_id=device, device_id_type=MESH,
            )

        def expect(self, stage, many):
            sends.append(lambda: self.copy(stage, many, many, (b, h)).wait_send())
            due["bucket", self.sems + stage] = lambda: self.copy(stage, many, many, (b, h)).wait_recv()

        def arrived(self, stage):
            arrive(("bucket", self.sems + stage))

        def s0(self):
            self.copy(0, self.cut(self.full, (1 - kh) * self.u0, self.u0), self.in0, pair_one).start()
            self.expect(0, self.in0)

        def s1(self):
            self.arrived(0)
            step = self.u1

            def one(i, carry):
                at = self.whole(i * step)
                mine = self.full[pl.ds(self.whole(self.at0 + at), step), :].astype(F32)
                self.half[pl.ds(at, step), :] = (mine + self.in0[pl.ds(at, step), :].astype(F32)).astype(self.kind)
                return carry

            lax.fori_loop(0, 4, one, 0)
            for j in range(1, 4):
                t = lax.rem(plane + j, 4)
                self.copy(1, self.cut(self.half, t * self.u1, self.u1), self.in1.at[j - 1], in_plane(t)).start()
            self.expect(1, self.in1)

        def s2(self):
            self.arrived(1)
            step = self.u2

            def one(i, carry):
                at = self.whole(i * step)
                value = self.half[pl.ds(self.whole(plane * self.u1 + at), step), :].astype(F32)
                for j in range(3):
                    value = value + self.in1[j, pl.ds(at, step), :].astype(F32)
                self.sum1[pl.ds(at, step), :] = value.astype(self.kind)
                return carry

            lax.fori_loop(0, 4, one, 0)
            for j in range(1, 4):
                t = lax.rem(bz + j, 4)
                self.copy(2, self.cut(self.sum1, t * self.u2, self.u2), self.in2.at[j - 1], in_line(t)).start()
            self.expect(2, self.in2)

        def collect(self):
            self.arrived(2)
            value = self.sum1[pl.ds(self.whole(bz * self.u2), self.u2), :].astype(F32)
            for j in range(3):
                value = value + self.in2[j].astype(F32)
            if n_groups > 1:
                self.shard[...] = value.astype(self.kind)

                def send_group(j, carry):
                    t = lax.rem(group + j, n_groups)
                    self.copy(3, self.shard, self.in3.at[group], (b + GROUP * (t - group), h)).start()
                    return carry

                lax.fori_loop(1, n_groups, send_group, 0)
                self.expect(3, self.in3.at[pl.ds(0, n_groups - 1)])
                self.in3[group] = self.shard[...]
                self.arrived(3)
                value = self.in3[0].astype(F32)
                for t in range(1, n_groups):
                    value = value + self.in3[t].astype(F32)
            return value

        def s3(self):
            self.done[pl.ds(self.at2, self.u2), :] = self.final(self.collect()).astype(self.kind)
            mine = self.done.at[pl.ds(self.at2, self.u2)]
            for j in range(1, 4):
                self.copy(4, mine, mine, in_line(lax.rem(bz + j, 4))).start()
            self.expect(4, self.done.at[pl.ds(0, 3 * self.u2)])

        def s4(self):
            self.arrived(4)
            mine = self.done.at[pl.ds(self.at1, self.u1)]
            for j in range(1, 4):
                self.copy(5, mine, mine, in_plane(lax.rem(plane + j, 4))).start()
            self.expect(5, self.done.at[pl.ds(0, 3 * self.u1)])

        def s5(self):
            self.arrived(5)
            mine = self.done.at[pl.ds(self.at0, self.u0)]
            self.copy(6, mine, mine, pair_one).start()
            self.expect(6, mine)

        def s6(self):
            self.arrived(6)

    buckets = [Bucket(k) for k in range(6)]
    bucket_e, bucket_r, bucket_n = buckets[:3]
    taps_buckets = buckets[3:]
    bucket_a, bucket_b, bucket_c = taps_buckets

    def put_taps(at, value):
        start = 0
        for bucket in taps_buckets:
            size = bucket.full.shape[0]
            low, high = max(at, start), min(at + value.shape[0], start + size)
            if low < high:
                bucket.full[low - start : high - start, :] = value[low - at : high - at].astype(BF16)
            start += size

    place_in()
    arrive(("move", 0))
    pad_in(img4, x)
    arrive(("move", 1))
    sum_one = jnp.zeros((1, narrow), F32)
    square_one = jnp.zeros((1, narrow), F32)
    for q in range(rows // 2):
        value = dot(x[pl.ds(q * 2 * block, 2 * block), :], w_reduce[...])
        c1[pl.ds((1 + 2 * q) * block, 2 * block), :] = value
        sum_one = sum_one + colsum(value)
        square_one = square_one + colsum(value * value)
    put_rows(m1, 0, sum_one)
    put_rows(m1, narrow // 128, square_one)
    put_rows(m1, 4, jnp.zeros((1, 256), F32) + count.astype(F32))
    pl.semaphore_wait(barrier, total - 1)
    send_all(m1, s1, 0)
    set_edges(c1, first1, last1)
    halo_start(first1, last1, up1, down1, 0)
    arrive(("move", 3))
    pad_in(cot4, g)
    for j in range(width // 256):
        put_rows(mx, 2 * j, colsum(x[:, j * 256 : (j + 1) * 256].astype(F32)))
    exchange(mx, sx, 8, h, lambda t: (b, t))
    for k in range(9):
        arrive(("move", 8 + k))

    sum_all(s1, 0)
    slot_total = tot[4:5, :] / n_height
    pix_total = slot_total * area
    m_one = tiled(pix_total, narrow // 128)
    mean = get_rows(tot, 0, narrow // 128) / m_one
    inv_one = lax.rsqrt(get_rows(tot, 2, narrow // 128) / m_one - mean * mean + EPSILON)
    shift_one = mean * inv_one
    scale = inv_one * gain_one[...]
    offset = bias_one[...] - mean * scale
    scale_one, offset_one = scale, offset
    arrive(("halo", 0))
    patch(c1, up1, down1)

    def hide(at, carry):
        value = c1[block_at(at), :] * scale_one + offset_one
        value = swish(value) * mask(ext(at), narrow)
        hs[0, block_at(at), :] = pltpu.roll(value, 1, axis=0).astype(BF16)
        hs[1, block_at(at), :] = value.astype(BF16)
        hs[2, block_at(at), :] = pltpu.roll(value, block - 1, axis=0).astype(BF16)
        return carry

    lax.fori_loop(0, rows + 2, hide, 0)

    arrive(("move", 2))
    for q in range(rows // 2):
        for gr in range(2):
            lhs = jnp.concatenate(
                [
                    hs[bb, (a + 2 * q) * block : (a + 2 * q + 2) * block, gr * cg : (gr + 1) * cg]
                    for a in range(3)
                    for bb in range(3)
                ],
                axis=1,
            )
            c2[(1 + 2 * q) * block : (3 + 2 * q) * block, gr * half : (gr + 1) * half] = dot(
                lhs, w_split[:, gr * half : (gr + 1) * half]
            )
    m2[...] = jnp.zeros(m2.shape, F32)
    for j in range(2):
        lanes = pl.ds(j * half, half)

        def moments(r, carry):
            value = c2[block_at(r), lanes] * mask(own(r), half)
            return carry[0] + colsum(value), carry[1] + colsum(value * value)

        zero = jnp.zeros((1, half), F32)
        sums = lax.fori_loop(1, rows + 1, moments, (zero, zero))
        put_rows(m2, j * (half // 128), sums[0])
        put_rows(m2, split // 128 + j * (half // 128), sums[1])
    send_all(m2, s2, 1)
    set_edges(c2, first2, last2)
    halo_start(first2, last2, up2, down2, 1)
    arrive(("all", 8))
    mxb[...] = jnp.sum(sx[...], axis=0)
    exchange(mxb, sxb, 12, b, lambda t: (t, h))
    place_out()
    for bb in range(3):
        hs_t[bb] = hs[bb].T

    def slopes_one(r, carry):
        conv = c1[block_at(r + 1), :]
        live = mask(own(r + 1), narrow)
        slope1[block_at(r), :] = swish_slope(conv * scale_one + offset_one) * live
        n1[block_at(r), :] = ((conv * inv_one - shift_one) * live).astype(BF16)
        return carry

    lax.fori_loop(0, rows, slopes_one, 0)

    sum_all(s2, 1)
    m_two = tiled(pix_total, split // 128)
    mean = get_rows(tot, 0, split // 128) / m_two
    inv_two = lax.rsqrt(get_rows(tot, split // 128, split // 128) / m_two - mean * mean + EPSILON)
    shift_two = mean * inv_two
    scale_two = inv_two * gain_two[...]
    offset_two = bias_two[...] - mean * scale_two
    pool = jnp.zeros((slots, half), F32)
    for j in range(2):
        lanes = pl.ds(j * half, half)
        sc, of = scale_two[:, j * half : (j + 1) * half], offset_two[:, j * half : (j + 1) * half]

        def activate(r, acc):
            value = swish(c2[block_at(r), lanes] * sc + of) * mask(own(r), half)
            act[block_at(r - 1), lanes] = value
            return acc + value

        acc = lax.fori_loop(1, rows + 1, activate, jnp.zeros((block, half), F32))
        pool = pool + per_slot(acc, slots)
    pool = pool / area
    pooled[...] = pool
    arrive(("move", 4))
    m34[...] = dot(pool, w_squeeze[...], precision=HIGHEST)
    send_all(m34, s34, 2)
    exchange(pooled, pool_h, 13, h, lambda t: (b, t))
    arrive(("all", 12))
    tot[0:8, :] = jnp.sum(sxb[...], axis=0)
    x_mean = get_rows(tot, 0, width // 128) / tiled(pix_total, width // 128)

    def centre(r, carry):
        value = (x[block_at(r), :].astype(F32) - x_mean) * mask(own(r + 1), width)
        x_t[:, block_at(r)] = value.T.astype(BF16)
        return carry

    lax.fori_loop(0, rows, centre, 0)
    for q in range(2):
        at = slice(q * (width // 2), (q + 1) * (width // 2))
        bucket_n.full[at, :] = dot(x_t[at, :], n1[...]).astype(BF16)
    bucket_n.s0()
    arrive(("move", 5))
    arrive(("all", 2))

    def gather(i, carry):
        value = jnp.sum(s34[pl.ds(i * n_height, n_height)], axis=0)
        sq_all[i] = value
        return carry[0] + colsum(value), carry[1] + colsum(value * value)

    zero = jnp.zeros((1, inner), F32)
    sum_mid, square_mid = lax.fori_loop(0, n_batch, gather, (zero, zero))
    mean_mid = sum_mid / slot_total
    inv_mid = lax.rsqrt(square_mid / slot_total - mean_mid * mean_mid + EPSILON)
    norm_mid = (sq_all[b] - mean_mid) * inv_mid
    pre_mid = norm_mid * gain_mid[...] + bias_mid[...]
    middle = swish(pre_mid)
    logits = dot(middle, w_excite[...], precision=HIGHEST) + bias_excite[...]
    top = jnp.maximum(logits[:, :half], logits[:, half:])
    expo_one = jnp.exp(logits[:, :half] - top)
    expo_two = jnp.exp(logits[:, half:] - top)
    att_one = expo_one / (expo_one + expo_two)
    att_two = expo_two / (expo_one + expo_two)
    att[:, 0:half] = att_one
    att[:, half:split] = att_two
    for s in range(slots):
        attx[s * COLS : (s + 1) * COLS, :] = jnp.broadcast_to(att[s : s + 1, :], (COLS, split))

    def mix(r, carry):
        at = block_at(r)
        mixed[at, :] = (
            attx[:, 0:half] * act[at, 0:half] + attx[:, half:split] * act[at, half:split]
        ).astype(BF16)
        return carry

    lax.fori_loop(0, rows, mix, 0)
    arrive(("move", 6))
    for j in range(width // 256):
        lanes = pl.ds(j * 256, 256)
        sums = jnp.zeros((1, 256), F32)
        squares = jnp.zeros((1, 256), F32)
        for q in range(rows // 2):
            at = pl.ds(q * 2 * block, 2 * block)
            value = dot(mixed[at, :], w_expand[:, lanes])
            c3[at, lanes] = value
            sums = sums + colsum(value)
            squares = squares + colsum(value * value)
        put_rows(m5, j * 2, sums)
        put_rows(m5, width // 128 + j * 2, squares)
    send_pairs(m5, p5, s5, 3)
    mixed_t[...] = mixed[...].T
    bucket_n.s1()
    arrive(("all", 13))
    pool_sum[...] = jnp.sum(pool_h[...], axis=0)
    exchange(pool_sum, pool_b, 14, b, lambda t: (t, h))
    arrive(("halo", 1))
    patch(c2, up2, down2)
    for j in range(2):
        lanes = pl.ds(j * half, half)
        cut = slice(j * half, (j + 1) * half)
        sc, of = scale_two[:, cut], offset_two[:, cut]
        iv, sh = inv_two[:, cut], shift_two[:, cut]

        def slopes(at, carry):
            conv = c2[block_at(at), lanes]
            value = swish_slope(conv * sc + of) * mask(ext(at), half)
            slope2[block_at(at), lanes] = value
            value = value * own(at)
            more = value * (conv * iv - sh)
            slope2n[block_at(at), lanes] = more
            return carry[0] + value, carry[1] + more

        zero = jnp.zeros((block, half), F32)
        sums = lax.fori_loop(0, rows + 2, slopes, (zero, zero))
        st_src[0:slots, lanes] = per_slot(sums[0], slots)
        st_src[slots : 2 * slots, lanes] = per_slot(sums[1], slots)
    exchange(st_src, st_h, 10, h, lambda t: (b, t))

    sum_all(s5, 3)
    wide = width // 128
    m_three = tiled(pix_total, wide)
    mean = get_rows(tot, 0, wide) / m_three
    inv_three = lax.rsqrt(get_rows(tot, wide, wide) / m_three - mean * mean + EPSILON)
    shift_three = mean * inv_three
    scale_three = inv_three * gain_three[...]
    offset_three = bias_three[...] - mean * scale_three
    part = block // 2
    for j in range(width // 256):
        lanes = pl.ds(j * 256, 256)
        cut = slice(j * 256, (j + 1) * 256)
        sc, of = scale_three[:, cut], offset_three[:, cut]
        iv, sh = inv_three[:, cut], shift_three[:, cut]

        def finish_row(i, carry):
            r, k = i // 2, lax.rem(i, 2)
            at = pl.ds(pl.multiple_of(i * part, part), part)
            conv = c3[at, lanes]
            pre = conv * sc + of + x[at, lanes].astype(F32)
            sigma = sigmoid(pre)
            value = pre * sigma
            live = tiled(pix[pl.ds(pl.multiple_of(k * part, part), part), :] * own(r + 1), 2)
            xo[at, lanes] = (value * live).astype(BF16)
            slope = sigma + value * (1.0 - sigma)
            grad = g[at, lanes].astype(F32) * slope
            d3[at, lanes] = grad
            return carry[0] + colsum(grad), carry[1] + colsum(grad * (conv * iv - sh))

        zero = jnp.zeros((1, 256), F32)
        sums = lax.fori_loop(0, 2 * rows, finish_row, (zero, zero))
        put_rows(p6, j * 2, sums[0])
        put_rows(p6, wide + j * 2, sums[1])
    m6[...] = p6[...].astype(BF16)
    send_all(m6, s6, 4)
    pad_out(xo, out4)
    move(7, out4, output)
    bucket_n.s2()
    arrive(("all", 10))
    st_sum[...] = jnp.sum(st_h[...], axis=0)
    st_low[...] = st_sum[...].astype(BF16)
    exchange(st_low, st_b, 11, b, lambda t: (t, h))

    sum_all(s6, 4)
    gb_three = get_rows(tot, 0, wide)
    gg_three = get_rows(tot, wide, wide)
    vectors[0:1, :] = gb_three
    vectors[1:2, :] = gg_three
    gg = gg_three / m_three
    k_one = scale_three
    k_three = k_one * inv_three * gg
    k_two = k_one * (gb_three / m_three - shift_three * gg)
    for j in range(width // 256):
        lanes = pl.ds(j * 256, 256)
        cut = slice(j * 256, (j + 1) * 256)
        ka, kb, kc = k_one[:, cut], k_two[:, cut], k_three[:, cut]

        def back_three(i, carry):
            at = pl.ds(pl.multiple_of(i * part, part), part)
            gc3[at, lanes] = (d3[at, lanes] * ka - kb - c3[at, lanes] * kc).astype(BF16)
            return carry

        lax.fori_loop(0, 2 * rows, back_three, 0)
    for q in range(rows // 2):
        gm[pl.ds((1 + 2 * q) * block, 2 * block), :] = dot(
            gc3[pl.ds(2 * q * block, 2 * block), :], w_expand[...], NT
        )
    att_sums = [[], [], []]
    for j in range(2):
        lanes = pl.ds(j * half, half)
        parts = [[], [], []]
        for k in range(2):
            zero = jnp.zeros((part, half), F32)

            def attend(r, acc):
                at = pl.ds(pl.multiple_of(r * block + k * part, part), part)
                up_at = pl.ds(pl.multiple_of((r + 1) * block + k * part, part), part)
                value = gm[up_at, :]
                return (
                    acc[0] + value * act[at, lanes],
                    acc[1] + value * own(r + 1) * slope2[up_at, lanes],
                    acc[2] + value * slope2n[up_at, lanes],
                )

            acc = lax.fori_loop(0, rows, attend, (zero, zero, zero))
            for i in range(3):
                parts[i].append(per_slot(acc[i], slots // 2))
        for i in range(3):
            att_sums[i].append(jnp.concatenate(parts[i], axis=0))
    grad_att = att_sums[0]
    blend = att_one * grad_att[0] + att_two * grad_att[1]
    grad_logits = jnp.concatenate(
        [att_one * (grad_att[0] - blend), att_two * (grad_att[1] - blend)], axis=1
    )
    em_part = dot(grad_logits, w_excite[...], NT, HIGHEST) * swish_slope(pre_mid)
    em_src[...] = em_part
    mid_scale = inv_mid * gain_mid[...] / area
    pooled_part = dot(em_part * mid_scale, w_squeeze[...], NT, HIGHEST)
    for j in range(2):
        lanes = pl.ds(j * half, half)
        weight = att_one if j == 0 else att_two
        for i in range(2):
            sums = weight * att_sums[1 + i][j] + pooled_part * st_sum[i * slots : (i + 1) * slots, lanes]
            put_rows(m78, (i * 2 + j) * (half // 128), colsum(sums))
    put_rows(m78, 2 * split // 128, colsum(em_part))
    put_rows(m78, 2 * split // 128 + 1, colsum(em_part * norm_mid))
    send_all(m78, s78, 5)
    exchange(em_src, em_all, 9, h, lambda t: (b, t))
    set_edges(gm, first3, last3)
    halo_start(first3, last3, up3, down3, 2)
    for j in range(width // 256):
        bucket_e.full[j * narrow : (j + 1) * narrow, :] = dot(
            mixed_t[...], gc3[:, j * 256 : (j + 1) * 256]
        ).astype(BF16)
    bucket_e.s0()
    grad_excite = dot(middle, grad_logits, TN, HIGHEST)
    for gr in range(2):
        put_taps(18 * cg + gr * inner, grad_excite[:, gr * half : (gr + 1) * half])
    bias_part = colsum(grad_logits)
    put_rows(m10, 2 * (narrow // 128), bias_part)
    bucket_e.s1()
    arrive(("all", 11))
    every = n_batch * slots
    mid_all = ((sq_all[...] - mean_mid) * inv_mid).reshape(every, inner)
    st_all = st_b[...].astype(F32)
    w_turned = tiled(w_squeeze[...].T, 2)
    for i in range(2):
        sums = st_all[:, i * slots : (i + 1) * slots, :].reshape(every, split)
        wns[:, i * split : (i + 1) * split] = w_turned * dot(mid_all, sums, TN, HIGHEST)
        st_tot[i : i + 1, :] = colsum(sums)

    sum_all(s78, 5)
    rows_mid = 2 * split // 128
    gb_mid, gg_mid = tot[rows_mid : rows_mid + 1, :], tot[rows_mid + 1 : rows_mid + 2, :]
    vectors[4:5, 0:128] = gb_mid
    vectors[4:5, 128:256] = gg_mid
    mid_k = mid_scale / slot_total
    pooled_all = dot(jnp.broadcast_to(mid_k * gb_mid, (8, inner)), w_squeeze[...], NT, HIGHEST)[0:1]
    turned = dot(jnp.broadcast_to(mid_k * gg_mid, (8, inner)), wns[...], precision=HIGHEST)[0:1]
    pooled_all = tiled(pooled_all, 2)
    gb_two = get_rows(tot, 0, split // 128) - pooled_all * st_tot[0:1, :] - turned[:, :split]
    gg_two = get_rows(tot, split // 128, split // 128) - pooled_all * st_tot[1:2, :] - turned[:, split:]
    vectors[2:3, 0:split] = gb_two
    vectors[2:3, split : 2 * split] = gg_two
    arrive(("all", 9))
    em = jnp.sum(em_all[...], axis=0)
    em_sum[...] = em
    slot_live = jnp.where(lax.broadcasted_iota(jnp.int32, (slots, inner), 0) < count, 1.0, 0.0)
    grad_sq = (
        slot_live * inv_mid * gain_mid[...]
        * (em - gb_mid / slot_total - norm_mid * gg_mid / slot_total)
    )
    grad_pooled = dot(grad_sq, w_squeeze[...], NT, HIGHEST) / area
    att[:, 0:half] = grad_pooled
    for s in range(slots):
        gpx[s * COLS : (s + 1) * COLS, :] = jnp.broadcast_to(att[s : s + 1, 0:half], (COLS, half))
    arrive(("halo", 2))
    patch(gm, up3, down3)
    gg = gg_two / m_two
    k_one = scale_two
    k_three = k_one * inv_two * gg
    k_two = k_one * (gb_two / m_two - shift_two * gg)
    for j in range(2):
        lanes = pl.ds(j * half, half)
        cut = slice(j * half, (j + 1) * half)
        ka, kb, kc = k_one[:, cut], k_two[:, cut], k_three[:, cut]

        def back_two(at, carry):
            value = (attx[:, lanes] * gm[block_at(at), :] + gpx[...]) * slope2[block_at(at), lanes]
            value = value * ka - kb - c2[block_at(at), lanes] * kc
            gc2[block_at(at), lanes] = (value * mask(ext(at), half)).astype(BF16)
            return carry

        lax.fori_loop(0, rows + 2, back_two, 0)
    gc2_own[...] = (gc2[block_at(rows), :].astype(F32) * own(rows)).astype(BF16)

    def taps_grad(k):
        gr, bb = k // 3, k % 3
        lhs = jnp.concatenate(
            [hs_t[bb, gr * cg : (gr + 1) * cg, a * block : a * block + pixels] for a in range(3)], axis=0
        )
        lanes = slice(gr * half, (gr + 1) * half)
        rhs = jnp.concatenate([gc2[block:pixels, lanes], gc2_own[:, lanes]], axis=0)
        put_taps(k * 3 * cg, dot(lhs, rhs))

    begun = []
    for k in range(6):
        taps_grad(k)
        ready = 0
        for bucket in taps_buckets[:2]:
            ready += bucket.full.shape[0]
            if ready <= (k + 1) * 3 * cg and bucket not in begun:
                begun.append(bucket)
                bucket.s0()
    bucket_e.s2()
    exchange(em_sum, em_b, 15, b, lambda t: (t, h))
    for gr in range(2):
        outs = []
        for bb in range(3):
            lhs = jnp.concatenate(
                [gc2[(2 - a) * block : (2 - a) * block + pixels, gr * half : (gr + 1) * half] for a in range(3)],
                axis=1,
            )
            rhs = jnp.concatenate(
                [
                    w_split[(a * 3 + bb) * cg : (a * 3 + bb + 1) * cg, gr * half : (gr + 1) * half]
                    for a in range(3)
                ],
                axis=1,
            )
            outs.append(dot(lhs, rhs, NT))
        gh[:, gr * cg : (gr + 1) * cg] = (
            outs[1] + pltpu.roll(outs[2], 1, axis=0) + pltpu.roll(outs[0], pixels - 1, axis=0)
        )

    bucket_a.s1()
    bucket_b.s1()

    def back_hidden(r, carry):
        value = gh[block_at(r), :] * slope1[block_at(r), :]
        gh[block_at(r), :] = value
        d1[block_at(r), :] = value.astype(BF16)
        norm = c1[block_at(r + 1), :] * inv_one - shift_one
        return carry[0] + colsum(value), carry[1] + colsum(value * norm)

    zero = jnp.zeros((1, narrow), F32)
    sums = lax.fori_loop(0, rows, back_hidden, (zero, zero))
    put_rows(m10, 0, sums[0])
    put_rows(m10, narrow // 128, sums[1])
    send_all(m10, s10, 7)
    for q in range(2):
        at = slice(q * (width // 2), (q + 1) * (width // 2))
        bucket_r.full[at, :] = dot(x_t[at, :], d1[...]).astype(BF16)
    bucket_r.s0()
    bucket_c.s0()
    bucket_r.s1()
    bucket_a.s2()
    bucket_e.s3()
    bucket_c.s1()
    bucket_b.s2()
    kept_n = bucket_n.collect()
    sum_all(s10, 7)
    gb_one = get_rows(tot, 0, narrow // 128)
    gg_one = get_rows(tot, narrow // 128, narrow // 128)
    vectors[3:4, 0:narrow] = gb_one
    vectors[3:4, narrow : 2 * narrow] = gg_one
    vectors[3:4, 2 * narrow : 2 * narrow + split] = get_rows(tot, 2 * (narrow // 128), split // 128)
    move(6, vectors, vectors_out)
    gg = gg_one / m_one
    k_one = scale_one
    k_three = k_one * inv_one * gg
    k_two = k_one * (gb_one / m_one - shift_one * gg)

    def back_one(r, carry):
        value = gh[block_at(r), :] * k_one - k_two - c1[block_at(r + 1), :] * k_three
        gc1[block_at(r), :] = (value * mask(own(r + 1), narrow)).astype(BF16)
        return carry

    lax.fori_loop(0, rows, back_one, 0)
    bucket_r.final = lambda value: scale_one * (value - kept_n * gg)
    arrive(("all", 14))
    arrive(("all", 15))
    sq_grads = (inv_mid * gain_mid[...]) * (
        em_b[...].reshape(every, inner) - gb_mid / slot_total - mid_all * gg_mid / slot_total
    )
    squeeze_grad[...] = dot(pool_b[...].reshape(every, half), sq_grads, TN, HIGHEST)
    move(3, squeeze_grad, big_q)
    arrive(("move", 7))

    def back_image(r, carry):
        value = d3[block_at(r), :] + dot(gc1[block_at(r), :], w_reduce[...], NT)
        xo[block_at(r), :] = value.astype(BF16)
        return carry

    lax.fori_loop(0, rows, back_image, 0)
    bucket_a.s3()
    bucket_r.s2()
    bucket_e.s4()
    bucket_c.s2()
    pad_out(xo, out4)
    move(7, out4, grad_images)
    bucket_b.s3()
    bucket_a.s4()
    bucket_r.s3()
    bucket_c.s3()
    bucket_e.s5()
    bucket_b.s4()
    bucket_e.s6()
    move(0, bucket_e.done, big_e)
    bucket_a.s5()
    bucket_r.s4()
    bucket_c.s4()
    bucket_a.s6()
    move(1, bucket_a.done, big_a)
    bucket_b.s5()
    bucket_b.s6()
    move(4, bucket_b.done, big_b)
    bucket_r.s5()
    bucket_c.s5()
    bucket_r.s6()
    move(2, bucket_r.done, big_r)
    bucket_c.s6()
    move(5, bucket_c.done, big_c)

    for wait in sends:
        wait()
    for key in list(due):
        arrive(key)


def unpack_kernel(
    out_a, gimg_a, big_e, big_a, big_b, big_c, big_r, big_q, vectors,
    output, grad_images, grad_reduce, grad_split, grad_squeeze, grad_excite, grad_expand,
    grad_gain_one, grad_bias_one, grad_gain_two, grad_bias_two,
    grad_gain_mid, grad_bias_mid, grad_bias_excite, grad_gain_three, grad_bias_three,
    in_e, in_a, in_b, in_c, in_r, in_v, in_o, in_g, in_q, out_e, out_s, out_x, out_r, sems,
):
    def move(k, src, dst):
        copy = pltpu.make_async_copy(src, dst, sems.at[k])
        copy.start()
        return copy

    ins = [move(k, src, dst) for k, (src, dst) in enumerate([
        (out_a, in_o), (big_e, in_e), (gimg_a, in_g), (big_r, in_r), (big_a, in_a), (big_b, in_b), (big_c, in_c),
        (big_q, in_q), (vectors, in_v),
    ])]
    narrow = grad_expand.shape[0]
    taps, split = grad_split.shape
    half = split // 2
    inner = grad_excite.shape[0]
    outs = []
    ins[0].wait()
    outs.append(move(9, in_o, output))
    ins[1].wait()
    for j in range(grad_expand.shape[1] // 256):
        out_e[:, j * 256 : (j + 1) * 256] = in_e[j * narrow : (j + 1) * narrow, :].astype(F32)
    outs.append(move(10, out_e, grad_expand))
    ins[2].wait()
    outs.append(move(11, in_g, grad_images))
    ins[3].wait()
    out_r[...] = in_r[...].astype(F32)
    outs.append(move(12, out_r, grad_reduce))
    for k in range(4, 7):
        ins[k].wait()

    def put(at, dst, to, lanes, size):
        start = 0
        for ref in (in_a, in_b, in_c):
            low, high = max(at, start), min(at + size, start + ref.shape[0])
            if low < high:
                dst[to + low - at : to + high - at, lanes] = ref[low - start : high - start, :].astype(F32)
            start += ref.shape[0]

    cg = taps // 9
    for k in range(18):
        gr, bb, a = k // 9, k // 3 % 3, k % 3
        put(k * cg, out_s, (a * 3 + bb) * cg, slice(gr * half, (gr + 1) * half), cg)
    outs.append(move(13, out_s, grad_split))
    for gr in range(2):
        put(18 * cg + gr * inner, out_x, 0, slice(gr * half, (gr + 1) * half), inner)
    outs.append(move(14, out_x, grad_excite))
    ins[7].wait()
    outs.append(move(15, in_q, grad_squeeze))
    ins[8].wait()
    for dst, line, at in [
        (grad_bias_three, 0, 0), (grad_gain_three, 1, 0), (grad_bias_two, 2, 0), (grad_gain_two, 2, split),
        (grad_bias_one, 3, 0), (grad_gain_one, 3, narrow), (grad_bias_excite, 3, 2 * narrow),
        (grad_bias_mid, 4, 0), (grad_gain_mid, 4, inner),
    ]:
        dst[...] = in_v[line : line + 1, at : at + dst.shape[1]]
    for copy in outs:
        copy.wait()


def shards(
    n_batch, n_height,
    images, counts, row_valid, w_reduce, gain_one, bias_one, w_split, gain_two, bias_two, w_squeeze,
    gain_mid, bias_mid, w_excite, bias_excite, w_expand, gain_three, bias_three, cotangent,
):
    slots, rows, cols, width = images.shape
    count = slots * rows * cols
    narrow = w_reduce.shape[1]
    split = w_split.shape[3]
    taps = 9 * w_split.shape[2]
    inner = w_squeeze.shape[1]
    half = split // 2
    total = n_batch * n_height
    block = slots * COLS
    pixels = rows * block
    padded = pixels + 2 * block
    n_groups = n_batch // GROUP

    def row(v):
        return v.reshape(1, -1)

    unit = 4 * GROUP * 16
    size_e = width // 256 * narrow
    size_r = width
    taps_rows = 2 * taps + 2 * inner
    size_a = -(-taps_rows // (5 * unit)) * 2 * unit
    size_c = taps_rows - 2 * size_a

    def bucket(size, lanes=256, kind=BF16):
        kept = size // 2
        shapes = [
            (size, lanes), (kept, lanes), (kept, lanes), (3, kept // 4, lanes), (kept // 4, lanes),
            (3, kept // 16, lanes), (n_groups, kept // 16, lanes), (kept // 16, lanes), (size, lanes),
        ]
        return [pltpu.VMEM(dims, kind) for dims in shapes]

    messages = [(3, 2, 128), (8, 128), (8, 128), (16, 128), (16, 128), (5, 2, 128), (8, 128), (8, 128), (8, 128)]
    kinds = [BF16 if k == 4 else F32 for k in range(len(messages))]
    vm = pltpu.VMEM
    scratch = (
        [vm((1, k), F32) for k in (narrow, narrow, split, split, inner, inner, split, width, width)]
        + [vm((slots * cols, rows, width), BF16)] * 3
        + [vm((width, narrow), BF16), vm((taps, split), BF16), vm((narrow, inner), F32), vm((inner, split), F32),
           vm((narrow, width), BF16)]
        + [vm((pixels, width), BF16), vm((pixels, width), BF16), vm((block, 128), F32), vm((pixels, count), BF16),
           vm((count, pixels), BF16)]
        + [vm((padded, narrow), F32), vm((3, padded, narrow), BF16), vm((padded, split), F32), vm((pixels, split), F32),
           vm((padded, split), F32), vm((pixels, half), BF16), vm((pixels, width), F32), vm((pixels, width), F32),
           vm((pixels, width), BF16), vm((pixels, width), BF16), vm((padded, half), F32),
           vm((padded, split), F32), vm((padded, split), BF16), vm((pixels, narrow), F32), vm((pixels, narrow), F32),
           vm((pixels, narrow), BF16), vm((block, split), BF16), vm((pixels, narrow), BF16), vm((pixels, narrow), BF16)]
        + [vm((2 * slots, split), F32), vm((n_height, 2 * slots, split), F32), vm((2 * slots, split), F32),
           vm((2 * slots, split), BF16), vm((n_batch, 2 * slots, split), BF16), vm((inner, 2 * split), F32),
           vm((8, split), F32)]
        + [vm((width, pixels), BF16), vm((half, pixels), BF16), vm((3, narrow, padded), BF16), vm((slots, split), F32),
           vm((block, split), F32), vm((block, half), F32), vm((slots, half), F32), vm((n_batch, slots, inner), F32),
           vm((16, 128), F32)]
        + [vm(dims, kinds[k]) for k, dims in enumerate(messages)] + [vm((16, 128), F32)] * 2 + [vm((8, width), F32)]
        + [vm((n_height, slots, half), F32), vm((slots, half), F32), vm((n_batch, slots, half), F32), vm((slots, inner), F32),
           vm((n_batch, slots, inner), F32), vm((narrow, inner), F32), vm((slots, inner), F32)]
        + [vm((total // 2 if k == 3 else total,) + dims, kinds[k]) for k, dims in enumerate(messages[:-2])]
        + [vm((n_height,) + messages[-1], F32), vm((n_batch,) + messages[-1], F32)] + [vm((n_height, slots, inner), F32)]
        + [vm((block, narrow), F32)] * 4 + [vm((block, split), BF16)] * 4 + [vm((block, half), BF16)] * 4
        + [pltpu.SMEM((1,), jnp.int32), pltpu.SMEM((rows,), jnp.int32)]
        + [pltpu.SemaphoreType.DMA((k,)) for k in (19, 16, 16, 8, 8, 6, 6, 48, 48)]
        + bucket(size_e) + bucket(size_r) * 2 + bucket(size_a) * 2 + bucket(size_c)
    )
    vmem = pl.BlockSpec(memory_space=pltpu.VMEM)
    hbm = pl.BlockSpec(memory_space=pltpu.HBM)
    shape = jax.ShapeDtypeStruct
    flat = (slots * cols, rows, width)

    def by_column(value):
        return value.transpose(0, 2, 1, 3).reshape(flat)

    def by_row(value):
        return value.reshape(slots, cols, rows, width).transpose(0, 2, 1, 3)

    out_a, gimg_a, big_e, big_a, big_b, big_c, big_r, big_q, vectors = pl.pallas_call(
        functools.partial(main_kernel, n_batch, n_height, (slots, cols, rows, width)),
        out_shape=(
            shape(flat, BF16), shape(flat, BF16), shape((size_e, 256), BF16),
            shape((size_a, 256), BF16), shape((size_a, 256), BF16), shape((size_c, 256), BF16), shape((size_r, 256), BF16),
            shape((narrow, inner), F32),
            shape((8, width), F32),
        ),
        in_specs=[hbm] * 18,
        out_specs=[hbm] * 9,
        scratch_shapes=scratch,
        compiler_params=pltpu.CompilerParams(
            collective_id=0, has_side_effects=True, vmem_limit_bytes=58 * 1024 * 1024
        ),
    )(
        counts, row_valid, row(gain_one), row(bias_one), row(gain_two), row(bias_two), row(gain_mid), row(bias_mid),
        row(bias_excite), row(gain_three), row(bias_three),
        by_column(images), by_column(cotangent), w_reduce, w_split.reshape(taps, split), w_squeeze, w_excite, w_expand,
    )
    (
        output, grad_images, grad_reduce, grad_split, grad_squeeze, grad_excite, grad_expand,
        grad_gain_one, grad_bias_one, grad_gain_two, grad_bias_two,
        grad_gain_mid, grad_bias_mid, grad_bias_excite, grad_gain_three, grad_bias_three,
    ) = pl.pallas_call(
        unpack_kernel,
        out_shape=(
            shape(flat, BF16), shape(flat, BF16), shape((width, narrow), F32), shape((taps, split), F32),
            shape((narrow, inner), F32), shape((inner, split), F32), shape((narrow, width), F32),
            shape((1, narrow), F32), shape((1, narrow), F32), shape((1, split), F32), shape((1, split), F32),
            shape((1, inner), F32), shape((1, inner), F32), shape((1, split), F32), shape((1, width), F32),
            shape((1, width), F32),
        ),
        in_specs=[hbm] * 9,
        out_specs=[hbm] * 7 + [vmem] * 9,
        scratch_shapes=[
            vm((size_e, 256), BF16), vm((size_a, 256), BF16), vm((size_a, 256), BF16), vm((size_c, 256), BF16), vm((size_r, 256), BF16),
            vm((8, width), F32),
            vm(flat, BF16), vm(flat, BF16), vm((narrow, inner), F32),
            vm((narrow, width), F32), vm((taps, split), F32), vm((inner, split), F32), vm((width, narrow), F32),
            pltpu.SemaphoreType.DMA((16,)),
        ],
        compiler_params=pltpu.CompilerParams(vmem_limit_bytes=60 * 1024 * 1024),
    )(out_a, gimg_a, big_e, big_a, big_b, big_c, big_r, big_q, vectors)

    def like(value, other):
        return value.reshape(other.shape)

    return (
        by_row(output), by_row(grad_images), grad_reduce, like(grad_gain_one, gain_one), like(grad_bias_one, bias_one),
        like(grad_split, w_split), like(grad_gain_two, gain_two), like(grad_bias_two, bias_two), grad_squeeze,
        like(grad_gain_mid, gain_mid), like(grad_bias_mid, bias_mid), grad_excite, like(grad_bias_excite, bias_excite),
        grad_expand, like(grad_gain_three, gain_three), like(grad_bias_three, bias_three),
    )


def solution(mesh):
    axes = mesh.shape
    split_in = P("batch", "height", None, None)
    return jax.shard_map(
        functools.partial(shards, axes["batch"], axes["height"]),
        mesh=mesh,
        in_specs=(split_in, P("batch"), P("height")) + (P(),) * 14 + (split_in,),
        out_specs=(split_in, split_in) + (P(),) * 14,
        check_vma=False,
    )
```

```python
import functools

import jax
import jax.numpy as jnp
from jax import lax
from jax.experimental import pallas as pl
from jax.experimental.pallas import tpu as pltpu
from jax.sharding import PartitionSpec as P

IMG_H = 14
IMG_W = 14
EPSILON = 1e-05
MESH = pl.DeviceIdType.MESH
F32 = jnp.float32
BF16 = jnp.bfloat16
HIGHEST = lax.Precision.HIGHEST
COLS = 16
GROUP = 8
NN = (((1,), (0,)), ((), ()))
NT = (((1,), (1,)), ((), ()))
TN = (((0,), (0,)), ((), ()))


def dot(lhs, rhs, dims=NN, precision=None):
    return lax.dot_general(lhs, rhs, dims, precision=precision, preferred_element_type=F32)


def sigmoid(values):
    return 0.5 * jnp.tanh(0.5 * values) + 0.5


def swish(values):
    return values * sigmoid(values)


def swish_slope(values):
    sigma = sigmoid(values)
    return sigma + values * sigma * (1.0 - sigma)


def tiled(row, times):
    return jnp.concatenate([row] * times, axis=1) if times > 1 else row


def colsum(values):
    return jnp.sum(values, axis=0, keepdims=True)


def put_rows(ref, at, row):
    for k in range(row.shape[1] // 128):
        piece = row[:, k * 128 : (k + 1) * 128]
        if len(ref.shape) == 3:
            ref[(at + k) // 2, (at + k) % 2 : (at + k) % 2 + 1, :] = piece
        else:
            ref[at + k : at + k + 1, :] = piece


def get_rows(ref, at, count):
    return jnp.concatenate([ref[at + k : at + k + 1, :] for k in range(count)], axis=1)


def per_slot(values, slots):
    return jnp.sum(values.reshape(slots, COLS, values.shape[1]), axis=1)


def main_kernel(n_batch, n_height, sizes, *refs):
    (
        counts_in, row_valid_in, *refs,
    ) = refs
    small_in, refs = refs[:9], refs[9:]
    (
        images, cotangent, w_reduce_in, w_split_in, w_squeeze_in, w_excite_in, w_expand_in,
        output, grad_images, big_e, big_a, big_b, big_c, big_r, big_q, vectors_out,
        gain_one, bias_one, gain_two, bias_two, gain_mid, bias_mid, bias_excite, gain_three, bias_three,
        img4, cot4, out4, w_reduce, w_split, w_squeeze, w_excite, w_expand,
        x, g, pix, to_pad, from_pad, c1, hs, c2, act, slope2, mixed, c3, d3, xo, gc3, gm, slope2n, gc2, gh, slope1, gc1,
        gc2_own, n1, d1, st_src, st_h, st_sum, st_low, st_b, wns, st_tot, x_t, mixed_t, hs_t, att, attx, gpx, pooled, sq_all, tot,
        m1, m2, m34, m5, m6, m78, m10, mx, mxb, p5, p6, vectors, pool_h, pool_sum, pool_b, em_sum, em_b, squeeze_grad, em_src,
        s1, s2, s34, s5, s6, s78, s10, sx, sxb, em_all,
        first1, last1, up1, down1, first2, last2, up2, down2, first3, last3, up3, down3,
        counts, row_valid, local_sem, all_send, all_recv, pair_send, pair_recv, halo_send, halo_recv, red_send, red_recv,
        *bucket_refs,
    ) = refs
    slots, cols, rows, width = sizes
    narrow = w_reduce.shape[1]
    split = w_split.shape[1]
    half = split // 2
    cg = w_split.shape[0] // 9
    inner = w_squeeze.shape[1]
    block = slots * COLS
    pixels = rows * block
    total = n_batch * n_height
    area = float(IMG_H * IMG_W)
    b = lax.axis_index("batch")
    h = lax.axis_index("height")
    me = b * n_height + h

    sends = []
    due = {}

    def arrive(key):
        due.pop(key)()

    def move(key, src, dst):
        copy = pltpu.make_async_copy(src, dst, local_sem.at[key])
        copy.start()
        due["move", key] = copy.wait

    move(17, counts_in, counts)
    move(18, row_valid_in, row_valid)
    move(0, images, img4)
    move(1, w_reduce_in, w_reduce)
    barrier = pltpu.get_barrier_semaphore()

    def greet(j, carry):
        t = lax.rem(me + j, total)
        pl.semaphore_signal(
            barrier, inc=1, device_id=(t // n_height, lax.rem(t, n_height)), device_id_type=MESH
        )
        return carry

    lax.fori_loop(1, total, greet, 0)
    small = (gain_one, bias_one, gain_two, bias_two, gain_mid, bias_mid, bias_excite, gain_three, bias_three)
    for k, (src, dst) in enumerate(zip(small_in, small)):
        move(8 + k, src, dst)
    move(2, w_split_in, w_split)
    move(3, cotangent, cot4)
    move(4, w_squeeze_in, w_squeeze)
    move(5, w_excite_in, w_excite)
    move(6, w_expand_in, w_expand)


    kh, kq = lax.rem(h, 2), h // 2
    pair_one = (b, h + 1 - 2 * kh)
    pair_two = (b, h + 2 - 4 * kq)

    def circle(dst):
        if dst.shape[0] == total:
            return me, lambda t: (t // n_height, lax.rem(t, n_height))
        pairs = n_height // 2
        return b * pairs + kq, lambda t: (t // pairs, 2 * lax.rem(t, pairs) + kh)

    def send_all(src, dst, k):
        exchange(src, dst, k, *circle(dst))

    def exchange(src, dst, k, here, device):
        others = dst.shape[0]

        def one(j, carry):
            t = jnp.where(2 * here < others, others - 1 - j, j)

            @pl.when(t != here)
            def _():
                pltpu.make_async_remote_copy(
                    src_ref=src, dst_ref=dst.at[here], send_sem=all_send.at[k], recv_sem=all_recv.at[k],
                    device_id=device(t), device_id_type=MESH,
                ).start()

            return carry

        lax.fori_loop(0, others, one, 0)
        dst[here] = src[...]
        sends.append(lambda: all_copy(dst, k).wait_send())
        due["all", k] = lambda: all_copy(dst, k).wait_recv()

    def all_copy(dst, k):
        many = dst.at[pl.ds(0, dst.shape[0] - 1)]
        return pltpu.make_async_remote_copy(
            src_ref=many, dst_ref=many,
            send_sem=all_send.at[k], recv_sem=all_recv.at[k], device_id=(b, h), device_id_type=MESH,
        )

    def send_pairs(src, arrived, dst, k):
        copy = pltpu.make_async_remote_copy(
            src_ref=src, dst_ref=arrived, send_sem=pair_send.at[k], recv_sem=pair_recv.at[k],
            device_id=pair_one, device_id_type=MESH,
        )
        copy.start()
        copy.wait()
        src[...] = src[...] + arrived[...]
        send_all(src, dst, k)

    def sum_all(dst, k):
        arrive(("all", k))

        def one(i, acc):
            return acc + jnp.sum(dst[pl.ds(i * 8, 8)].astype(F32), axis=0)

        acc = lax.fori_loop(0, dst.shape[0] // 8, one, jnp.zeros(dst.shape[1:], F32))
        if len(dst.shape) == 4:
            for i in range(dst.shape[1]):
                tot[2 * i : 2 * i + 2, :] = acc[i]
        else:
            tot[0 : dst.shape[1], :] = acc

    def halo_copies(first, last, up, down, k):
        above = pltpu.make_async_remote_copy(
            src_ref=last, dst_ref=up, send_sem=halo_send.at[2 * k], recv_sem=halo_recv.at[2 * k],
            device_id=(b, lax.rem(h + 1, n_height)), device_id_type=MESH,
        )
        below = pltpu.make_async_remote_copy(
            src_ref=first, dst_ref=down, send_sem=halo_send.at[2 * k + 1],
            recv_sem=halo_recv.at[2 * k + 1],
            device_id=(b, lax.rem(h + n_height - 1, n_height)), device_id_type=MESH,
        )
        return above, below

    def halo_start(first, last, up, down, k):
        above, below = halo_copies(first, last, up, down, k)

        @pl.when(h < n_height - 1)
        def _():
            above.start()

        @pl.when(h > 0)
        def _():
            below.start()

        sends.append(lambda: halo_sent(first, last, up, down, k))
        due["halo", k] = lambda: halo_here(first, last, up, down, k)

        @pl.when(h == 0)
        def _():
            up[...] = jnp.zeros(up.shape, up.dtype)

        @pl.when(h == n_height - 1)
        def _():
            down[...] = jnp.zeros(down.shape, down.dtype)

    def halo_here(first, last, up, down, k):
        above, below = halo_copies(first, last, up, down, k)

        @pl.when(h > 0)
        def _():
            above.wait_recv()

        @pl.when(h < n_height - 1)
        def _():
            below.wait_recv()

    def halo_sent(first, last, up, down, k):
        above, below = halo_copies(first, last, up, down, k)

        @pl.when(h < n_height - 1)
        def _():
            above.wait_send()

        @pl.when(h > 0)
        def _():
            below.wait_send()

    arrive(("move", 17))
    arrive(("move", 18))
    count = counts[0]
    filled = row_valid[0]
    for r in range(1, rows):
        filled = filled + row_valid[r]

    def flag(cond):
        return jnp.where(cond, 1.0, 0.0).astype(F32)

    def own(at):
        return flag((at >= 1) & (at <= filled))

    def ext(at):
        return flag(
            ((at >= 1) & (at <= filled))
            | ((at == 0) & (h > 0))
            | ((at == filled + 1) & (h < n_height - 1))
        )

    def mask(scale, lanes, start=0, size=block):
        return tiled(pix[start : start + size, :] * scale, lanes // 128)

    def block_at(at):
        return pl.ds(at * block if isinstance(at, int) else pl.multiple_of(at * block, block), block)

    def set_edges(src, first, last):
        first[...] = src[block_at(1), :].astype(first.dtype)
        value = jnp.zeros(last.shape, F32)
        for r in range(IMG_H // n_height - 1, rows):
            value = value + src[block_at(r + 1), :] * flag(filled == r + 1)
        last[...] = value.astype(last.dtype)

    def patch(ref, up, down):
        below = down[...].astype(F32)
        ref[block_at(0), :] = up[...].astype(F32)
        ref[block_at(rows + 1), :] = below
        whole = flag(filled == rows)
        ref[block_at(rows), :] = ref[block_at(rows), :] * whole + below * (1.0 - whole)

    iota = lax.broadcasted_iota(jnp.int32, (block, 128), 0)
    pix[...] = jnp.where(((iota >> 4) < count) & ((iota & 15) < cols), 1.0, 0.0)

    def places(shape, dim):
        at = lax.broadcasted_iota(jnp.int32, shape, dim)
        r, s, c = at // block, (at >> 4) & (slots - 1), at & 15
        return r, s, c, (s * cols + c) * rows + r

    def place_in():
        shape = (pixels, slots * cols * rows)
        r, s, c, at = places(shape, 0)
        live = (c < cols) & (s < count) & (r < filled)
        other = lax.broadcasted_iota(jnp.int32, shape, 1)
        to_pad[...] = jnp.where((other == at) & live, 1.0, 0.0).astype(BF16)

    def place_out():
        shape = (slots * cols * rows, pixels)
        r, s, c, at = places(shape, 1)
        other = lax.broadcasted_iota(jnp.int32, shape, 0)
        from_pad[...] = jnp.where((other == at) & (c < cols), 1.0, 0.0).astype(BF16)

    def pad_in(src, dst):
        value = src[...].reshape(slots * cols * rows, width)
        for q in range(rows):
            at = slice(q * block, (q + 1) * block)
            dst[at, :] = dot(to_pad[at, :], value).astype(BF16)

    def pad_out(src, dst):
        for j in range(width // 256):
            lanes = slice(j * 256, (j + 1) * 256)
            value = dot(from_pad[...], src[:, lanes]).astype(BF16)
            dst[:, :, lanes] = value.reshape(slots * cols, rows, 256)

    bx, bz = lax.rem(b, 2), lax.rem(b // 2, 4)
    group, n_groups = b // GROUP, n_batch // GROUP
    plane = 2 * kq + bx
    bucket_refs = iter(bucket_refs)

    def in_plane(t):
        return (b - bx + lax.rem(t, 2), 2 * (t // 2) + kh)

    def in_line(t):
        return (b + 2 * (t - bz), h)

    class Bucket:
        def __init__(self, at):
            self.full, self.in0, self.half, self.in1, self.sum1, self.in2, self.in3, self.shard, self.done = (
                next(bucket_refs) for _ in range(9)
            )
            self.kind = self.full.dtype
            self.tile = 8 if self.kind == F32 else 16
            self.sems = at * 8
            self.u0 = self.full.shape[0] // 2
            self.u1, self.u2 = self.u0 // 4, self.u0 // 16
            self.at0 = self.whole(kh * self.u0)
            self.at1 = self.whole(self.at0 + plane * self.u1)
            self.at2 = self.whole(self.at1 + bz * self.u2)
            self.final = lambda value: value

        def whole(self, at):
            return pl.multiple_of(at, self.tile)

        def cut(self, ref, at, size):
            return ref.at[pl.ds(self.whole(at), size)]

        def copy(self, stage, src, dst, device):
            k = self.sems + stage
            return pltpu.make_async_remote_copy(
                src_ref=src, dst_ref=dst, send_sem=red_send.at[k], recv_sem=red_recv.at[k],
                device_id=device, device_id_type=MESH,
            )

        def expect(self, stage, many):
            sends.append(lambda: self.copy(stage, many, many, (b, h)).wait_send())
            due["bucket", self.sems + stage] = lambda: self.copy(stage, many, many, (b, h)).wait_recv()

        def arrived(self, stage):
            arrive(("bucket", self.sems + stage))

        def s0(self):
            self.copy(0, self.cut(self.full, (1 - kh) * self.u0, self.u0), self.in0, pair_one).start()
            self.expect(0, self.in0)

        def s1(self):
            self.arrived(0)
            step = self.u1

            def one(i, carry):
                at = self.whole(i * step)
                mine = self.full[pl.ds(self.whole(self.at0 + at), step), :].astype(F32)
                self.half[pl.ds(at, step), :] = (mine + self.in0[pl.ds(at, step), :].astype(F32)).astype(self.kind)
                return carry

            lax.fori_loop(0, 4, one, 0)
            for j in range(1, 4):
                t = lax.rem(plane + j, 4)
                self.copy(1, self.cut(self.half, t * self.u1, self.u1), self.in1.at[j - 1], in_plane(t)).start()
            self.expect(1, self.in1)

        def s2(self):
            self.arrived(1)
            step = self.u2

            def one(i, carry):
                at = self.whole(i * step)
                value = self.half[pl.ds(self.whole(plane * self.u1 + at), step), :].astype(F32)
                for j in range(3):
                    value = value + self.in1[j, pl.ds(at, step), :].astype(F32)
                self.sum1[pl.ds(at, step), :] = value.astype(self.kind)
                return carry

            lax.fori_loop(0, 4, one, 0)
            for j in range(1, 4):
                t = lax.rem(bz + j, 4)
                self.copy(2, self.cut(self.sum1, t * self.u2, self.u2), self.in2.at[j - 1], in_line(t)).start()
            self.expect(2, self.in2)

        def collect(self):
            self.arrived(2)
            value = self.sum1[pl.ds(self.whole(bz * self.u2), self.u2), :].astype(F32)
            for j in range(3):
                value = value + self.in2[j].astype(F32)
            if n_groups > 1:
                self.shard[...] = value.astype(self.kind)

                def send_group(j, carry):
                    t = lax.rem(group + j, n_groups)
                    self.copy(3, self.shard, self.in3.at[group], (b + GROUP * (t - group), h)).start()
                    return carry

                lax.fori_loop(1, n_groups, send_group, 0)
                self.expect(3, self.in3.at[pl.ds(0, n_groups - 1)])
                self.in3[group] = self.shard[...]
                self.arrived(3)
                value = self.in3[0].astype(F32)
                for t in range(1, n_groups):
                    value = value + self.in3[t].astype(F32)
            return value

        def s3(self):
            self.done[pl.ds(self.at2, self.u2), :] = self.final(self.collect()).astype(self.kind)
            mine = self.done.at[pl.ds(self.at2, self.u2)]
            for j in range(1, 4):
                self.copy(4, mine, mine, in_line(lax.rem(bz + j, 4))).start()
            self.expect(4, self.done.at[pl.ds(0, 3 * self.u2)])

        def s4(self):
            self.arrived(4)
            mine = self.done.at[pl.ds(self.at1, self.u1)]
            for j in range(1, 4):
                self.copy(5, mine, mine, in_plane(lax.rem(plane + j, 4))).start()
            self.expect(5, self.done.at[pl.ds(0, 3 * self.u1)])

        def s5(self):
            self.arrived(5)
            mine = self.done.at[pl.ds(self.at0, self.u0)]
            self.copy(6, mine, mine, pair_one).start()
            self.expect(6, mine)

        def s6(self):
            self.arrived(6)

    buckets = [Bucket(k) for k in range(6)]
    bucket_e, bucket_r, bucket_n = buckets[:3]
    taps_buckets = buckets[3:]
    bucket_a, bucket_b, bucket_c = taps_buckets

    def put_taps(at, value):
        start = 0
        for bucket in taps_buckets:
            size = bucket.full.shape[0]
            low, high = max(at, start), min(at + value.shape[0], start + size)
            if low < high:
                bucket.full[low - start : high - start, :] = value[low - at : high - at].astype(BF16)
            start += size

    place_in()
    arrive(("move", 0))
    pad_in(img4, x)
    arrive(("move", 1))
    sum_one = jnp.zeros((1, narrow), F32)
    square_one = jnp.zeros((1, narrow), F32)
    for q in range(rows // 2):
        value = dot(x[pl.ds(q * 2 * block, 2 * block), :], w_reduce[...])
        c1[pl.ds((1 + 2 * q) * block, 2 * block), :] = value
        sum_one = sum_one + colsum(value)
        square_one = square_one + colsum(value * value)
    put_rows(m1, 0, sum_one)
    put_rows(m1, narrow // 128, square_one)
    put_rows(m1, 4, jnp.zeros((1, 256), F32) + count.astype(F32))
    pl.semaphore_wait(barrier, total - 1)
    send_all(m1, s1, 0)
    set_edges(c1, first1, last1)
    halo_start(first1, last1, up1, down1, 0)
    arrive(("move", 3))
    pad_in(cot4, g)
    for j in range(width // 256):
        put_rows(mx, 2 * j, colsum(x[:, j * 256 : (j + 1) * 256].astype(F32)))
    exchange(mx, sx, 8, h, lambda t: (b, t))
    for k in range(9):
        arrive(("move", 8 + k))

    sum_all(s1, 0)
    slot_total = tot[4:5, :] / n_height
    pix_total = slot_total * area
    m_one = tiled(pix_total, narrow // 128)
    mean = get_rows(tot, 0, narrow // 128) / m_one
    inv_one = lax.rsqrt(get_rows(tot, 2, narrow // 128) / m_one - mean * mean + EPSILON)
    shift_one = mean * inv_one
    scale = inv_one * gain_one[...]
    offset = bias_one[...] - mean * scale
    scale_one, offset_one = scale, offset
    arrive(("halo", 0))
    patch(c1, up1, down1)

    def hide(at, carry):
        value = c1[block_at(at), :] * scale_one + offset_one
        value = swish(value) * mask(ext(at), narrow)
        hs[0, block_at(at), :] = pltpu.roll(value, 1, axis=0).astype(BF16)
        hs[1, block_at(at), :] = value.astype(BF16)
        hs[2, block_at(at), :] = pltpu.roll(value, block - 1, axis=0).astype(BF16)
        return carry

    lax.fori_loop(0, rows + 2, hide, 0)

    arrive(("move", 2))
    for q in range(rows // 2):
        for gr in range(2):
            lhs = jnp.concatenate(
                [
                    hs[bb, (a + 2 * q) * block : (a + 2 * q + 2) * block, gr * cg : (gr + 1) * cg]
                    for a in range(3)
                    for bb in range(3)
                ],
                axis=1,
            )
            c2[(1 + 2 * q) * block : (3 + 2 * q) * block, gr * half : (gr + 1) * half] = dot(
                lhs, w_split[:, gr * half : (gr + 1) * half]
            )
    m2[...] = jnp.zeros(m2.shape, F32)
    for j in range(2):
        lanes = pl.ds(j * half, half)

        def moments(r, carry):
            value = c2[block_at(r), lanes] * mask(own(r), half)
            return carry[0] + colsum(value), carry[1] + colsum(value * value)

        zero = jnp.zeros((1, half), F32)
        sums = lax.fori_loop(1, rows + 1, moments, (zero, zero))
        put_rows(m2, j * (half // 128), sums[0])
        put_rows(m2, split // 128 + j * (half // 128), sums[1])
    send_all(m2, s2, 1)
    set_edges(c2, first2, last2)
    halo_start(first2, last2, up2, down2, 1)
    arrive(("all", 8))
    mxb[...] = jnp.sum(sx[...], axis=0)
    exchange(mxb, sxb, 12, b, lambda t: (t, h))
    place_out()
    for bb in range(3):
        hs_t[bb] = hs[bb].T

    def slopes_one(r, carry):
        conv = c1[block_at(r + 1), :]
        live = mask(own(r + 1), narrow)
        slope1[block_at(r), :] = swish_slope(conv * scale_one + offset_one) * live
        n1[block_at(r), :] = ((conv * inv_one - shift_one) * live).astype(BF16)
        return carry

    lax.fori_loop(0, rows, slopes_one, 0)

    sum_all(s2, 1)
    m_two = tiled(pix_total, split // 128)
    mean = get_rows(tot, 0, split // 128) / m_two
    inv_two = lax.rsqrt(get_rows(tot, split // 128, split // 128) / m_two - mean * mean + EPSILON)
    shift_two = mean * inv_two
    scale_two = inv_two * gain_two[...]
    offset_two = bias_two[...] - mean * scale_two
    pool = jnp.zeros((slots, half), F32)
    for j in range(2):
        lanes = pl.ds(j * half, half)
        sc, of = scale_two[:, j * half : (j + 1) * half], offset_two[:, j * half : (j + 1) * half]

        def activate(r, acc):
            value = swish(c2[block_at(r), lanes] * sc + of) * mask(own(r), half)
            act[block_at(r - 1), lanes] = value
            return acc + value

        acc = lax.fori_loop(1, rows + 1, activate, jnp.zeros((block, half), F32))
        pool = pool + per_slot(acc, slots)
    pool = pool / area
    pooled[...] = pool
    arrive(("move", 4))
    m34[...] = dot(pool, w_squeeze[...], precision=HIGHEST)
    send_all(m34, s34, 2)
    exchange(pooled, pool_h, 13, h, lambda t: (b, t))
    arrive(("all", 12))
    tot[0:8, :] = jnp.sum(sxb[...], axis=0)
    x_mean = get_rows(tot, 0, width // 128) / tiled(pix_total, width // 128)

    def centre(r, carry):
        value = (x[block_at(r), :].astype(F32) - x_mean) * mask(own(r + 1), width)
        x_t[:, block_at(r)] = value.T.astype(BF16)
        return carry

    lax.fori_loop(0, rows, centre, 0)
    for q in range(2):
        at = slice(q * (width // 2), (q + 1) * (width // 2))
        bucket_n.full[at, :] = dot(x_t[at, :], n1[...]).astype(BF16)
    bucket_n.s0()
    arrive(("move", 5))
    arrive(("all", 2))

    def gather(i, carry):
        value = jnp.sum(s34[pl.ds(i * n_height, n_height)], axis=0)
        sq_all[i] = value
        return carry[0] + colsum(value), carry[1] + colsum(value * value)

    zero = jnp.zeros((1, inner), F32)
    sum_mid, square_mid = lax.fori_loop(0, n_batch, gather, (zero, zero))
    mean_mid = sum_mid / slot_total
    inv_mid = lax.rsqrt(square_mid / slot_total - mean_mid * mean_mid + EPSILON)
    norm_mid = (sq_all[b] - mean_mid) * inv_mid
    pre_mid = norm_mid * gain_mid[...] + bias_mid[...]
    middle = swish(pre_mid)
    logits = dot(middle, w_excite[...], precision=HIGHEST) + bias_excite[...]
    top = jnp.maximum(logits[:, :half], logits[:, half:])
    expo_one = jnp.exp(logits[:, :half] - top)
    expo_two = jnp.exp(logits[:, half:] - top)
    att_one = expo_one / (expo_one + expo_two)
    att_two = expo_two / (expo_one + expo_two)
    att[:, 0:half] = att_one
    att[:, half:split] = att_two
    for s in range(slots):
        attx[s * COLS : (s + 1) * COLS, :] = jnp.broadcast_to(att[s : s + 1, :], (COLS, split))

    def mix(r, carry):
        at = block_at(r)
        mixed[at, :] = (
            attx[:, 0:half] * act[at, 0:half] + attx[:, half:split] * act[at, half:split]
        ).astype(BF16)
        return carry

    lax.fori_loop(0, rows, mix, 0)
    arrive(("move", 6))
    for j in range(width // 256):
        lanes = pl.ds(j * 256, 256)
        sums = jnp.zeros((1, 256), F32)
        squares = jnp.zeros((1, 256), F32)
        for q in range(rows // 2):
            at = pl.ds(q * 2 * block, 2 * block)
            value = dot(mixed[at, :], w_expand[:, lanes])
            c3[at, lanes] = value
            sums = sums + colsum(value)
            squares = squares + colsum(value * value)
        put_rows(m5, j * 2, sums)
        put_rows(m5, width // 128 + j * 2, squares)
    send_pairs(m5, p5, s5, 3)
    mixed_t[...] = mixed[...].T
    bucket_n.s1()
    arrive(("all", 13))
    pool_sum[...] = jnp.sum(pool_h[...], axis=0)
    exchange(pool_sum, pool_b, 14, b, lambda t: (t, h))
    arrive(("halo", 1))
    patch(c2, up2, down2)
    for j in range(2):
        lanes = pl.ds(j * half, half)
        cut = slice(j * half, (j + 1) * half)
        sc, of = scale_two[:, cut], offset_two[:, cut]
        iv, sh = inv_two[:, cut], shift_two[:, cut]

        def slopes(at, carry):
            conv = c2[block_at(at), lanes]
            value = swish_slope(conv * sc + of) * mask(ext(at), half)
            slope2[block_at(at), lanes] = value
            value = value * own(at)
            more = value * (conv * iv - sh)
            slope2n[block_at(at), lanes] = more
            return carry[0] + value, carry[1] + more

        zero = jnp.zeros((block, half), F32)
        sums = lax.fori_loop(0, rows + 2, slopes, (zero, zero))
        st_src[0:slots, lanes] = per_slot(sums[0], slots)
        st_src[slots : 2 * slots, lanes] = per_slot(sums[1], slots)
    exchange(st_src, st_h, 10, h, lambda t: (b, t))

    sum_all(s5, 3)
    wide = width // 128
    m_three = tiled(pix_total, wide)
    mean = get_rows(tot, 0, wide) / m_three
    inv_three = lax.rsqrt(get_rows(tot, wide, wide) / m_three - mean * mean + EPSILON)
    shift_three = mean * inv_three
    scale_three = inv_three * gain_three[...]
    offset_three = bias_three[...] - mean * scale_three
    part = block // 2
    for j in range(width // 256):
        lanes = pl.ds(j * 256, 256)
        cut = slice(j * 256, (j + 1) * 256)
        sc, of = scale_three[:, cut], offset_three[:, cut]
        iv, sh = inv_three[:, cut], shift_three[:, cut]

        def finish_row(i, carry):
            r, k = i // 2, lax.rem(i, 2)
            at = pl.ds(pl.multiple_of(i * part, part), part)
            conv = c3[at, lanes]
            pre = conv * sc + of + x[at, lanes].astype(F32)
            sigma = sigmoid(pre)
            value = pre * sigma
            live = tiled(pix[pl.ds(pl.multiple_of(k * part, part), part), :] * own(r + 1), 2)
            xo[at, lanes] = (value * live).astype(BF16)
            slope = sigma + value * (1.0 - sigma)
            grad = g[at, lanes].astype(F32) * slope
            d3[at, lanes] = grad
            return carry[0] + colsum(grad), carry[1] + colsum(grad * (conv * iv - sh))

        zero = jnp.zeros((1, 256), F32)
        sums = lax.fori_loop(0, 2 * rows, finish_row, (zero, zero))
        put_rows(p6, j * 2, sums[0])
        put_rows(p6, wide + j * 2, sums[1])
    m6[...] = p6[...].astype(BF16)
    send_all(m6, s6, 4)
    pad_out(xo, out4)
    move(7, out4, output)
    bucket_n.s2()
    arrive(("all", 10))
    st_sum[...] = jnp.sum(st_h[...], axis=0)
    st_low[...] = st_sum[...].astype(BF16)
    exchange(st_low, st_b, 11, b, lambda t: (t, h))

    sum_all(s6, 4)
    gb_three = get_rows(tot, 0, wide)
    gg_three = get_rows(tot, wide, wide)
    vectors[0:1, :] = gb_three
    vectors[1:2, :] = gg_three
    gg = gg_three / m_three
    k_one = scale_three
    k_three = k_one * inv_three * gg
    k_two = k_one * (gb_three / m_three - shift_three * gg)
    for j in range(width // 256):
        lanes = pl.ds(j * 256, 256)
        cut = slice(j * 256, (j + 1) * 256)
        ka, kb, kc = k_one[:, cut], k_two[:, cut], k_three[:, cut]

        def back_three(i, carry):
            at = pl.ds(pl.multiple_of(i * part, part), part)
            gc3[at, lanes] = (d3[at, lanes] * ka - kb - c3[at, lanes] * kc).astype(BF16)
            return carry

        lax.fori_loop(0, 2 * rows, back_three, 0)
    for q in range(rows // 2):
        gm[pl.ds((1 + 2 * q) * block, 2 * block), :] = dot(
            gc3[pl.ds(2 * q * block, 2 * block), :], w_expand[...], NT
        )
    att_sums = [[], [], []]
    for j in range(2):
        lanes = pl.ds(j * half, half)
        parts = [[], [], []]
        for k in range(2):
            zero = jnp.zeros((part, half), F32)

            def attend(r, acc):
                at = pl.ds(pl.multiple_of(r * block + k * part, part), part)
                up_at = pl.ds(pl.multiple_of((r + 1) * block + k * part, part), part)
                value = gm[up_at, :]
                return (
                    acc[0] + value * act[at, lanes],
                    acc[1] + value * own(r + 1) * slope2[up_at, lanes],
                    acc[2] + value * slope2n[up_at, lanes],
                )

            acc = lax.fori_loop(0, rows, attend, (zero, zero, zero))
            for i in range(3):
                parts[i].append(per_slot(acc[i], slots // 2))
        for i in range(3):
            att_sums[i].append(jnp.concatenate(parts[i], axis=0))
    grad_att = att_sums[0]
    blend = att_one * grad_att[0] + att_two * grad_att[1]
    grad_logits = jnp.concatenate(
        [att_one * (grad_att[0] - blend), att_two * (grad_att[1] - blend)], axis=1
    )
    em_part = dot(grad_logits, w_excite[...], NT, HIGHEST) * swish_slope(pre_mid)
    em_src[...] = em_part
    mid_scale = inv_mid * gain_mid[...] / area
    pooled_part = dot(em_part * mid_scale, w_squeeze[...], NT, HIGHEST)
    for j in range(2):
        lanes = pl.ds(j * half, half)
        weight = att_one if j == 0 else att_two
        for i in range(2):
            sums = weight * att_sums[1 + i][j] + pooled_part * st_sum[i * slots : (i + 1) * slots, lanes]
            put_rows(m78, (i * 2 + j) * (half // 128), colsum(sums))
    put_rows(m78, 2 * split // 128, colsum(em_part))
    put_rows(m78, 2 * split // 128 + 1, colsum(em_part * norm_mid))
    send_all(m78, s78, 5)
    exchange(em_src, em_all, 9, h, lambda t: (b, t))
    set_edges(gm, first3, last3)
    halo_start(first3, last3, up3, down3, 2)
    for j in range(width // 256):
        bucket_e.full[j * narrow : (j + 1) * narrow, :] = dot(
            mixed_t[...], gc3[:, j * 256 : (j + 1) * 256]
        ).astype(BF16)
    bucket_e.s0()
    grad_excite = dot(middle, grad_logits, TN, HIGHEST)
    for gr in range(2):
        put_taps(18 * cg + gr * inner, grad_excite[:, gr * half : (gr + 1) * half])
    bias_part = colsum(grad_logits)
    put_rows(m10, 2 * (narrow // 128), bias_part)
    bucket_e.s1()
    arrive(("all", 11))
    every = n_batch * slots
    mid_all = ((sq_all[...] - mean_mid) * inv_mid).reshape(every, inner)
    st_all = st_b[...].astype(F32)
    w_turned = tiled(w_squeeze[...].T, 2)
    for i in range(2):
        sums = st_all[:, i * slots : (i + 1) * slots, :].reshape(every, split)
        wns[:, i * split : (i + 1) * split] = w_turned * dot(mid_all, sums, TN, HIGHEST)
        st_tot[i : i + 1, :] = colsum(sums)

    sum_all(s78, 5)
    rows_mid = 2 * split // 128
    gb_mid, gg_mid = tot[rows_mid : rows_mid + 1, :], tot[rows_mid + 1 : rows_mid + 2, :]
    vectors[4:5, 0:128] = gb_mid
    vectors[4:5, 128:256] = gg_mid
    mid_k = mid_scale / slot_total
    pooled_all = dot(jnp.broadcast_to(mid_k * gb_mid, (8, inner)), w_squeeze[...], NT, HIGHEST)[0:1]
    turned = dot(jnp.broadcast_to(mid_k * gg_mid, (8, inner)), wns[...], precision=HIGHEST)[0:1]
    pooled_all = tiled(pooled_all, 2)
    gb_two = get_rows(tot, 0, split // 128) - pooled_all * st_tot[0:1, :] - turned[:, :split]
    gg_two = get_rows(tot, split // 128, split // 128) - pooled_all * st_tot[1:2, :] - turned[:, split:]
    vectors[2:3, 0:split] = gb_two
    vectors[2:3, split : 2 * split] = gg_two
    arrive(("all", 9))
    em = jnp.sum(em_all[...], axis=0)
    em_sum[...] = em
    slot_live = jnp.where(lax.broadcasted_iota(jnp.int32, (slots, inner), 0) < count, 1.0, 0.0)
    grad_sq = (
        slot_live * inv_mid * gain_mid[...]
        * (em - gb_mid / slot_total - norm_mid * gg_mid / slot_total)
    )
    grad_pooled = dot(grad_sq, w_squeeze[...], NT, HIGHEST) / area
    att[:, 0:half] = grad_pooled
    for s in range(slots):
        gpx[s * COLS : (s + 1) * COLS, :] = jnp.broadcast_to(att[s : s + 1, 0:half], (COLS, half))
    arrive(("halo", 2))
    patch(gm, up3, down3)
    gg = gg_two / m_two
    k_one = scale_two
    k_three = k_one * inv_two * gg
    k_two = k_one * (gb_two / m_two - shift_two * gg)
    for j in range(2):
        lanes = pl.ds(j * half, half)
        cut = slice(j * half, (j + 1) * half)
        ka, kb, kc = k_one[:, cut], k_two[:, cut], k_three[:, cut]

        def back_two(at, carry):
            value = (attx[:, lanes] * gm[block_at(at), :] + gpx[...]) * slope2[block_at(at), lanes]
            value = value * ka - kb - c2[block_at(at), lanes] * kc
            gc2[block_at(at), lanes] = (value * mask(ext(at), half)).astype(BF16)
            return carry

        lax.fori_loop(0, rows + 2, back_two, 0)
    gc2_own[...] = (gc2[block_at(rows), :].astype(F32) * own(rows)).astype(BF16)

    def taps_grad(k):
        gr, bb = k // 3, k % 3
        lhs = jnp.concatenate(
            [hs_t[bb, gr * cg : (gr + 1) * cg, a * block : a * block + pixels] for a in range(3)], axis=0
        )
        lanes = slice(gr * half, (gr + 1) * half)
        rhs = jnp.concatenate([gc2[block:pixels, lanes], gc2_own[:, lanes]], axis=0)
        put_taps(k * 3 * cg, dot(lhs, rhs))

    for k in range(3):
        taps_grad(k)
    bucket_a.s0()
    for k in range(3, 6):
        taps_grad(k)
    exchange(em_sum, em_b, 15, b, lambda t: (t, h))
    bucket_a.s1()
    bucket_e.s2()
    bucket_b.s0()
    for gr in range(2):
        outs = []
        for bb in range(3):
            lhs = jnp.concatenate(
                [gc2[(2 - a) * block : (2 - a) * block + pixels, gr * half : (gr + 1) * half] for a in range(3)],
                axis=1,
            )
            rhs = jnp.concatenate(
                [
                    w_split[(a * 3 + bb) * cg : (a * 3 + bb + 1) * cg, gr * half : (gr + 1) * half]
                    for a in range(3)
                ],
                axis=1,
            )
            outs.append(dot(lhs, rhs, NT))
        gh[:, gr * cg : (gr + 1) * cg] = (
            outs[1] + pltpu.roll(outs[2], 1, axis=0) + pltpu.roll(outs[0], pixels - 1, axis=0)
        )
    bucket_b.s1()
    def back_hidden(r, carry):
        value = gh[block_at(r), :] * slope1[block_at(r), :]
        gh[block_at(r), :] = value
        d1[block_at(r), :] = value.astype(BF16)
        norm = c1[block_at(r + 1), :] * inv_one - shift_one
        return carry[0] + colsum(value), carry[1] + colsum(value * norm)
    zero = jnp.zeros((1, narrow), F32)
    sums = lax.fori_loop(0, rows, back_hidden, (zero, zero))
    put_rows(m10, 0, sums[0])
    put_rows(m10, narrow // 128, sums[1])
    send_all(m10, s10, 7)
    for q in range(2):
        at = slice(q * (width // 2), (q + 1) * (width // 2))
        bucket_r.full[at, :] = dot(x_t[at, :], d1[...]).astype(BF16)
    bucket_r.s0()
    bucket_c.s0()
    bucket_r.s1()
    bucket_a.s2()
    bucket_e.s3()
    bucket_c.s1()
    bucket_b.s2()
    kept_n = bucket_n.collect()
    sum_all(s10, 7)
    gb_one = get_rows(tot, 0, narrow // 128)
    gg_one = get_rows(tot, narrow // 128, narrow // 128)
    vectors[3:4, 0:narrow] = gb_one
    vectors[3:4, narrow : 2 * narrow] = gg_one
    vectors[3:4, 2 * narrow : 2 * narrow + split] = get_rows(tot, 2 * (narrow // 128), split // 128)
    move(6, vectors, vectors_out)
    gg = gg_one / m_one
    k_one = scale_one
    k_three = k_one * inv_one * gg
    k_two = k_one * (gb_one / m_one - shift_one * gg)
    def back_one(r, carry):
        value = gh[block_at(r), :] * k_one - k_two - c1[block_at(r + 1), :] * k_three
        gc1[block_at(r), :] = (value * mask(own(r + 1), narrow)).astype(BF16)
        return carry
    lax.fori_loop(0, rows, back_one, 0)
    bucket_r.final = lambda value: scale_one * (value - kept_n * gg)
    arrive(("all", 14))
    arrive(("all", 15))
    sq_grads = (inv_mid * gain_mid[...]) * (
        em_b[...].reshape(every, inner) - gb_mid / slot_total - mid_all * gg_mid / slot_total
    )
    squeeze_grad[...] = dot(pool_b[...].reshape(every, half), sq_grads, TN, HIGHEST)
    move(3, squeeze_grad, big_q)
    arrive(("move", 7))
    bucket_a.s3()
    def back_image(r, carry):
        value = d3[block_at(r), :] + dot(gc1[block_at(r), :], w_reduce[...], NT)
        xo[block_at(r), :] = value.astype(BF16)
        return carry
    lax.fori_loop(0, rows, back_image, 0)
    bucket_r.s2()
    bucket_e.s4()
    bucket_c.s2()
    pad_out(xo, out4)
    move(7, out4, grad_images)
    bucket_b.s3()
    bucket_a.s4()
    bucket_r.s3()
    bucket_c.s3()
    bucket_e.s5()
    bucket_b.s4()
    bucket_e.s6()
    move(0, bucket_e.done, big_e)
    bucket_a.s5()
    bucket_r.s4()
    bucket_c.s4()
    bucket_a.s6()
    move(1, bucket_a.done, big_a)
    bucket_b.s5()
    bucket_b.s6()
    move(4, bucket_b.done, big_b)
    bucket_r.s5()
    bucket_c.s5()
    bucket_r.s6()
    move(2, bucket_r.done, big_r)
    bucket_c.s6()
    move(5, bucket_c.done, big_c)

    for wait in sends:
        wait()
    for key in list(due):
        arrive(key)


def unpack_kernel(
    out_a, gimg_a, big_e, big_a, big_b, big_c, big_r, big_q, vectors,
    output, grad_images, grad_reduce, grad_split, grad_squeeze, grad_excite, grad_expand,
    grad_gain_one, grad_bias_one, grad_gain_two, grad_bias_two,
    grad_gain_mid, grad_bias_mid, grad_bias_excite, grad_gain_three, grad_bias_three,
    in_e, in_a, in_b, in_c, in_r, in_v, in_o, in_g, in_q, out_e, out_s, out_x, out_r, sems,
):
    def move(k, src, dst):
        copy = pltpu.make_async_copy(src, dst, sems.at[k])
        copy.start()
        return copy

    ins = [move(k, src, dst) for k, (src, dst) in enumerate([
        (out_a, in_o), (big_e, in_e), (gimg_a, in_g), (big_r, in_r), (big_a, in_a), (big_b, in_b), (big_c, in_c),
        (big_q, in_q), (vectors, in_v),
    ])]
    narrow = grad_expand.shape[0]
    taps, split = grad_split.shape
    half = split // 2
    inner = grad_excite.shape[0]
    outs = []
    ins[0].wait()
    outs.append(move(9, in_o, output))
    ins[1].wait()
    for j in range(grad_expand.shape[1] // 256):
        out_e[:, j * 256 : (j + 1) * 256] = in_e[j * narrow : (j + 1) * narrow, :].astype(F32)
    outs.append(move(10, out_e, grad_expand))
    ins[2].wait()
    outs.append(move(11, in_g, grad_images))
    ins[3].wait()
    out_r[...] = in_r[...].astype(F32)
    outs.append(move(12, out_r, grad_reduce))
    for k in range(4, 7):
        ins[k].wait()

    def put(at, dst, to, lanes, size):
        start = 0
        for ref in (in_a, in_b, in_c):
            low, high = max(at, start), min(at + size, start + ref.shape[0])
            if low < high:
                dst[to + low - at : to + high - at, lanes] = ref[low - start : high - start, :].astype(F32)
            start += ref.shape[0]

    cg = taps // 9
    for k in range(18):
        gr, bb, a = k // 9, k // 3 % 3, k % 3
        put(k * cg, out_s, (a * 3 + bb) * cg, slice(gr * half, (gr + 1) * half), cg)
    outs.append(move(13, out_s, grad_split))
    for gr in range(2):
        put(18 * cg + gr * inner, out_x, 0, slice(gr * half, (gr + 1) * half), inner)
    outs.append(move(14, out_x, grad_excite))
    ins[7].wait()
    outs.append(move(15, in_q, grad_squeeze))
    ins[8].wait()
    for dst, line, at in [
        (grad_bias_three, 0, 0), (grad_gain_three, 1, 0), (grad_bias_two, 2, 0), (grad_gain_two, 2, split),
        (grad_bias_one, 3, 0), (grad_gain_one, 3, narrow), (grad_bias_excite, 3, 2 * narrow),
        (grad_bias_mid, 4, 0), (grad_gain_mid, 4, inner),
    ]:
        dst[...] = in_v[line : line + 1, at : at + dst.shape[1]]
    for copy in outs:
        copy.wait()


def shards(
    n_batch, n_height,
    images, counts, row_valid, w_reduce, gain_one, bias_one, w_split, gain_two, bias_two, w_squeeze,
    gain_mid, bias_mid, w_excite, bias_excite, w_expand, gain_three, bias_three, cotangent,
):
    slots, rows, cols, width = images.shape
    count = slots * rows * cols
    narrow = w_reduce.shape[1]
    split = w_split.shape[3]
    taps = 9 * w_split.shape[2]
    inner = w_squeeze.shape[1]
    half = split // 2
    total = n_batch * n_height
    block = slots * COLS
    pixels = rows * block
    padded = pixels + 2 * block
    n_groups = n_batch // GROUP

    def row(v):
        return v.reshape(1, -1)

    unit = 4 * GROUP * 16
    size_e = width // 256 * narrow
    size_r = width
    taps_rows = 2 * taps + 2 * inner
    size_a = -(-taps_rows // (5 * unit)) * 2 * unit
    size_c = taps_rows - 2 * size_a

    def bucket(size, lanes=256, kind=BF16):
        kept = size // 2
        shapes = [
            (size, lanes), (kept, lanes), (kept, lanes), (3, kept // 4, lanes), (kept // 4, lanes),
            (3, kept // 16, lanes), (n_groups, kept // 16, lanes), (kept // 16, lanes), (size, lanes),
        ]
        return [pltpu.VMEM(dims, kind) for dims in shapes]

    messages = [(3, 2, 128), (8, 128), (8, 128), (16, 128), (16, 128), (5, 2, 128), (8, 128), (8, 128), (8, 128)]
    kinds = [BF16 if k == 4 else F32 for k in range(len(messages))]
    vm = pltpu.VMEM
    scratch = (
        [vm((1, k), F32) for k in (narrow, narrow, split, split, inner, inner, split, width, width)]
        + [vm((slots * cols, rows, width), BF16)] * 3
        + [vm((width, narrow), BF16), vm((taps, split), BF16), vm((narrow, inner), F32), vm((inner, split), F32),
           vm((narrow, width), BF16)]
        + [vm((pixels, width), BF16), vm((pixels, width), BF16), vm((block, 128), F32), vm((pixels, count), BF16),
           vm((count, pixels), BF16)]
        + [vm((padded, narrow), F32), vm((3, padded, narrow), BF16), vm((padded, split), F32), vm((pixels, split), F32),
           vm((padded, split), F32), vm((pixels, half), BF16), vm((pixels, width), F32), vm((pixels, width), F32),
           vm((pixels, width), BF16), vm((pixels, width), BF16), vm((padded, half), F32),
           vm((padded, split), F32), vm((padded, split), BF16), vm((pixels, narrow), F32), vm((pixels, narrow), F32),
           vm((pixels, narrow), BF16), vm((block, split), BF16), vm((pixels, narrow), BF16), vm((pixels, narrow), BF16)]
        + [vm((2 * slots, split), F32), vm((n_height, 2 * slots, split), F32), vm((2 * slots, split), F32),
           vm((2 * slots, split), BF16), vm((n_batch, 2 * slots, split), BF16), vm((inner, 2 * split), F32),
           vm((8, split), F32)]
        + [vm((width, pixels), BF16), vm((half, pixels), BF16), vm((3, narrow, padded), BF16), vm((slots, split), F32),
           vm((block, split), F32), vm((block, half), F32), vm((slots, half), F32), vm((n_batch, slots, inner), F32),
           vm((16, 128), F32)]
        + [vm(dims, kinds[k]) for k, dims in enumerate(messages)] + [vm((16, 128), F32)] * 2 + [vm((8, width), F32)]
        + [vm((n_height, slots, half), F32), vm((slots, half), F32), vm((n_batch, slots, half), F32), vm((slots, inner), F32),
           vm((n_batch, slots, inner), F32), vm((narrow, inner), F32), vm((slots, inner), F32)]
        + [vm((total // 2 if k == 3 else total,) + dims, kinds[k]) for k, dims in enumerate(messages[:-2])]
        + [vm((n_height,) + messages[-1], F32), vm((n_batch,) + messages[-1], F32)] + [vm((n_height, slots, inner), F32)]
        + [vm((block, narrow), F32)] * 4 + [vm((block, split), BF16)] * 4 + [vm((block, half), BF16)] * 4
        + [pltpu.SMEM((1,), jnp.int32), pltpu.SMEM((rows,), jnp.int32)]
        + [pltpu.SemaphoreType.DMA((k,)) for k in (19, 16, 16, 8, 8, 6, 6, 48, 48)]
        + bucket(size_e) + bucket(size_r) * 2 + bucket(size_a) * 2 + bucket(size_c)
    )
    vmem = pl.BlockSpec(memory_space=pltpu.VMEM)
    hbm = pl.BlockSpec(memory_space=pltpu.HBM)
    shape = jax.ShapeDtypeStruct
    flat = (slots * cols, rows, width)

    def by_column(value):
        return value.transpose(0, 2, 1, 3).reshape(flat)

    def by_row(value):
        return value.reshape(slots, cols, rows, width).transpose(0, 2, 1, 3)

    out_a, gimg_a, big_e, big_a, big_b, big_c, big_r, big_q, vectors = pl.pallas_call(
        functools.partial(main_kernel, n_batch, n_height, (slots, cols, rows, width)),
        out_shape=(
            shape(flat, BF16), shape(flat, BF16), shape((size_e, 256), BF16),
            shape((size_a, 256), BF16), shape((size_a, 256), BF16), shape((size_c, 256), BF16), shape((size_r, 256), BF16),
            shape((narrow, inner), F32),
            shape((8, width), F32),
        ),
        in_specs=[hbm] * 18,
        out_specs=[hbm] * 9,
        scratch_shapes=scratch,
        compiler_params=pltpu.CompilerParams(
            collective_id=0, has_side_effects=True, vmem_limit_bytes=58 * 1024 * 1024
        ),
    )(
        counts, row_valid, row(gain_one), row(bias_one), row(gain_two), row(bias_two), row(gain_mid), row(bias_mid),
        row(bias_excite), row(gain_three), row(bias_three),
        by_column(images), by_column(cotangent), w_reduce, w_split.reshape(taps, split), w_squeeze, w_excite, w_expand,
    )
    (
        output, grad_images, grad_reduce, grad_split, grad_squeeze, grad_excite, grad_expand,
        grad_gain_one, grad_bias_one, grad_gain_two, grad_bias_two,
        grad_gain_mid, grad_bias_mid, grad_bias_excite, grad_gain_three, grad_bias_three,
    ) = pl.pallas_call(
        unpack_kernel,
        out_shape=(
            shape(flat, BF16), shape(flat, BF16), shape((width, narrow), F32), shape((taps, split), F32),
            shape((narrow, inner), F32), shape((inner, split), F32), shape((narrow, width), F32),
            shape((1, narrow), F32), shape((1, narrow), F32), shape((1, split), F32), shape((1, split), F32),
            shape((1, inner), F32), shape((1, inner), F32), shape((1, split), F32), shape((1, width), F32),
            shape((1, width), F32),
        ),
        in_specs=[hbm] * 9,
        out_specs=[hbm] * 7 + [vmem] * 9,
        scratch_shapes=[
            vm((size_e, 256), BF16), vm((size_a, 256), BF16), vm((size_a, 256), BF16), vm((size_c, 256), BF16), vm((size_r, 256), BF16),
            vm((8, width), F32),
            vm(flat, BF16), vm(flat, BF16), vm((narrow, inner), F32),
            vm((narrow, width), F32), vm((taps, split), F32), vm((inner, split), F32), vm((width, narrow), F32),
            pltpu.SemaphoreType.DMA((16,)),
        ],
        compiler_params=pltpu.CompilerParams(vmem_limit_bytes=60 * 1024 * 1024),
    )(out_a, gimg_a, big_e, big_a, big_b, big_c, big_r, big_q, vectors)

    def like(value, other):
        return value.reshape(other.shape)

    return (
        by_row(output), by_row(grad_images), grad_reduce, like(grad_gain_one, gain_one), like(grad_bias_one, bias_one),
        like(grad_split, w_split), like(grad_gain_two, gain_two), like(grad_bias_two, bias_two), grad_squeeze,
        like(grad_gain_mid, gain_mid), like(grad_bias_mid, bias_mid), grad_excite, like(grad_bias_excite, bias_excite),
        grad_expand, like(grad_gain_three, gain_three), like(grad_bias_three, bias_three),
    )


def solution(mesh):
    axes = mesh.shape
    split_in = P("batch", "height", None, None)
    return jax.shard_map(
        functools.partial(shards, axes["batch"], axes["height"]),
        mesh=mesh,
        in_specs=(split_in, P("batch"), P("height")) + (P(),) * 14 + (split_in,),
        out_specs=(split_in, split_in) + (P(),) * 14,
        check_vma=False,
    )
```

```python
import functools

import jax
import jax.numpy as jnp
from jax import lax
from jax.experimental import pallas as pl
from jax.experimental.pallas import tpu as pltpu
from jax.sharding import PartitionSpec as P

IMG_H = 14
IMG_W = 14
EPSILON = 1e-05
MESH = pl.DeviceIdType.MESH
F32 = jnp.float32
BF16 = jnp.bfloat16
HIGHEST = lax.Precision.HIGHEST
COLS = 16
GROUP = 8
NN = (((1,), (0,)), ((), ()))
NT = (((1,), (1,)), ((), ()))
TN = (((0,), (0,)), ((), ()))


def dot(lhs, rhs, dims=NN, precision=None):
    return lax.dot_general(lhs, rhs, dims, precision=precision, preferred_element_type=F32)


def sigmoid(values):
    return 0.5 * jnp.tanh(0.5 * values) + 0.5


def swish(values):
    return values * sigmoid(values)


def swish_slope(values):
    sigma = sigmoid(values)
    return sigma + values * sigma * (1.0 - sigma)


def tiled(row, times):
    return jnp.concatenate([row] * times, axis=1) if times > 1 else row


def colsum(values):
    return jnp.sum(values, axis=0, keepdims=True)


def put_rows(ref, at, row):
    for k in range(row.shape[1] // 128):
        piece = row[:, k * 128 : (k + 1) * 128]
        if len(ref.shape) == 3:
            ref[(at + k) // 2, (at + k) % 2 : (at + k) % 2 + 1, :] = piece
        else:
            ref[at + k : at + k + 1, :] = piece


def get_rows(ref, at, count):
    return jnp.concatenate([ref[at + k : at + k + 1, :] for k in range(count)], axis=1)


def per_slot(values, slots):
    return jnp.sum(values.reshape(slots, COLS, values.shape[1]), axis=1)


def main_kernel(n_batch, n_height, sizes, *refs):
    (
        counts_in, row_valid_in, *refs,
    ) = refs
    small_in, refs = refs[:9], refs[9:]
    (
        images, cotangent, w_reduce_in, w_split_in, w_squeeze_in, w_excite_in, w_expand_in,
        output, grad_images, big_e, big_a, big_b, big_c, big_r, big_q, vectors_out,
        gain_one, bias_one, gain_two, bias_two, gain_mid, bias_mid, bias_excite, gain_three, bias_three,
        img4, cot4, out4, w_reduce, w_split, w_squeeze, w_excite, w_expand,
        x, g, pix, to_pad, from_pad, c1, hs, c2, act, slope2, mixed, c3, d3, xo, gc3, gm, slope2n, gc2, gh, slope1, gc1,
        gc2_own, n1, d1, st_src, st_h, st_sum, st_low, st_b, wns, st_tot, x_t, mixed_t, hs_t, att, attx, gpx, pooled, sq_all, tot,
        m1, m2, m34, m5, m6, m78, m10, mx, mxb, p5, p6, vectors, pool_h, pool_sum, pool_b, em_sum, em_b, squeeze_grad, em_src,
        s1, s2, s34, s5, s6, s78, s10, sx, sxb, em_all,
        first1, last1, up1, down1, first2, last2, up2, down2, first3, last3, up3, down3,
        counts, row_valid, local_sem, all_send, all_recv, pair_send, pair_recv, halo_send, halo_recv, red_send, red_recv,
        *bucket_refs,
    ) = refs
    slots, cols, rows, width = sizes
    narrow = w_reduce.shape[1]
    split = w_split.shape[1]
    half = split // 2
    cg = w_split.shape[0] // 9
    inner = w_squeeze.shape[1]
    block = slots * COLS
    pixels = rows * block
    total = n_batch * n_height
    area = float(IMG_H * IMG_W)
    b = lax.axis_index("batch")
    h = lax.axis_index("height")
    me = b * n_height + h

    sends = []
    due = {}

    def arrive(key):
        due.pop(key)()

    def move(key, src, dst):
        copy = pltpu.make_async_copy(src, dst, local_sem.at[key])
        copy.start()
        due["move", key] = copy.wait

    move(17, counts_in, counts)
    move(18, row_valid_in, row_valid)
    move(0, images, img4)
    move(1, w_reduce_in, w_reduce)
    barrier = pltpu.get_barrier_semaphore()

    def greet(j, carry):
        t = lax.rem(me + j, total)
        pl.semaphore_signal(
            barrier, inc=1, device_id=(t // n_height, lax.rem(t, n_height)), device_id_type=MESH
        )
        return carry

    lax.fori_loop(1, total, greet, 0)
    small = (gain_one, bias_one, gain_two, bias_two, gain_mid, bias_mid, bias_excite, gain_three, bias_three)
    for k, (src, dst) in enumerate(zip(small_in, small)):
        move(8 + k, src, dst)
    move(2, w_split_in, w_split)
    move(3, cotangent, cot4)
    move(4, w_squeeze_in, w_squeeze)
    move(5, w_excite_in, w_excite)
    move(6, w_expand_in, w_expand)


    kh, kq = lax.rem(h, 2), h // 2
    pair_one = (b, h + 1 - 2 * kh)
    pair_two = (b, h + 2 - 4 * kq)

    def circle(dst):
        if dst.shape[0] == total:
            return me, lambda t: (t // n_height, lax.rem(t, n_height))
        pairs = n_height // 2
        return b * pairs + kq, lambda t: (t // pairs, 2 * lax.rem(t, pairs) + kh)

    def send_all(src, dst, k):
        exchange(src, dst, k, *circle(dst))

    def exchange(src, dst, k, here, device):
        others = dst.shape[0]

        def one(j, carry):
            t = jnp.where(2 * here < others, others - 1 - j, j)

            @pl.when(t != here)
            def _():
                pltpu.make_async_remote_copy(
                    src_ref=src, dst_ref=dst.at[here], send_sem=all_send.at[k], recv_sem=all_recv.at[k],
                    device_id=device(t), device_id_type=MESH,
                ).start()

            return carry

        lax.fori_loop(0, others, one, 0)
        dst[here] = src[...]
        sends.append(lambda: all_copy(dst, k).wait_send())
        due["all", k] = lambda: all_copy(dst, k).wait_recv()

    def all_copy(dst, k):
        many = dst.at[pl.ds(0, dst.shape[0] - 1)]
        return pltpu.make_async_remote_copy(
            src_ref=many, dst_ref=many,
            send_sem=all_send.at[k], recv_sem=all_recv.at[k], device_id=(b, h), device_id_type=MESH,
        )

    def send_pairs(src, arrived, dst, k):
        copy = pltpu.make_async_remote_copy(
            src_ref=src, dst_ref=arrived, send_sem=pair_send.at[k], recv_sem=pair_recv.at[k],
            device_id=pair_one, device_id_type=MESH,
        )
        copy.start()
        copy.wait()
        src[...] = src[...] + arrived[...]
        send_all(src, dst, k)

    def sum_all(dst, k):
        arrive(("all", k))

        def one(i, acc):
            return acc + jnp.sum(dst[pl.ds(i * 8, 8)].astype(F32), axis=0)

        acc = lax.fori_loop(0, dst.shape[0] // 8, one, jnp.zeros(dst.shape[1:], F32))
        if len(dst.shape) == 4:
            for i in range(dst.shape[1]):
                tot[2 * i : 2 * i + 2, :] = acc[i]
        else:
            tot[0 : dst.shape[1], :] = acc

    def halo_copies(first, last, up, down, k):
        above = pltpu.make_async_remote_copy(
            src_ref=last, dst_ref=up, send_sem=halo_send.at[2 * k], recv_sem=halo_recv.at[2 * k],
            device_id=(b, lax.rem(h + 1, n_height)), device_id_type=MESH,
        )
        below = pltpu.make_async_remote_copy(
            src_ref=first, dst_ref=down, send_sem=halo_send.at[2 * k + 1],
            recv_sem=halo_recv.at[2 * k + 1],
            device_id=(b, lax.rem(h + n_height - 1, n_height)), device_id_type=MESH,
        )
        return above, below

    def halo_start(first, last, up, down, k):
        above, below = halo_copies(first, last, up, down, k)

        @pl.when(h < n_height - 1)
        def _():
            above.start()

        @pl.when(h > 0)
        def _():
            below.start()

        sends.append(lambda: halo_sent(first, last, up, down, k))
        due["halo", k] = lambda: halo_here(first, last, up, down, k)

        @pl.when(h == 0)
        def _():
            up[...] = jnp.zeros(up.shape, up.dtype)

        @pl.when(h == n_height - 1)
        def _():
            down[...] = jnp.zeros(down.shape, down.dtype)

    def halo_here(first, last, up, down, k):
        above, below = halo_copies(first, last, up, down, k)

        @pl.when(h > 0)
        def _():
            above.wait_recv()

        @pl.when(h < n_height - 1)
        def _():
            below.wait_recv()

    def halo_sent(first, last, up, down, k):
        above, below = halo_copies(first, last, up, down, k)

        @pl.when(h < n_height - 1)
        def _():
            above.wait_send()

        @pl.when(h > 0)
        def _():
            below.wait_send()

    arrive(("move", 17))
    arrive(("move", 18))
    count = counts[0]
    filled = row_valid[0]
    for r in range(1, rows):
        filled = filled + row_valid[r]

    def flag(cond):
        return jnp.where(cond, 1.0, 0.0).astype(F32)

    def own(at):
        return flag((at >= 1) & (at <= filled))

    def ext(at):
        return flag(
            ((at >= 1) & (at <= filled))
            | ((at == 0) & (h > 0))
            | ((at == filled + 1) & (h < n_height - 1))
        )

    def mask(scale, lanes, start=0, size=block):
        return tiled(pix[start : start + size, :] * scale, lanes // 128)

    def block_at(at):
        return pl.ds(at * block if isinstance(at, int) else pl.multiple_of(at * block, block), block)

    def set_edges(src, first, last):
        first[...] = src[block_at(1), :].astype(first.dtype)
        value = jnp.zeros(last.shape, F32)
        for r in range(IMG_H // n_height - 1, rows):
            value = value + src[block_at(r + 1), :] * flag(filled == r + 1)
        last[...] = value.astype(last.dtype)

    def patch(ref, up, down):
        below = down[...].astype(F32)
        ref[block_at(0), :] = up[...].astype(F32)
        ref[block_at(rows + 1), :] = below
        whole = flag(filled == rows)
        ref[block_at(rows), :] = ref[block_at(rows), :] * whole + below * (1.0 - whole)

    iota = lax.broadcasted_iota(jnp.int32, (block, 128), 0)
    pix[...] = jnp.where(((iota >> 4) < count) & ((iota & 15) < cols), 1.0, 0.0)

    def places(shape, dim):
        at = lax.broadcasted_iota(jnp.int32, shape, dim)
        r, s, c = at // block, (at >> 4) & (slots - 1), at & 15
        return r, s, c, (s * cols + c) * rows + r

    def place_in():
        shape = (pixels, slots * cols * rows)
        r, s, c, at = places(shape, 0)
        live = (c < cols) & (s < count) & (r < filled)
        other = lax.broadcasted_iota(jnp.int32, shape, 1)
        to_pad[...] = jnp.where((other == at) & live, 1.0, 0.0).astype(BF16)

    def place_out():
        shape = (slots * cols * rows, pixels)
        r, s, c, at = places(shape, 1)
        other = lax.broadcasted_iota(jnp.int32, shape, 0)
        from_pad[...] = jnp.where((other == at) & (c < cols), 1.0, 0.0).astype(BF16)

    def pad_in(src, dst):
        value = src[...].reshape(slots * cols * rows, width)
        for q in range(rows):
            at = slice(q * block, (q + 1) * block)
            dst[at, :] = dot(to_pad[at, :], value).astype(BF16)

    def pad_out(src, dst):
        for j in range(width // 256):
            lanes = slice(j * 256, (j + 1) * 256)
            value = dot(from_pad[...], src[:, lanes]).astype(BF16)
            dst[:, :, lanes] = value.reshape(slots * cols, rows, 256)

    bx, bz = lax.rem(b, 2), lax.rem(b // 2, 4)
    group, n_groups = b // GROUP, n_batch // GROUP
    plane = 2 * kq + bx
    bucket_refs = iter(bucket_refs)

    def in_plane(t):
        return (b - bx + lax.rem(t, 2), 2 * (t // 2) + kh)

    def in_line(t):
        return (b + 2 * (t - bz), h)

    class Bucket:
        def __init__(self, at):
            self.full, self.in0, self.half, self.in1, self.sum1, self.in2, self.in3, self.shard, self.done = (
                next(bucket_refs) for _ in range(9)
            )
            self.kind = self.full.dtype
            self.tile = 8 if self.kind == F32 else 16
            self.sems = at * 8
            self.u0 = self.full.shape[0] // 2
            self.u1, self.u2 = self.u0 // 4, self.u0 // 16
            self.at0 = self.whole(kh * self.u0)
            self.at1 = self.whole(self.at0 + plane * self.u1)
            self.at2 = self.whole(self.at1 + bz * self.u2)
            self.final = lambda value: value

        def whole(self, at):
            return pl.multiple_of(at, self.tile)

        def cut(self, ref, at, size):
            return ref.at[pl.ds(self.whole(at), size)]

        def copy(self, stage, src, dst, device):
            k = self.sems + stage
            return pltpu.make_async_remote_copy(
                src_ref=src, dst_ref=dst, send_sem=red_send.at[k], recv_sem=red_recv.at[k],
                device_id=device, device_id_type=MESH,
            )

        def expect(self, stage, many):
            sends.append(lambda: self.copy(stage, many, many, (b, h)).wait_send())
            due["bucket", self.sems + stage] = lambda: self.copy(stage, many, many, (b, h)).wait_recv()

        def arrived(self, stage):
            arrive(("bucket", self.sems + stage))

        def s0(self):
            self.copy(0, self.cut(self.full, (1 - kh) * self.u0, self.u0), self.in0, pair_one).start()
            self.expect(0, self.in0)

        def s1(self):
            self.arrived(0)
            step = self.u1

            def one(i, carry):
                at = self.whole(i * step)
                mine = self.full[pl.ds(self.whole(self.at0 + at), step), :].astype(F32)
                self.half[pl.ds(at, step), :] = (mine + self.in0[pl.ds(at, step), :].astype(F32)).astype(self.kind)
                return carry

            lax.fori_loop(0, 4, one, 0)
            for j in range(1, 4):
                t = lax.rem(plane + j, 4)
                self.copy(1, self.cut(self.half, t * self.u1, self.u1), self.in1.at[j - 1], in_plane(t)).start()
            self.expect(1, self.in1)

        def s2(self):
            self.arrived(1)
            step = self.u2

            def one(i, carry):
                at = self.whole(i * step)
                value = self.half[pl.ds(self.whole(plane * self.u1 + at), step), :].astype(F32)
                for j in range(3):
                    value = value + self.in1[j, pl.ds(at, step), :].astype(F32)
                self.sum1[pl.ds(at, step), :] = value.astype(self.kind)
                return carry

            lax.fori_loop(0, 4, one, 0)
            for j in range(1, 4):
                t = lax.rem(bz + j, 4)
                self.copy(2, self.cut(self.sum1, t * self.u2, self.u2), self.in2.at[j - 1], in_line(t)).start()
            self.expect(2, self.in2)

        def collect(self):
            self.arrived(2)
            value = self.sum1[pl.ds(self.whole(bz * self.u2), self.u2), :].astype(F32)
            for j in range(3):
                value = value + self.in2[j].astype(F32)
            if n_groups > 1:
                self.shard[...] = value.astype(self.kind)

                def send_group(j, carry):
                    t = lax.rem(group + j, n_groups)
                    self.copy(3, self.shard, self.in3.at[group], (b + GROUP * (t - group), h)).start()
                    return carry

                lax.fori_loop(1, n_groups, send_group, 0)
                self.expect(3, self.in3.at[pl.ds(0, n_groups - 1)])
                self.in3[group] = self.shard[...]
                self.arrived(3)
                value = self.in3[0].astype(F32)
                for t in range(1, n_groups):
                    value = value + self.in3[t].astype(F32)
            return value

        def s3(self):
            self.done[pl.ds(self.at2, self.u2), :] = self.final(self.collect()).astype(self.kind)
            mine = self.done.at[pl.ds(self.at2, self.u2)]
            for j in range(1, 4):
                self.copy(4, mine, mine, in_line(lax.rem(bz + j, 4))).start()
            self.expect(4, self.done.at[pl.ds(0, 3 * self.u2)])

        def s4(self):
            self.arrived(4)
            mine = self.done.at[pl.ds(self.at1, self.u1)]
            for j in range(1, 4):
                self.copy(5, mine, mine, in_plane(lax.rem(plane + j, 4))).start()
            self.expect(5, self.done.at[pl.ds(0, 3 * self.u1)])

        def s5(self):
            self.arrived(5)
            mine = self.done.at[pl.ds(self.at0, self.u0)]
            self.copy(6, mine, mine, pair_one).start()
            self.expect(6, mine)

        def s6(self):
            self.arrived(6)

    buckets = [Bucket(k) for k in range(6)]
    bucket_e, bucket_r, bucket_n = buckets[:3]
    taps_buckets = buckets[3:]
    bucket_a, bucket_b, bucket_c = taps_buckets

    def put_taps(at, value):
        start = 0
        for bucket in taps_buckets:
            size = bucket.full.shape[0]
            low, high = max(at, start), min(at + value.shape[0], start + size)
            if low < high:
                bucket.full[low - start : high - start, :] = value[low - at : high - at].astype(BF16)
            start += size

    place_in()
    arrive(("move", 0))
    pad_in(img4, x)
    arrive(("move", 1))
    sum_one = jnp.zeros((1, narrow), F32)
    square_one = jnp.zeros((1, narrow), F32)
    for q in range(rows // 2):
        value = dot(x[pl.ds(q * 2 * block, 2 * block), :], w_reduce[...])
        c1[pl.ds((1 + 2 * q) * block, 2 * block), :] = value
        sum_one = sum_one + colsum(value)
        square_one = square_one + colsum(value * value)
    put_rows(m1, 0, sum_one)
    put_rows(m1, narrow // 128, square_one)
    put_rows(m1, 4, jnp.zeros((1, 256), F32) + count.astype(F32))
    pl.semaphore_wait(barrier, total - 1)
    send_all(m1, s1, 0)
    set_edges(c1, first1, last1)
    halo_start(first1, last1, up1, down1, 0)
    arrive(("move", 3))
    pad_in(cot4, g)
    for j in range(width // 256):
        put_rows(mx, 2 * j, colsum(x[:, j * 256 : (j + 1) * 256].astype(F32)))
    exchange(mx, sx, 8, h, lambda t: (b, t))
    for k in range(9):
        arrive(("move", 8 + k))

    sum_all(s1, 0)
    slot_total = tot[4:5, :] / n_height
    pix_total = slot_total * area
    m_one = tiled(pix_total, narrow // 128)
    mean = get_rows(tot, 0, narrow // 128) / m_one
    inv_one = lax.rsqrt(get_rows(tot, 2, narrow // 128) / m_one - mean * mean + EPSILON)
    shift_one = mean * inv_one
    scale = inv_one * gain_one[...]
    offset = bias_one[...] - mean * scale
    scale_one, offset_one = scale, offset
    arrive(("halo", 0))
    patch(c1, up1, down1)

    def hide(at, carry):
        value = c1[block_at(at), :] * scale_one + offset_one
        value = swish(value) * mask(ext(at), narrow)
        hs[0, block_at(at), :] = pltpu.roll(value, 1, axis=0).astype(BF16)
        hs[1, block_at(at), :] = value.astype(BF16)
        hs[2, block_at(at), :] = pltpu.roll(value, block - 1, axis=0).astype(BF16)
        return carry

    lax.fori_loop(0, rows + 2, hide, 0)

    arrive(("move", 2))
    for q in range(rows // 2):
        for gr in range(2):
            lhs = jnp.concatenate(
                [
                    hs[bb, (a + 2 * q) * block : (a + 2 * q + 2) * block, gr * cg : (gr + 1) * cg]
                    for a in range(3)
                    for bb in range(3)
                ],
                axis=1,
            )
            c2[(1 + 2 * q) * block : (3 + 2 * q) * block, gr * half : (gr + 1) * half] = dot(
                lhs, w_split[:, gr * half : (gr + 1) * half]
            )
    m2[...] = jnp.zeros(m2.shape, F32)
    for j in range(2):
        lanes = pl.ds(j * half, half)

        def moments(r, carry):
            value = c2[block_at(r), lanes] * mask(own(r), half)
            return carry[0] + colsum(value), carry[1] + colsum(value * value)

        zero = jnp.zeros((1, half), F32)
        sums = lax.fori_loop(1, rows + 1, moments, (zero, zero))
        put_rows(m2, j * (half // 128), sums[0])
        put_rows(m2, split // 128 + j * (half // 128), sums[1])
    send_all(m2, s2, 1)
    set_edges(c2, first2, last2)
    halo_start(first2, last2, up2, down2, 1)
    arrive(("all", 8))
    mxb[...] = jnp.sum(sx[...], axis=0)
    exchange(mxb, sxb, 12, b, lambda t: (t, h))
    place_out()
    for bb in range(3):
        hs_t[bb] = hs[bb].T

    def slopes_one(r, carry):
        conv = c1[block_at(r + 1), :]
        live = mask(own(r + 1), narrow)
        slope1[block_at(r), :] = swish_slope(conv * scale_one + offset_one) * live
        n1[block_at(r), :] = ((conv * inv_one - shift_one) * live).astype(BF16)
        return carry

    lax.fori_loop(0, rows, slopes_one, 0)

    sum_all(s2, 1)
    m_two = tiled(pix_total, split // 128)
    mean = get_rows(tot, 0, split // 128) / m_two
    inv_two = lax.rsqrt(get_rows(tot, split // 128, split // 128) / m_two - mean * mean + EPSILON)
    shift_two = mean * inv_two
    scale_two = inv_two * gain_two[...]
    offset_two = bias_two[...] - mean * scale_two
    pool = jnp.zeros((slots, half), F32)
    for j in range(2):
        lanes = pl.ds(j * half, half)
        sc, of = scale_two[:, j * half : (j + 1) * half], offset_two[:, j * half : (j + 1) * half]

        def activate(r, acc):
            value = swish(c2[block_at(r), lanes] * sc + of) * mask(own(r), half)
            act[block_at(r - 1), lanes] = value
            return acc + value

        acc = lax.fori_loop(1, rows + 1, activate, jnp.zeros((block, half), F32))
        pool = pool + per_slot(acc, slots)
    pool = pool / area
    pooled[...] = pool
    arrive(("move", 4))
    m34[...] = dot(pool, w_squeeze[...], precision=HIGHEST)
    send_all(m34, s34, 2)
    exchange(pooled, pool_h, 13, h, lambda t: (b, t))
    arrive(("all", 12))
    tot[0:8, :] = jnp.sum(sxb[...], axis=0)
    x_mean = get_rows(tot, 0, width // 128) / tiled(pix_total, width // 128)

    def centre(r, carry):
        value = (x[block_at(r), :].astype(F32) - x_mean) * mask(own(r + 1), width)
        x_t[:, block_at(r)] = value.T.astype(BF16)
        return carry

    lax.fori_loop(0, rows, centre, 0)
    for q in range(2):
        at = slice(q * (width // 2), (q + 1) * (width // 2))
        bucket_n.full[at, :] = dot(x_t[at, :], n1[...]).astype(BF16)
    bucket_n.s0()
    arrive(("move", 5))
    arrive(("all", 2))

    def gather(i, carry):
        value = jnp.sum(s34[pl.ds(i * n_height, n_height)], axis=0)
        sq_all[i] = value
        return carry[0] + colsum(value), carry[1] + colsum(value * value)

    zero = jnp.zeros((1, inner), F32)
    sum_mid, square_mid = lax.fori_loop(0, n_batch, gather, (zero, zero))
    mean_mid = sum_mid / slot_total
    inv_mid = lax.rsqrt(square_mid / slot_total - mean_mid * mean_mid + EPSILON)
    norm_mid = (sq_all[b] - mean_mid) * inv_mid
    pre_mid = norm_mid * gain_mid[...] + bias_mid[...]
    middle = swish(pre_mid)
    logits = dot(middle, w_excite[...], precision=HIGHEST) + bias_excite[...]
    top = jnp.maximum(logits[:, :half], logits[:, half:])
    expo_one = jnp.exp(logits[:, :half] - top)
    expo_two = jnp.exp(logits[:, half:] - top)
    att_one = expo_one / (expo_one + expo_two)
    att_two = expo_two / (expo_one + expo_two)
    att[:, 0:half] = att_one
    att[:, half:split] = att_two
    for s in range(slots):
        attx[s * COLS : (s + 1) * COLS, :] = jnp.broadcast_to(att[s : s + 1, :], (COLS, split))

    def mix(r, carry):
        at = block_at(r)
        mixed[at, :] = (
            attx[:, 0:half] * act[at, 0:half] + attx[:, half:split] * act[at, half:split]
        ).astype(BF16)
        return carry

    lax.fori_loop(0, rows, mix, 0)
    arrive(("move", 6))
    for j in range(width // 256):
        lanes = pl.ds(j * 256, 256)
        sums = jnp.zeros((1, 256), F32)
        squares = jnp.zeros((1, 256), F32)
        for q in range(rows // 2):
            at = pl.ds(q * 2 * block, 2 * block)
            value = dot(mixed[at, :], w_expand[:, lanes])
            c3[at, lanes] = value
            sums = sums + colsum(value)
            squares = squares + colsum(value * value)
        put_rows(m5, j * 2, sums)
        put_rows(m5, width // 128 + j * 2, squares)
    send_pairs(m5, p5, s5, 3)
    mixed_t[...] = mixed[...].T
    bucket_n.s1()
    arrive(("all", 13))
    pool_sum[...] = jnp.sum(pool_h[...], axis=0)
    exchange(pool_sum, pool_b, 14, b, lambda t: (t, h))
    arrive(("halo", 1))
    patch(c2, up2, down2)
    for j in range(2):
        lanes = pl.ds(j * half, half)
        cut = slice(j * half, (j + 1) * half)
        sc, of = scale_two[:, cut], offset_two[:, cut]
        iv, sh = inv_two[:, cut], shift_two[:, cut]

        def slopes(at, carry):
            conv = c2[block_at(at), lanes]
            value = swish_slope(conv * sc + of) * mask(ext(at), half)
            slope2[block_at(at), lanes] = value
            value = value * own(at)
            more = value * (conv * iv - sh)
            slope2n[block_at(at), lanes] = more
            return carry[0] + value, carry[1] + more

        zero = jnp.zeros((block, half), F32)
        sums = lax.fori_loop(0, rows + 2, slopes, (zero, zero))
        st_src[0:slots, lanes] = per_slot(sums[0], slots)
        st_src[slots : 2 * slots, lanes] = per_slot(sums[1], slots)
    exchange(st_src, st_h, 10, h, lambda t: (b, t))

    sum_all(s5, 3)
    wide = width // 128
    m_three = tiled(pix_total, wide)
    mean = get_rows(tot, 0, wide) / m_three
    inv_three = lax.rsqrt(get_rows(tot, wide, wide) / m_three - mean * mean + EPSILON)
    shift_three = mean * inv_three
    scale_three = inv_three * gain_three[...]
    offset_three = bias_three[...] - mean * scale_three
    part = block // 2
    for j in range(width // 256):
        lanes = pl.ds(j * 256, 256)
        cut = slice(j * 256, (j + 1) * 256)
        sc, of = scale_three[:, cut], offset_three[:, cut]
        iv, sh = inv_three[:, cut], shift_three[:, cut]

        def finish_row(i, carry):
            r, k = i // 2, lax.rem(i, 2)
            at = pl.ds(pl.multiple_of(i * part, part), part)
            conv = c3[at, lanes]
            pre = conv * sc + of + x[at, lanes].astype(F32)
            sigma = sigmoid(pre)
            value = pre * sigma
            live = tiled(pix[pl.ds(pl.multiple_of(k * part, part), part), :] * own(r + 1), 2)
            xo[at, lanes] = (value * live).astype(BF16)
            slope = sigma + value * (1.0 - sigma)
            grad = g[at, lanes].astype(F32) * slope
            d3[at, lanes] = grad
            return carry[0] + colsum(grad), carry[1] + colsum(grad * (conv * iv - sh))

        zero = jnp.zeros((1, 256), F32)
        sums = lax.fori_loop(0, 2 * rows, finish_row, (zero, zero))
        put_rows(p6, j * 2, sums[0])
        put_rows(p6, wide + j * 2, sums[1])
    m6[...] = p6[...].astype(BF16)
    send_all(m6, s6, 4)
    pad_out(xo, out4)
    move(7, out4, output)

    sum_all(s6, 4)
    arrive(("all", 10))
    st_sum[...] = jnp.sum(st_h[...], axis=0)
    st_low[...] = st_sum[...].astype(BF16)
    exchange(st_low, st_b, 11, b, lambda t: (t, h))
    gb_three = get_rows(tot, 0, wide)
    gg_three = get_rows(tot, wide, wide)
    vectors[0:1, :] = gb_three
    vectors[1:2, :] = gg_three
    gg = gg_three / m_three
    k_one = scale_three
    k_three = k_one * inv_three * gg
    k_two = k_one * (gb_three / m_three - shift_three * gg)
    for j in range(width // 256):
        lanes = pl.ds(j * 256, 256)
        cut = slice(j * 256, (j + 1) * 256)
        ka, kb, kc = k_one[:, cut], k_two[:, cut], k_three[:, cut]

        def back_three(i, carry):
            at = pl.ds(pl.multiple_of(i * part, part), part)
            gc3[at, lanes] = (d3[at, lanes] * ka - kb - c3[at, lanes] * kc).astype(BF16)
            return carry

        lax.fori_loop(0, 2 * rows, back_three, 0)
    for q in range(rows // 2):
        gm[pl.ds((1 + 2 * q) * block, 2 * block), :] = dot(
            gc3[pl.ds(2 * q * block, 2 * block), :], w_expand[...], NT
        )
    att_sums = [[], [], []]
    for j in range(2):
        lanes = pl.ds(j * half, half)
        parts = [[], [], []]
        for k in range(2):
            zero = jnp.zeros((part, half), F32)

            def attend(r, acc):
                at = pl.ds(pl.multiple_of(r * block + k * part, part), part)
                up_at = pl.ds(pl.multiple_of((r + 1) * block + k * part, part), part)
                value = gm[up_at, :]
                return (
                    acc[0] + value * act[at, lanes],
                    acc[1] + value * own(r + 1) * slope2[up_at, lanes],
                    acc[2] + value * slope2n[up_at, lanes],
                )

            acc = lax.fori_loop(0, rows, attend, (zero, zero, zero))
            for i in range(3):
                parts[i].append(per_slot(acc[i], slots // 2))
        for i in range(3):
            att_sums[i].append(jnp.concatenate(parts[i], axis=0))
    grad_att = att_sums[0]
    blend = att_one * grad_att[0] + att_two * grad_att[1]
    grad_logits = jnp.concatenate(
        [att_one * (grad_att[0] - blend), att_two * (grad_att[1] - blend)], axis=1
    )
    em_part = dot(grad_logits, w_excite[...], NT, HIGHEST) * swish_slope(pre_mid)
    em_src[...] = em_part
    mid_scale = inv_mid * gain_mid[...] / area
    pooled_part = dot(em_part * mid_scale, w_squeeze[...], NT, HIGHEST)
    for j in range(2):
        lanes = pl.ds(j * half, half)
        weight = att_one if j == 0 else att_two
        for i in range(2):
            sums = weight * att_sums[1 + i][j] + pooled_part * st_sum[i * slots : (i + 1) * slots, lanes]
            put_rows(m78, (i * 2 + j) * (half // 128), colsum(sums))
    put_rows(m78, 2 * split // 128, colsum(em_part))
    put_rows(m78, 2 * split // 128 + 1, colsum(em_part * norm_mid))
    send_all(m78, s78, 5)
    exchange(em_src, em_all, 9, h, lambda t: (b, t))
    bucket_n.s2()
    set_edges(gm, first3, last3)
    halo_start(first3, last3, up3, down3, 2)
    for j in range(width // 256):
        bucket_e.full[j * narrow : (j + 1) * narrow, :] = dot(
            mixed_t[...], gc3[:, j * 256 : (j + 1) * 256]
        ).astype(BF16)
    bucket_e.s0()
    grad_excite = dot(middle, grad_logits, TN, HIGHEST)
    for gr in range(2):
        put_taps(18 * cg + gr * inner, grad_excite[:, gr * half : (gr + 1) * half])
    bias_part = colsum(grad_logits)
    put_rows(m10, 2 * (narrow // 128), bias_part)
    bucket_e.s1()
    arrive(("all", 11))
    every = n_batch * slots
    mid_all = ((sq_all[...] - mean_mid) * inv_mid).reshape(every, inner)
    st_all = st_b[...].astype(F32)
    w_turned = tiled(w_squeeze[...].T, 2)
    for i in range(2):
        sums = st_all[:, i * slots : (i + 1) * slots, :].reshape(every, split)
        wns[:, i * split : (i + 1) * split] = w_turned * dot(mid_all, sums, TN, HIGHEST)
        st_tot[i : i + 1, :] = colsum(sums)

    sum_all(s78, 5)
    rows_mid = 2 * split // 128
    gb_mid, gg_mid = tot[rows_mid : rows_mid + 1, :], tot[rows_mid + 1 : rows_mid + 2, :]
    vectors[4:5, 0:128] = gb_mid
    vectors[4:5, 128:256] = gg_mid
    mid_k = mid_scale / slot_total
    pooled_all = dot(jnp.broadcast_to(mid_k * gb_mid, (8, inner)), w_squeeze[...], NT, HIGHEST)[0:1]
    turned = dot(jnp.broadcast_to(mid_k * gg_mid, (8, inner)), wns[...], precision=HIGHEST)[0:1]
    pooled_all = tiled(pooled_all, 2)
    gb_two = get_rows(tot, 0, split // 128) - pooled_all * st_tot[0:1, :] - turned[:, :split]
    gg_two = get_rows(tot, split // 128, split // 128) - pooled_all * st_tot[1:2, :] - turned[:, split:]
    vectors[2:3, 0:split] = gb_two
    vectors[2:3, split : 2 * split] = gg_two
    arrive(("all", 9))
    em = jnp.sum(em_all[...], axis=0)
    em_sum[...] = em
    slot_live = jnp.where(lax.broadcasted_iota(jnp.int32, (slots, inner), 0) < count, 1.0, 0.0)
    grad_sq = (
        slot_live * inv_mid * gain_mid[...]
        * (em - gb_mid / slot_total - norm_mid * gg_mid / slot_total)
    )
    grad_pooled = dot(grad_sq, w_squeeze[...], NT, HIGHEST) / area
    att[:, 0:half] = grad_pooled
    for s in range(slots):
        gpx[s * COLS : (s + 1) * COLS, :] = jnp.broadcast_to(att[s : s + 1, 0:half], (COLS, half))
    arrive(("halo", 2))
    patch(gm, up3, down3)
    gg = gg_two / m_two
    k_one = scale_two
    k_three = k_one * inv_two * gg
    k_two = k_one * (gb_two / m_two - shift_two * gg)
    for j in range(2):
        lanes = pl.ds(j * half, half)
        cut = slice(j * half, (j + 1) * half)
        ka, kb, kc = k_one[:, cut], k_two[:, cut], k_three[:, cut]

        def back_two(at, carry):
            value = (attx[:, lanes] * gm[block_at(at), :] + gpx[...]) * slope2[block_at(at), lanes]
            value = value * ka - kb - c2[block_at(at), lanes] * kc
            gc2[block_at(at), lanes] = (value * mask(ext(at), half)).astype(BF16)
            return carry

        lax.fori_loop(0, rows + 2, back_two, 0)
    gc2_own[...] = (gc2[block_at(rows), :].astype(F32) * own(rows)).astype(BF16)

    def taps_grad(k):
        gr, bb = k // 3, k % 3
        lhs = jnp.concatenate(
            [hs_t[bb, gr * cg : (gr + 1) * cg, a * block : a * block + pixels] for a in range(3)], axis=0
        )
        lanes = slice(gr * half, (gr + 1) * half)
        rhs = jnp.concatenate([gc2[block:pixels, lanes], gc2_own[:, lanes]], axis=0)
        put_taps(k * 3 * cg, dot(lhs, rhs))

    for k in range(3):
        taps_grad(k)
    bucket_a.s0()
    for k in range(3, 6):
        taps_grad(k)
    exchange(em_sum, em_b, 15, b, lambda t: (t, h))
    bucket_a.s1()
    bucket_e.s2()
    bucket_b.s0()
    for gr in range(2):
        outs = []
        for bb in range(3):
            lhs = jnp.concatenate(
                [gc2[(2 - a) * block : (2 - a) * block + pixels, gr * half : (gr + 1) * half] for a in range(3)],
                axis=1,
            )
            rhs = jnp.concatenate(
                [
                    w_split[(a * 3 + bb) * cg : (a * 3 + bb + 1) * cg, gr * half : (gr + 1) * half]
                    for a in range(3)
                ],
                axis=1,
            )
            outs.append(dot(lhs, rhs, NT))
        gh[:, gr * cg : (gr + 1) * cg] = (
            outs[1] + pltpu.roll(outs[2], 1, axis=0) + pltpu.roll(outs[0], pixels - 1, axis=0)
        )
    bucket_b.s1()
    def back_hidden(r, carry):
        value = gh[block_at(r), :] * slope1[block_at(r), :]
        gh[block_at(r), :] = value
        d1[block_at(r), :] = value.astype(BF16)
        norm = c1[block_at(r + 1), :] * inv_one - shift_one
        return carry[0] + colsum(value), carry[1] + colsum(value * norm)
    zero = jnp.zeros((1, narrow), F32)
    sums = lax.fori_loop(0, rows, back_hidden, (zero, zero))
    put_rows(m10, 0, sums[0])
    put_rows(m10, narrow // 128, sums[1])
    send_all(m10, s10, 7)
    for q in range(2):
        at = slice(q * (width // 2), (q + 1) * (width // 2))
        bucket_r.full[at, :] = dot(x_t[at, :], d1[...]).astype(BF16)
    bucket_r.s0()
    bucket_c.s0()
    bucket_r.s1()
    bucket_a.s2()
    bucket_e.s3()
    bucket_c.s1()
    bucket_b.s2()
    kept_n = bucket_n.collect()
    sum_all(s10, 7)
    gb_one = get_rows(tot, 0, narrow // 128)
    gg_one = get_rows(tot, narrow // 128, narrow // 128)
    vectors[3:4, 0:narrow] = gb_one
    vectors[3:4, narrow : 2 * narrow] = gg_one
    vectors[3:4, 2 * narrow : 2 * narrow + split] = get_rows(tot, 2 * (narrow // 128), split // 128)
    move(6, vectors, vectors_out)
    gg = gg_one / m_one
    k_one = scale_one
    k_three = k_one * inv_one * gg
    k_two = k_one * (gb_one / m_one - shift_one * gg)
    def back_one(r, carry):
        value = gh[block_at(r), :] * k_one - k_two - c1[block_at(r + 1), :] * k_three
        gc1[block_at(r), :] = (value * mask(own(r + 1), narrow)).astype(BF16)
        return carry
    lax.fori_loop(0, rows, back_one, 0)
    bucket_r.final = lambda value: scale_one * (value - kept_n * gg)
    arrive(("all", 14))
    arrive(("all", 15))
    sq_grads = (inv_mid * gain_mid[...]) * (
        em_b[...].reshape(every, inner) - gb_mid / slot_total - mid_all * gg_mid / slot_total
    )
    squeeze_grad[...] = dot(pool_b[...].reshape(every, half), sq_grads, TN, HIGHEST)
    move(3, squeeze_grad, big_q)
    arrive(("move", 7))
    bucket_a.s3()
    def back_image(r, carry):
        value = d3[block_at(r), :] + dot(gc1[block_at(r), :], w_reduce[...], NT)
        xo[block_at(r), :] = value.astype(BF16)
        return carry
    lax.fori_loop(0, rows, back_image, 0)
    bucket_r.s2()
    bucket_e.s4()
    bucket_c.s2()
    pad_out(xo, out4)
    move(7, out4, grad_images)
    bucket_b.s3()
    bucket_a.s4()
    bucket_r.s3()
    bucket_c.s3()
    bucket_e.s5()
    bucket_b.s4()
    bucket_e.s6()
    move(0, bucket_e.done, big_e)
    bucket_a.s5()
    bucket_r.s4()
    bucket_c.s4()
    bucket_a.s6()
    move(1, bucket_a.done, big_a)
    bucket_b.s5()
    bucket_b.s6()
    move(4, bucket_b.done, big_b)
    bucket_r.s5()
    bucket_c.s5()
    bucket_r.s6()
    move(2, bucket_r.done, big_r)
    bucket_c.s6()
    move(5, bucket_c.done, big_c)

    for wait in sends:
        wait()
    for key in list(due):
        arrive(key)


def unpack_kernel(
    out_a, gimg_a, big_e, big_a, big_b, big_c, big_r, big_q, vectors,
    output, grad_images, grad_reduce, grad_split, grad_squeeze, grad_excite, grad_expand,
    grad_gain_one, grad_bias_one, grad_gain_two, grad_bias_two,
    grad_gain_mid, grad_bias_mid, grad_bias_excite, grad_gain_three, grad_bias_three,
    in_e, in_a, in_b, in_c, in_r, in_v, in_o, in_g, in_q, out_e, out_s, out_x, out_r, sems,
):
    def move(k, src, dst):
        copy = pltpu.make_async_copy(src, dst, sems.at[k])
        copy.start()
        return copy

    ins = [move(k, src, dst) for k, (src, dst) in enumerate([
        (out_a, in_o), (big_e, in_e), (gimg_a, in_g), (big_r, in_r), (big_a, in_a), (big_b, in_b), (big_c, in_c),
        (big_q, in_q), (vectors, in_v),
    ])]
    narrow = grad_expand.shape[0]
    taps, split = grad_split.shape
    half = split // 2
    inner = grad_excite.shape[0]
    outs = []
    ins[0].wait()
    outs.append(move(9, in_o, output))
    ins[1].wait()
    for j in range(grad_expand.shape[1] // 256):
        out_e[:, j * 256 : (j + 1) * 256] = in_e[j * narrow : (j + 1) * narrow, :].astype(F32)
    outs.append(move(10, out_e, grad_expand))
    ins[2].wait()
    outs.append(move(11, in_g, grad_images))
    ins[3].wait()
    out_r[...] = in_r[...].astype(F32)
    outs.append(move(12, out_r, grad_reduce))
    for k in range(4, 7):
        ins[k].wait()

    def put(at, dst, to, lanes, size):
        start = 0
        for ref in (in_a, in_b, in_c):
            low, high = max(at, start), min(at + size, start + ref.shape[0])
            if low < high:
                dst[to + low - at : to + high - at, lanes] = ref[low - start : high - start, :].astype(F32)
            start += ref.shape[0]

    cg = taps // 9
    for k in range(18):
        gr, bb, a = k // 9, k // 3 % 3, k % 3
        put(k * cg, out_s, (a * 3 + bb) * cg, slice(gr * half, (gr + 1) * half), cg)
    outs.append(move(13, out_s, grad_split))
    for gr in range(2):
        put(18 * cg + gr * inner, out_x, 0, slice(gr * half, (gr + 1) * half), inner)
    outs.append(move(14, out_x, grad_excite))
    ins[7].wait()
    outs.append(move(15, in_q, grad_squeeze))
    ins[8].wait()
    for dst, line, at in [
        (grad_bias_three, 0, 0), (grad_gain_three, 1, 0), (grad_bias_two, 2, 0), (grad_gain_two, 2, split),
        (grad_bias_one, 3, 0), (grad_gain_one, 3, narrow), (grad_bias_excite, 3, 2 * narrow),
        (grad_bias_mid, 4, 0), (grad_gain_mid, 4, inner),
    ]:
        dst[...] = in_v[line : line + 1, at : at + dst.shape[1]]
    for copy in outs:
        copy.wait()


def shards(
    n_batch, n_height,
    images, counts, row_valid, w_reduce, gain_one, bias_one, w_split, gain_two, bias_two, w_squeeze,
    gain_mid, bias_mid, w_excite, bias_excite, w_expand, gain_three, bias_three, cotangent,
):
    slots, rows, cols, width = images.shape
    count = slots * rows * cols
    narrow = w_reduce.shape[1]
    split = w_split.shape[3]
    taps = 9 * w_split.shape[2]
    inner = w_squeeze.shape[1]
    half = split // 2
    total = n_batch * n_height
    block = slots * COLS
    pixels = rows * block
    padded = pixels + 2 * block
    n_groups = n_batch // GROUP

    def row(v):
        return v.reshape(1, -1)

    unit = 4 * GROUP * 16
    size_e = width // 256 * narrow
    size_r = width
    taps_rows = 2 * taps + 2 * inner
    size_a = -(-taps_rows // (5 * unit)) * 2 * unit
    size_c = taps_rows - 2 * size_a

    def bucket(size, lanes=256, kind=BF16):
        kept = size // 2
        shapes = [
            (size, lanes), (kept, lanes), (kept, lanes), (3, kept // 4, lanes), (kept // 4, lanes),
            (3, kept // 16, lanes), (n_groups, kept // 16, lanes), (kept // 16, lanes), (size, lanes),
        ]
        return [pltpu.VMEM(dims, kind) for dims in shapes]

    messages = [(3, 2, 128), (8, 128), (8, 128), (16, 128), (16, 128), (5, 2, 128), (8, 128), (8, 128), (8, 128)]
    kinds = [BF16 if k == 4 else F32 for k in range(len(messages))]
    vm = pltpu.VMEM
    scratch = (
        [vm((1, k), F32) for k in (narrow, narrow, split, split, inner, inner, split, width, width)]
        + [vm((slots * cols, rows, width), BF16)] * 3
        + [vm((width, narrow), BF16), vm((taps, split), BF16), vm((narrow, inner), F32), vm((inner, split), F32),
           vm((narrow, width), BF16)]
        + [vm((pixels, width), BF16), vm((pixels, width), BF16), vm((block, 128), F32), vm((pixels, count), BF16),
           vm((count, pixels), BF16)]
        + [vm((padded, narrow), F32), vm((3, padded, narrow), BF16), vm((padded, split), F32), vm((pixels, split), F32),
           vm((padded, split), F32), vm((pixels, half), BF16), vm((pixels, width), F32), vm((pixels, width), F32),
           vm((pixels, width), BF16), vm((pixels, width), BF16), vm((padded, half), F32),
           vm((padded, split), F32), vm((padded, split), BF16), vm((pixels, narrow), F32), vm((pixels, narrow), F32),
           vm((pixels, narrow), BF16), vm((block, split), BF16), vm((pixels, narrow), BF16), vm((pixels, narrow), BF16)]
        + [vm((2 * slots, split), F32), vm((n_height, 2 * slots, split), F32), vm((2 * slots, split), F32),
           vm((2 * slots, split), BF16), vm((n_batch, 2 * slots, split), BF16), vm((inner, 2 * split), F32),
           vm((8, split), F32)]
        + [vm((width, pixels), BF16), vm((half, pixels), BF16), vm((3, narrow, padded), BF16), vm((slots, split), F32),
           vm((block, split), F32), vm((block, half), F32), vm((slots, half), F32), vm((n_batch, slots, inner), F32),
           vm((16, 128), F32)]
        + [vm(dims, kinds[k]) for k, dims in enumerate(messages)] + [vm((16, 128), F32)] * 2 + [vm((8, width), F32)]
        + [vm((n_height, slots, half), F32), vm((slots, half), F32), vm((n_batch, slots, half), F32), vm((slots, inner), F32),
           vm((n_batch, slots, inner), F32), vm((narrow, inner), F32), vm((slots, inner), F32)]
        + [vm((total // 2 if k == 3 else total,) + dims, kinds[k]) for k, dims in enumerate(messages[:-2])]
        + [vm((n_height,) + messages[-1], F32), vm((n_batch,) + messages[-1], F32)] + [vm((n_height, slots, inner), F32)]
        + [vm((block, narrow), F32)] * 4 + [vm((block, split), BF16)] * 4 + [vm((block, half), BF16)] * 4
        + [pltpu.SMEM((1,), jnp.int32), pltpu.SMEM((rows,), jnp.int32)]
        + [pltpu.SemaphoreType.DMA((k,)) for k in (19, 16, 16, 8, 8, 6, 6, 48, 48)]
        + bucket(size_e) + bucket(size_r) * 2 + bucket(size_a) * 2 + bucket(size_c)
    )
    vmem = pl.BlockSpec(memory_space=pltpu.VMEM)
    hbm = pl.BlockSpec(memory_space=pltpu.HBM)
    shape = jax.ShapeDtypeStruct
    flat = (slots * cols, rows, width)

    def by_column(value):
        return value.transpose(0, 2, 1, 3).reshape(flat)

    def by_row(value):
        return value.reshape(slots, cols, rows, width).transpose(0, 2, 1, 3)

    out_a, gimg_a, big_e, big_a, big_b, big_c, big_r, big_q, vectors = pl.pallas_call(
        functools.partial(main_kernel, n_batch, n_height, (slots, cols, rows, width)),
        out_shape=(
            shape(flat, BF16), shape(flat, BF16), shape((size_e, 256), BF16),
            shape((size_a, 256), BF16), shape((size_a, 256), BF16), shape((size_c, 256), BF16), shape((size_r, 256), BF16),
            shape((narrow, inner), F32),
            shape((8, width), F32),
        ),
        in_specs=[hbm] * 18,
        out_specs=[hbm] * 9,
        scratch_shapes=scratch,
        compiler_params=pltpu.CompilerParams(
            collective_id=0, has_side_effects=True, vmem_limit_bytes=58 * 1024 * 1024
        ),
    )(
        counts, row_valid, row(gain_one), row(bias_one), row(gain_two), row(bias_two), row(gain_mid), row(bias_mid),
        row(bias_excite), row(gain_three), row(bias_three),
        by_column(images), by_column(cotangent), w_reduce, w_split.reshape(taps, split), w_squeeze, w_excite, w_expand,
    )
    (
        output, grad_images, grad_reduce, grad_split, grad_squeeze, grad_excite, grad_expand,
        grad_gain_one, grad_bias_one, grad_gain_two, grad_bias_two,
        grad_gain_mid, grad_bias_mid, grad_bias_excite, grad_gain_three, grad_bias_three,
    ) = pl.pallas_call(
        unpack_kernel,
        out_shape=(
            shape(flat, BF16), shape(flat, BF16), shape((width, narrow), F32), shape((taps, split), F32),
            shape((narrow, inner), F32), shape((inner, split), F32), shape((narrow, width), F32),
            shape((1, narrow), F32), shape((1, narrow), F32), shape((1, split), F32), shape((1, split), F32),
            shape((1, inner), F32), shape((1, inner), F32), shape((1, split), F32), shape((1, width), F32),
            shape((1, width), F32),
        ),
        in_specs=[hbm] * 9,
        out_specs=[hbm] * 7 + [vmem] * 9,
        scratch_shapes=[
            vm((size_e, 256), BF16), vm((size_a, 256), BF16), vm((size_a, 256), BF16), vm((size_c, 256), BF16), vm((size_r, 256), BF16),
            vm((8, width), F32),
            vm(flat, BF16), vm(flat, BF16), vm((narrow, inner), F32),
            vm((narrow, width), F32), vm((taps, split), F32), vm((inner, split), F32), vm((width, narrow), F32),
            pltpu.SemaphoreType.DMA((16,)),
        ],
        compiler_params=pltpu.CompilerParams(vmem_limit_bytes=60 * 1024 * 1024),
    )(out_a, gimg_a, big_e, big_a, big_b, big_c, big_r, big_q, vectors)

    def like(value, other):
        return value.reshape(other.shape)

    return (
        by_row(output), by_row(grad_images), grad_reduce, like(grad_gain_one, gain_one), like(grad_bias_one, bias_one),
        like(grad_split, w_split), like(grad_gain_two, gain_two), like(grad_bias_two, bias_two), grad_squeeze,
        like(grad_gain_mid, gain_mid), like(grad_bias_mid, bias_mid), grad_excite, like(grad_bias_excite, bias_excite),
        grad_expand, like(grad_gain_three, gain_three), like(grad_bias_three, bias_three),
    )


def solution(mesh):
    axes = mesh.shape
    split_in = P("batch", "height", None, None)
    return jax.shard_map(
        functools.partial(shards, axes["batch"], axes["height"]),
        mesh=mesh,
        in_specs=(split_in, P("batch"), P("height")) + (P(),) * 14 + (split_in,),
        out_specs=(split_in, split_in) + (P(),) * 14,
        check_vma=False,
    )
```
